32 devices in a mesh: rep: 4 (over x, core), shard: 8 (over z, y).
Axes of the slice: x: 2, y: 2, z: 4, core: 2. Of those that a mesh axis runs over, the one named last changes fastest.
Arguments:
- hidden_in: bfloat16 [4, 4096, 896], P('rep', 'shard'), may hold values from -6 to 6
- cotangent: bfloat16 [4, 4096, 896], P('rep', 'shard'), may hold values from -6 to 6
- norm_gains: bfloat16 [2, 896], P(None, 'shard'), may hold values from 0.5 to 1.5
- q_bias: bfloat16 [896], P('shard'), may hold values from -3 to 3
- kv_bias: bfloat16 [256], P('shard'), may hold values from -3 to 3
- q_weight: bfloat16 [896, 896], P('shard'), may hold values from -0.1875 to 0.1875
- kv_weight: bfloat16 [896, 256], P('shard'), may hold values from -0.1875 to 0.1875
- out_weight: bfloat16 [896, 896], P('shard'), may hold values from -1.5 to 1.5
- gate_weight: bfloat16 [896, 4864], P('shard'), may hold values from -0.1875 to 0.1875
- up_weight: bfloat16 [896, 4864], P('shard'), may hold values from -0.1875 to 0.1875
- down_weight: bfloat16 [896, 4864], P('shard'), may hold values from -0.078125 to 0.078125
Outputs:
- output: bfloat16 [4, 4096, 896], P('rep', 'shard')
- input_grad: bfloat16 [4, 4096, 896], P('rep', 'shard')
- gains_grad: float32 [2, 896], P(None, 'shard')
- q_bias_grad: float32 [896], P('shard')
- kv_bias_grad: float32 [256], P('shard')
- q_weight_grad: float32 [896, 896], P('shard')
- kv_weight_grad: float32 [896, 256], P('shard')
- out_weight_grad: float32 [896, 896], P('shard')
- gate_weight_grad: float32 [896, 4864], P('shard')
- up_weight_grad: float32 [896, 4864], P('shard')
- down_weight_grad: float32 [896, 4864], P('shard')
The draws below stay inside these ranges and needn't reach their ends.
All inputs are finite; a program needn't handle non-finite values.
Results may differ from the reference program's by a relative error of at most 0.02.
Values may be sent and summed in bfloat16 or wider, within the bound.
No kernel may reach another device: no remote copies, remote signals or barrier semaphores. Data moves between devices by JAX's collectives and lax.ppermute only.
A program may use at most 192 MiB of HBM per device.

```python
import math
import jax
import jax.numpy as jnp
from jax import lax

D = 896
HEADS = 14
KV_HEADS = 2
HEAD = 64
FF = 4864
QW = 896
KW = 128
KEY_BLOCK = 512
LEN = 4096
SEQS = 4


def block_scale(rng, shape, split, least, largest):
    loudness, own = 1.0, jax.random.fold_in(rng, 6)
    for position, parts in split:
        steps = jnp.exp(jax.random.uniform(jax.random.fold_in(own, position), (parts,), jnp.float32, least / len(split), largest / len(split)))
        loudness = loudness * jnp.repeat(steps, shape[position] // parts).reshape([-1 if axis == position else 1 for axis in range(len(shape))])
    return loudness


def bell_draw(stream_key, extent, deviation, bound, cuts=(), held_as=jnp.bfloat16):
    factor_of = block_scale(stream_key, extent, cuts, -0.22, 0.18) if cuts else 1.0
    result = jax.random.normal(stream_key, extent, jnp.float32) * deviation * factor_of
    return jnp.minimum(jnp.maximum(result, -bound), bound).astype(held_as)


def setup_inputs(seed: int = 0) -> dict:
    key_of = jax.random.split(jax.random.key(seed), 12)
    return {
        "hidden_in": bell_draw(key_of[0], (SEQS, LEN, D), 1.0, 6.0, ((0, 4), (1, 8))),
        "cotangent": bell_draw(key_of[1], (SEQS, LEN, D), 1.0, 6.0, ((0, 4), (1, 8))),
        "norm_gains": jnp.clip(1.0 + 0.1 * jax.random.normal(key_of[2], (2, D), jnp.float32), 0.5, 1.5).astype(jnp.bfloat16),
        "q_bias": bell_draw(key_of[3], (QW,), 0.5, 3.0, ((0, 8),)),
        "kv_bias": bell_draw(key_of[4], (2 * KW,), 0.5, 3.0, ((0, 8),)),
        "q_weight": bell_draw(key_of[5], (D, QW), D ** -0.5, 0.1875, ((0, 8),)),
        "kv_weight": bell_draw(key_of[6], (D, 2 * KW), D ** -0.5, 0.1875, ((0, 8),)),
        "out_weight": bell_draw(key_of[7], (D, QW), (QW // 64) ** -0.5, 1.5, ((0, 8),)),
        "gate_weight": bell_draw(key_of[8], (D, FF), D ** -0.5, 0.1875, ((0, 8),)),
        "up_weight": bell_draw(key_of[9], (D, FF), D ** -0.5, 0.1875, ((0, 8),)),
        "down_weight": bell_draw(key_of[10], (D, FF), FF ** -0.5, 0.078125, ((0, 8),)),
    }


EPS = 1e-06
ROPE_BASE = 1000000.0
HIGHEST = lax.Precision.HIGHEST

@jax.custom_vjp
def low(v):
    return lax.optimization_barrier(v.astype(jnp.bfloat16)).astype(jnp.float32)

@jax.custom_vjp
def low_back(v):
    return v

def low_keep(v):
    return (low(v), None)

def low_pass(kept, grad):
    return (grad,)

def back_keep(v):
    return (v, None)

def back_low(kept, grad):
    return (low(grad),)
low.defvjp(low_keep, low_pass)
low_back.defvjp(back_keep, back_low)

def rope_tables(positions, head_width):
    half_width = head_width // 2
    inverse = jnp.exp(jnp.arange(half_width, dtype=jnp.float32) * (-2.0 * math.log(ROPE_BASE) / head_width))
    angles = positions.astype(jnp.float32)[:, None] * inverse[None, :]
    angles = jnp.concatenate([angles, angles], axis=1)
    return (jnp.cos(angles), jnp.sin(angles))

def rotate(source, cosine, sine):
    half_width = source.shape[-1] // 2
    turned = jnp.concatenate([-source[..., half_width:], source[..., :half_width]], axis=-1)
    return source * cosine[:, None, :] + turned * sine[:, None, :]

def sequence_forward(states, norm_gains, q_bias, kv_bias, q_weight, kv_weight, out_weight, gate_weight, up_weight, down_weight):
    inv_one = lax.rsqrt(lax.optimization_barrier(jnp.mean(states * states, axis=1, keepdims=True)) + EPS)
    h_one = low(states * inv_one * norm_gains[0])
    queries = low_back(jnp.dot(h_one, q_weight, precision=HIGHEST) + q_bias)
    keyvals = low_back(jnp.dot(h_one, kv_weight, precision=HIGHEST) + kv_bias)
    positions = jnp.arange(LEN, dtype=jnp.int32)
    cosine, sine = rope_tables(positions, HEAD)
    group = HEADS // KV_HEADS
    q_rot = low(rotate(queries.reshape(LEN, HEADS, HEAD), cosine, sine))
    q_rot = q_rot.reshape(LEN // KEY_BLOCK, KEY_BLOCK, KV_HEADS, group, HEAD)
    k_rot = low(rotate(keyvals[:, :KW].reshape(LEN, KV_HEADS, HEAD), cosine, sine))
    values = low(keyvals[:, KW:].reshape(LEN, KV_HEADS, HEAD))
    scale = HEAD ** (-0.5)

    def attend(block):
        q_block, offset = block
        scores = low_back(jnp.einsum('qgjd,kgd->qgjk', q_block, k_rot, precision=HIGHEST) * scale)
        query_pos = offset + jnp.arange(KEY_BLOCK, dtype=jnp.int32)
        allowed = positions[None, :] <= query_pos[:, None]
        scores = jnp.where(allowed[:, None, None, :], scores, -jnp.inf)
        probab = low(jax.nn.softmax(scores, axis=3))
        return low(low_back(jnp.einsum('qgjk,kgd->qgjd', probab, values, precision=HIGHEST)))
    offsets = jnp.arange(LEN // KEY_BLOCK, dtype=jnp.int32) * KEY_BLOCK
    attended = lax.map(jax.checkpoint(attend), (q_rot, offsets)).reshape(LEN, QW)
    middle = states + low_back(jnp.dot(attended, out_weight.T, precision=HIGHEST))
    inv_two = lax.rsqrt(lax.optimization_barrier(jnp.mean(middle * middle, axis=1, keepdims=True)) + EPS)
    h_two = low(middle * inv_two * norm_gains[1])
    gate_lin = low_back(jnp.dot(h_two, gate_weight, precision=HIGHEST))
    up_lin = low_back(jnp.dot(h_two, up_weight, precision=HIGHEST))
    hidden = low(jax.nn.silu(gate_lin) * up_lin)
    return middle + low_back(jnp.dot(hidden, down_weight.T, precision=HIGHEST))

def reference(hidden_in, cotangent, norm_gains, q_bias, kv_bias, q_weight, kv_weight, out_weight, gate_weight, up_weight, down_weight):
    params = tuple((array.astype(jnp.float32) for array in (norm_gains, q_bias, kv_bias, q_weight, kv_weight, out_weight, gate_weight, up_weight, down_weight)))
    inputs = hidden_in.astype(jnp.float32)

    def forward(all_states, *weights):

        def one_sequence(states):
            return sequence_forward(states, *weights)
        return lax.map(one_sequence, all_states)
    outputs, pullback = jax.vjp(forward, inputs, *params)
    grads = pullback(cotangent.astype(jnp.float32))
    return (outputs.astype(jnp.bfloat16), grads[0].astype(jnp.bfloat16), grads[1], grads[2], grads[3], grads[4], grads[5], grads[6], grads[7], grads[8], grads[9])
```

```python
import functools
import math

import jax
import jax.numpy as jnp
from jax import lax
from jax.experimental import pallas as pl
from jax.experimental.pallas import tpu as pltpu
from jax.sharding import PartitionSpec as P

D = 896
HEADS = 14
KV_HEADS = 2
HEAD = 64
FF = 4864
QW = 896
KW = 128
LANES = 128
TEAM = 4
FF_PART = 1280
FF_TILE = 256

EPS = 1e-06
ROPE_BASE = 1000000.0
F32 = jnp.float32
BF16 = jnp.bfloat16
VMEM_BYTES = 56 * 1024 * 1024


def dot_nt(left, right):
    return lax.dot_general(left, right, (((1,), (1,)), ((), ())), preferred_element_type=F32)


def dot_tn(left, right):
    return lax.dot_general(left, right, (((0,), (0,)), ((), ())), preferred_element_type=F32)


def dot_nn(left, right):
    return jnp.dot(left, right, preferred_element_type=F32)


def half_mask(parity, kind):
    lane = lax.broadcasted_iota(jnp.int32, (1, LANES), 1)
    return ((lane // HEAD) == parity).astype(kind)


def swap_halves(source):
    lane = lax.broadcasted_iota(jnp.int32, source.shape, 1)
    ahead = jnp.roll(source, -(HEAD // 2), axis=1)
    behind = jnp.roll(source, HEAD // 2, axis=1)
    return jnp.where(lane % HEAD < HEAD // 2, ahead, behind)


def attn_forward_kernel(me_ref, q_ref, k_ref, v_ref, o_ref, lse_ref):
    pair = pl.program_id(0)
    me = me_ref[0]
    rows = q_ref.shape[0]
    group = HEADS // KV_HEADS
    row = lax.broadcasted_iota(jnp.int32, (rows, rows), 0)
    col = lax.broadcasted_iota(jnp.int32, (rows, rows), 1)
    results = []
    for parity in range(2):
        kv_head = (2 * pair + parity) // group
        q_head = q_ref[...] * half_mask(parity, BF16)

        def scores(block):
            return dot_nt(q_head, k_ref[kv_head, pl.ds(block * rows, rows), :])

        def weigh(block, probs):
            return dot_nn(probs.astype(BF16), v_ref[kv_head, pl.ds(block * rows, rows), :])

        first = jnp.where(col <= row, scores(me), -1e30)
        top = jnp.max(first, axis=1, keepdims=True)
        probs = jnp.exp(first - top)
        total = jnp.sum(probs, axis=1, keepdims=True)
        acc = weigh(me, probs)

        def step(block, running):
            top, total, acc = running
            s = scores(block)
            new_top = jnp.maximum(top, jnp.max(s, axis=1, keepdims=True))
            shrink = jnp.exp(top - new_top)
            probs = jnp.exp(s - new_top)
            total = total * shrink + jnp.sum(probs, axis=1, keepdims=True)
            return new_top, total, acc * shrink + weigh(block, probs)

        top, total, acc = lax.fori_loop(0, me, step, (top, total, acc))
        results.append(acc / total)
        lse = jnp.broadcast_to(top + jnp.log(total), (rows, LANES))
        lse_ref[0, parity : parity + 1, :] = jnp.transpose(lse)[0:1, :]
    o_ref[...] = jnp.where(half_mask(0, jnp.int32) > 0, results[0], results[1]).astype(BF16)


def attn_forward(me, q, k_twice, v_twice):
    rows = q.shape[0]
    length = k_twice.shape[1]
    whole = pl.BlockSpec((KV_HEADS, length, LANES), lambda i, me: (0, 0, 0))
    blocks = length // rows
    return pl.pallas_call(
        attn_forward_kernel,
        grid_spec=pltpu.PrefetchScalarGridSpec(
            num_scalar_prefetch=1,
            grid=(HEADS // 2,),
            in_specs=[pl.BlockSpec((rows, LANES), lambda i, me: (0, i)), whole, whole],
            out_specs=[
                pl.BlockSpec((rows, LANES), lambda i, me: (0, i)),
                pl.BlockSpec((1, 2, rows), lambda i, me: (i, 0, 0)),
            ],
        ),
        out_shape=[
            jax.ShapeDtypeStruct((rows, QW), BF16),
            jax.ShapeDtypeStruct((HEADS // 2, 2, rows), F32),
        ],
        compiler_params=pltpu.CompilerParams(vmem_limit_bytes=VMEM_BYTES),
        cost_estimate=pl.CostEstimate(
            flops=16 * blocks * HEADS * rows * rows * HEAD // 2,
            bytes_accessed=8 * rows * QW,
            transcendentals=blocks * HEADS * rows * rows,
        ),
        name="attn_forward",
    )(me, q, k_twice, v_twice)


def attn_backward_kernel(
    me_ref,
    q_ref,
    k_ref,
    v_ref,
    o_ref,
    do_ref,
    lse_ref,
    cos_ref,
    sin_ref,
    dq_ref,
    dkv_ref,
    dk_acc,
    dv_acc,
):
    pair = pl.program_id(0)
    me = me_ref[0]
    rows = q_ref.shape[0]
    group = HEADS // KV_HEADS
    key = lax.broadcasted_iota(jnp.int32, (rows, rows), 0)
    query = lax.broadcasted_iota(jnp.int32, (rows, rows), 1)

    @pl.when(pair == 0)
    def _():
        dk_acc[...] = jnp.zeros_like(dk_acc)
        dv_acc[...] = jnp.zeros_like(dv_acc)

    products = do_ref[...].astype(F32) * o_ref[...].astype(F32)
    results = []
    for parity in range(2):
        kv_head = (2 * pair + parity) // group
        mask = half_mask(parity, BF16)
        q_head = q_ref[...] * mask
        do_head = do_ref[...] * mask
        picks = jnp.broadcast_to(half_mask(parity, F32), (8, LANES))
        delta = lax.dot_general(
            picks,
            products,
            (((1,), (1,)), ((), ())),
            precision=lax.Precision.HIGHEST,
            preferred_element_type=F32,
        )[0:1, :]
        lse = lse_ref[0, parity : parity + 1, :]

        def block_step(block, dq, masked):
            span = pl.ds(block * rows, rows)
            keys = k_ref[kv_head, span, :]
            probs = jnp.exp(dot_nt(keys, q_head) - lse)
            if masked:
                probs = jnp.where(key <= query, probs, 0.0)
            d_probs = dot_nt(v_ref[kv_head, span, :], do_head)
            d_scores = (probs * (d_probs - delta)).astype(BF16)
            dv_acc[kv_head, span, :] += dot_nn(probs.astype(BF16), do_head)
            dk_acc[kv_head, span, :] += dot_nn(d_scores, q_head)
            return dq + dot_tn(d_scores, keys)

        dq = block_step(me, jnp.zeros((rows, LANES), F32), True)
        dq = lax.fori_loop(0, me, lambda block, dq: block_step(block, dq, False), dq)
        results.append(dq)
    dq = jnp.where(half_mask(0, jnp.int32) > 0, results[0], results[1]) * HEAD ** (-0.5)
    dq_ref[...] = (dq * cos_ref[...] + swap_halves(dq * sin_ref[...])).astype(BF16)

    @pl.when(pair == HEADS // 2 - 1)
    def _():
        low = half_mask(0, jnp.int32) > 0

        def fold(block, carry):
            span = pl.ds(block * rows, rows)
            for place, acc in ((0, dk_acc), (1, dv_acc)):
                zero = acc[0, span, :]
                one = acc[1, span, :]
                zero = zero + pltpu.roll(zero, HEAD, 1)
                one = one + pltpu.roll(one, HEAD, 1)
                dkv_ref[span, place * LANES : (place + 1) * LANES] = jnp.where(
                    low, zero, one
                ).astype(BF16)
            return carry

        lax.fori_loop(0, dk_acc.shape[1] // rows, fold, 0)


def attn_backward(me, q, k_twice, v_twice, o, d_o, lse, cosine, sine):
    rows = q.shape[0]
    length = k_twice.shape[1]
    whole = pl.BlockSpec((KV_HEADS, length, LANES), lambda i, me: (0, 0, 0))
    pair = pl.BlockSpec((rows, LANES), lambda i, me: (0, i))
    table = pl.BlockSpec((rows, LANES), lambda i, me: (0, 0))
    blocks = length // rows
    return pl.pallas_call(
        attn_backward_kernel,
        grid_spec=pltpu.PrefetchScalarGridSpec(
            num_scalar_prefetch=1,
            grid=(HEADS // 2,),
            in_specs=[
                pair,
                whole,
                whole,
                pair,
                pair,
                pl.BlockSpec((1, 2, rows), lambda i, me: (i, 0, 0)),
                table,
                table,
            ],
            out_specs=[pair, pl.BlockSpec((length, 2 * KW), lambda i, me: (0, 0))],
            scratch_shapes=[
                pltpu.VMEM((KV_HEADS, length, LANES), F32),
                pltpu.VMEM((KV_HEADS, length, LANES), F32),
            ],
        ),
        out_shape=[
            jax.ShapeDtypeStruct((rows, QW), BF16),
            jax.ShapeDtypeStruct((length, 2 * KW), BF16),
        ],
        compiler_params=pltpu.CompilerParams(vmem_limit_bytes=VMEM_BYTES),
        cost_estimate=pl.CostEstimate(
            flops=40 * blocks * HEADS * rows * rows * HEAD // 2,
            bytes_accessed=16 * rows * QW,
            transcendentals=blocks * HEADS * rows * rows,
        ),
        name="attn_backward",
    )(me, q, k_twice, v_twice, o, d_o, lse, cosine, sine)


def feed_kernel(
    h_ref, c_ref, g_ref, u_ref, d_ref, out_ref, dh_ref, hid_ref, dg_ref, du_ref, out_acc, dh_acc
):
    tile = pl.program_id(0)
    h = h_ref[...]
    c = c_ref[...]
    gate = dot_nn(h, g_ref[...])
    up = dot_nn(h, u_ref[...])
    d_hid = dot_nn(c, d_ref[...])
    sig = jax.nn.sigmoid(gate)
    silu = gate * sig
    hid = (silu * up).astype(BF16)
    d_gate = (d_hid * up * sig * (1.0 + gate * (1.0 - sig))).astype(BF16)
    d_up = (d_hid * silu).astype(BF16)
    hid_ref[...] = hid
    dg_ref[...] = d_gate
    du_ref[...] = d_up
    out_part = dot_nt(hid, d_ref[...])
    dh_part = dot_nt(d_gate, g_ref[...]) + dot_nt(d_up, u_ref[...])

    @pl.when(tile == 0)
    def _():
        out_acc[...] = out_part
        dh_acc[...] = dh_part

    @pl.when(tile > 0)
    def _():
        out_acc[...] += out_part
        dh_acc[...] += dh_part

    @pl.when(tile == pl.num_programs(0) - 1)
    def _():
        out_ref[...] = out_acc[...].astype(BF16)
        dh_ref[...] = dh_acc[...].astype(BF16)


def feed(h, c, gate, up, down):
    rows = h.shape[0]
    tokens = pl.BlockSpec((rows, D), lambda i: (0, 0))
    weights = pl.BlockSpec((D, FF_TILE), lambda i: (0, i))
    hidden = pl.BlockSpec((rows, FF_TILE), lambda i: (0, i))
    return pl.pallas_call(
        feed_kernel,
        grid=(FF_PART // FF_TILE,),
        in_specs=[tokens, tokens, weights, weights, weights],
        out_specs=[tokens, tokens, hidden, hidden, hidden],
        scratch_shapes=[pltpu.VMEM((rows, D), F32), pltpu.VMEM((rows, D), F32)],
        out_shape=[jax.ShapeDtypeStruct((rows, D), BF16)] * 2
        + [jax.ShapeDtypeStruct((rows, FF_PART), BF16)] * 3,
        compiler_params=pltpu.CompilerParams(vmem_limit_bytes=VMEM_BYTES),
        cost_estimate=pl.CostEstimate(
            flops=12 * rows * D * FF_PART,
            bytes_accessed=6 * D * FF_PART + 8 * rows * D + 6 * rows * FF_PART,
            transcendentals=rows * FF_PART,
        ),
        name="feed",
    )(h, c, gate, up, down)


def ring_order(count):
    if count == 8:
        return [0, 1, 3, 5, 7, 6, 4, 2]
    return list(range(count))


class Ring:
    def __init__(self, count):
        order = ring_order(count)
        self.count = count
        self.half = count // 2
        self.ahead = [(order[i], order[(i + 1) % count]) for i in range(count)]
        self.back = [(b, a) for a, b in self.ahead]
        place = [order.index(i) for i in range(count)]
        self.order = jnp.array(order + order + order, jnp.int32)
        self.place = jnp.array(place, jnp.int32)[lax.axis_index("shard")]

    def owner(self, offset):
        return self.order[self.place + self.count + offset]

    def send(self, array, ahead):
        return lax.ppermute(array, "shard", self.ahead if ahead else self.back)

    def gather(self, array):
        rows, cols = array.shape
        cut = (cols // (2 * LANES)) * LANES
        whole = jnp.zeros((self.count * rows, cols), array.dtype)

        def put(whole, piece, offset, column):
            return lax.dynamic_update_slice(whole, piece, (self.owner(offset) * rows, column))

        whole = put(whole, array, 0, 0)
        right = left = array
        for step in range(1, self.half):
            right = self.send(right, True)
            left = self.send(left, False)
            whole = put(whole, right, -step, 0)
            whole = put(whole, left, step, 0)
        whole = put(whole, self.send(right[:, :cut], True), self.half, 0)
        return put(whole, self.send(left[:, cut:], False), self.half, cut)

    def scatter_sum(self, array):
        rows = array.shape[0] // self.count
        cols = array.shape[1]
        cut = (cols // (2 * LANES)) * LANES

        def chunk(offset):
            return lax.dynamic_slice(array, (self.owner(offset) * rows, 0), (rows, cols))

        def add(left, right):
            return (left.astype(F32) + right.astype(F32)).astype(BF16)

        far = chunk(self.half)
        right = self.send(far[:, :cut], True)
        left = self.send(far[:, cut:], False)
        for step in range(self.half - 1, 0, -1):
            near = chunk(step)
            if step == self.half - 1:
                right = jnp.concatenate([add(near[:, :cut], right), near[:, cut:]], axis=1)
            else:
                right = add(near, right)
            right = self.send(right, True)
            near = chunk(-step)
            if step == self.half - 1:
                left = jnp.concatenate([near[:, :cut], add(near[:, cut:], left)], axis=1)
            else:
                left = add(near, left)
            left = self.send(left, False)
        return chunk(0).astype(F32) + right.astype(F32) + left.astype(F32)


def team_send(array, bit):
    return lax.ppermute(array, "rep", [(i, i ^ bit) for i in range(lax.axis_size("rep"))])


def team_sum(mine, core, cross, both):
    gathered = (cross.astype(F32) + team_send(both, 1).astype(F32)).astype(BF16)
    return (
        mine.astype(F32)
        + team_send(core, 1).astype(F32)
        + team_send(gathered, 2).astype(F32)
    )


def rope_tables(positions):
    half_width = HEAD // 2
    inverse = jnp.exp(
        jnp.arange(half_width, dtype=F32) * (-2.0 * math.log(ROPE_BASE) / HEAD)
    )
    angles = positions.astype(F32)[:, None] * inverse[None, :]
    cosine = jnp.cos(angles)
    sine = jnp.sin(angles)
    return (
        jnp.concatenate([cosine] * 4, axis=1),
        jnp.concatenate([-sine, sine, -sine, sine], axis=1),
    )


def rotate(source, cosine, sine):
    times = source.shape[1] // LANES
    return source * jnp.tile(cosine, (1, times)) + swap_halves(source) * jnp.tile(sine, (1, times))


def rotate_back(source, cosine, sine):
    times = source.shape[1] // LANES
    return source * jnp.tile(cosine, (1, times)) + swap_halves(source * jnp.tile(sine, (1, times)))


def norm_back(grad_normed, normed, inv_scale, gain_row):
    scaled = grad_normed * gain_row
    return inv_scale * (scaled - normed * jnp.mean(scaled * normed, axis=1, keepdims=True))


def body(
    hidden_in,
    cotangent,
    norm_gains,
    q_bias,
    kv_bias,
    q_weight,
    kv_weight,
    out_weight,
    gate_weight,
    up_weight,
    down_weight,
):
    tok_rows = hidden_in.shape[1]
    shard_count = lax.axis_size("shard")
    rep_count = lax.axis_size("rep")
    shard_place = lax.axis_index("shard")
    rep_place = lax.axis_index("rep")
    team_place = rep_place % TEAM
    row_share = D // shard_count
    kv_share = 2 * KW // shard_count
    ring = Ring(shard_count)

    small = jnp.concatenate([norm_gains[0], norm_gains[1], q_bias, kv_bias])
    spare = jnp.pad(small[None, :], ((0, 15), (0, QW + 2 * KW - small.shape[0])))
    qkv_piece = jnp.concatenate(
        [jnp.concatenate([q_weight, kv_weight], axis=1), spare], axis=0
    )
    qkv_rows = row_share + 16
    qkv_all = ring.gather(qkv_piece).reshape(shard_count, qkv_rows, QW + 2 * KW)
    qkv_full = qkv_all[:, :row_share].reshape(D, QW + 2 * KW)
    smalls = qkv_all[:, row_share].astype(F32)
    gain_one = smalls[:, :row_share].reshape(D)
    gain_two = smalls[:, row_share : 2 * row_share].reshape(D)
    q_bias_all = smalls[:, 2 * row_share : 3 * row_share].reshape(QW)
    kv_bias_all = smalls[:, 3 * row_share : 3 * row_share + kv_share].reshape(2 * KW)
    q_full = qkv_full[:, :QW]
    kv_full = qkv_full[:, QW:]

    grad_out = cotangent[0]
    inputs = hidden_in[0].astype(F32)
    inv_one = lax.rsqrt(jnp.mean(inputs * inputs, axis=1, keepdims=True) + EPS)
    normed_one = inputs * inv_one
    h_one = (normed_one * gain_one).astype(BF16)
    positions = shard_place * tok_rows + jnp.arange(tok_rows, dtype=jnp.int32)
    cosine, sine = rope_tables(positions)
    keyvals = dot_nn(h_one, kv_full) + kv_bias_all
    kv_local = jnp.concatenate(
        [rotate(keyvals[:, :KW], cosine, sine), keyvals[:, KW:]], axis=1
    ).astype(BF16)
    kv_whole = ring.gather(kv_local)
    queries = dot_nn(h_one, q_full) + q_bias_all
    q_scaled = rotate(queries, cosine, sine).astype(BF16) * jnp.asarray(HEAD ** (-0.5), BF16)
    out_full = ring.gather(out_weight)

    def quarter(weight):
        padded = jnp.pad(weight, ((0, 0), (0, TEAM * FF_PART - FF)))
        return lax.dynamic_slice_in_dim(padded, team_place * FF_PART, FF_PART, 1)

    gate_full = ring.gather(quarter(gate_weight))
    up_full = ring.gather(quarter(up_weight))
    down_full = ring.gather(quarter(down_weight))

    me = shard_place.astype(jnp.int32).reshape(1)
    heads = [kv_whole[:, HEAD * i : HEAD * (i + 1)] for i in range(2 * KV_HEADS)]
    k_twice = jnp.stack([jnp.concatenate([h, h], axis=1) for h in heads[:KV_HEADS]])
    v_twice = jnp.stack([jnp.concatenate([h, h], axis=1) for h in heads[KV_HEADS:]])
    attn_b, lse = attn_forward(me, q_scaled, k_twice, v_twice)

    middle = inputs + dot_nt(attn_b, out_full)
    inv_two = lax.rsqrt(jnp.mean(middle * middle, axis=1, keepdims=True) + EPS)
    normed_two = middle * inv_two
    h_two = (normed_two * gain_two).astype(BF16)

    c_core = team_send(grad_out, 1)
    c_cross = team_send(grad_out, 2)
    c_both = team_send(c_cross, 1)
    h_core = team_send(h_two, 1)
    h_cross = team_send(h_two, 2)
    h_both = team_send(h_cross, 1)
    sets = ((h_two, grad_out), (h_core, c_core), (h_cross, c_cross), (h_both, c_both))
    done = [feed(h, c, gate_full, up_full, down_full) for h, c in sets]
    grad_h_two = team_sum(*[one[1] for one in done])
    out_sum = team_sum(*[one[0] for one in done])
    output = middle + out_sum

    h_sets = jnp.concatenate([h for h, _ in sets], axis=0)
    c_sets = jnp.concatenate([c for _, c in sets], axis=0)
    hid_sets, dg_sets, du_sets = (
        jnp.concatenate([one[i] for one in done], axis=0) for i in (2, 3, 4)
    )
    feed_grads = [
        dot_tn(left, right).astype(BF16)
        for left, right in ((h_sets, dg_sets), (h_sets, du_sets), (c_sets, hid_sets))
    ]

    gain_two_grad = jnp.sum(grad_h_two * normed_two, axis=0)
    grad_middle = grad_out.astype(F32) + norm_back(grad_h_two, normed_two, inv_two, gain_two)
    grad_branch_b = grad_middle.astype(BF16)
    out_grad = dot_tn(grad_branch_b, attn_b)
    grad_attn = dot_nn(grad_branch_b, out_full).astype(BF16)
    grad_q_b, grad_kv_parts = attn_backward(
        me, q_scaled, k_twice, v_twice, attn_b, grad_attn, lse, cosine, sine
    )
    grad_kv_mine = ring.scatter_sum(grad_kv_parts)
    grad_kv_b = jnp.concatenate(
        [rotate_back(grad_kv_mine[:, :KW], cosine, sine), grad_kv_mine[:, KW:]], axis=1
    ).astype(BF16)
    q_bias_sum = jnp.sum(grad_q_b.astype(F32), axis=0)
    kv_bias_sum = jnp.sum(grad_kv_b.astype(F32), axis=0)
    grad_h_one = dot_nt(grad_q_b, q_full) + dot_nt(grad_kv_b, kv_full)
    gain_one_grad = jnp.sum(grad_h_one * normed_one, axis=0)
    input_grad = (grad_middle + norm_back(grad_h_one, normed_one, inv_one, gain_one)).astype(BF16)

    feed_rows = [ring.scatter_sum(grad).astype(BF16) for grad in feed_grads]
    teams = rep_count // TEAM
    if teams > 1:
        across = [[t * TEAM + i for t in range(teams)] for i in range(TEAM)]
        feed_rows = [lax.psum(rows, "rep", axis_index_groups=across) for rows in feed_rows]

    def team_columns(rows):
        core = team_send(rows, 1)
        cross = team_send(rows, 2)
        both = team_send(cross, 1)
        whole = jnp.zeros((row_share, TEAM * FF_PART), BF16)
        for bit, part in ((0, rows), (1, core), (2, cross), (3, both)):
            whole = lax.dynamic_update_slice(whole, part, (0, (team_place ^ bit) * FF_PART))
        return whole[:, :FF].astype(F32)

    gate_grad, up_grad, down_grad = (team_columns(rows) for rows in feed_rows)

    attn_grads = jnp.concatenate(
        [dot_tn(h_one, grad_q_b), dot_tn(h_one, grad_kv_b), out_grad], axis=1
    ).astype(BF16)
    attn_rows = ring.scatter_sum(attn_grads).astype(BF16)
    attn_rows = (attn_rows.astype(F32) + team_send(attn_rows, 1).astype(F32)).astype(BF16)
    attn_rows = attn_rows.astype(F32) + team_send(attn_rows, 2).astype(F32)
    if teams > 1:
        attn_rows = lax.psum(attn_rows.astype(BF16), "rep", axis_index_groups=across).astype(F32)

    gains_full, q_bias_full, kv_bias_full = lax.psum(
        (jnp.stack([gain_one_grad, gain_two_grad], axis=0), q_bias_sum, kv_bias_sum),
        ("rep", "shard"),
    )
    gains_grad = lax.dynamic_slice_in_dim(gains_full, shard_place * row_share, row_share, 1)
    q_bias_grad = lax.dynamic_slice_in_dim(q_bias_full, shard_place * row_share, row_share, 0)
    kv_bias_grad = lax.dynamic_slice_in_dim(kv_bias_full, shard_place * kv_share, kv_share, 0)
    return (
        output.astype(BF16)[None],
        input_grad[None],
        gains_grad,
        q_bias_grad,
        kv_bias_grad,
        attn_rows[:, :QW],
        attn_rows[:, QW : QW + 2 * KW],
        attn_rows[:, QW + 2 * KW :],
        gate_grad,
        up_grad,
        down_grad,
    )


def solution(mesh):
    tokens = P("rep", "shard", None)
    rows = P("shard", None)
    placed = (tokens, tokens, P(None, "shard"), P("shard"), P("shard")) + (rows,) * 6
    return jax.shard_map(body, mesh=mesh, in_specs=placed, out_specs=placed, check_vma=False)
```

```python
import functools
import math

import jax
import jax.numpy as jnp
from jax import lax
from jax.experimental import pallas as pl
from jax.experimental.pallas import tpu as pltpu
from jax.sharding import PartitionSpec as P

D = 896
HEADS = 14
KV_HEADS = 2
HEAD = 64
FF = 4864
QW = 896
KW = 128
LANES = 128
TEAM = 4
FF_PART = 1280
FF_TILE = 256
UNIT = 1024

EPS = 1e-06
ROPE_BASE = 1000000.0
F32 = jnp.float32
BF16 = jnp.bfloat16
VMEM_BYTES = 56 * 1024 * 1024


def dot_nt(left, right):
    return lax.dot_general(left, right, (((1,), (1,)), ((), ())), preferred_element_type=F32)


def dot_tn(left, right):
    return lax.dot_general(left, right, (((0,), (0,)), ((), ())), preferred_element_type=F32)


def dot_nn(left, right):
    return jnp.dot(left, right, preferred_element_type=F32)


def half_mask(parity, kind):
    lane = lax.broadcasted_iota(jnp.int32, (1, LANES), 1)
    return ((lane // HEAD) == parity).astype(kind)


def swap_halves(source):
    lane = lax.broadcasted_iota(jnp.int32, source.shape, 1)
    ahead = jnp.roll(source, -(HEAD // 2), axis=1)
    behind = jnp.roll(source, HEAD // 2, axis=1)
    return jnp.where(lane % HEAD < HEAD // 2, ahead, behind)


def seen(me, rows, unit):
    base = (me * rows // UNIT) * UNIT
    key = lax.broadcasted_iota(jnp.int32, (UNIT, rows), 0) + base
    query = lax.broadcasted_iota(jnp.int32, (UNIT, rows), 1) + me * rows
    return key <= query


def attn_forward_kernel(me_ref, q_ref, k_ref, vt_ref, o_ref, lse_ref):
    pair = pl.program_id(0) + me_ref[1]
    me = me_ref[0]
    rows = q_ref.shape[0]
    group = HEADS // KV_HEADS
    last = me * rows // UNIT
    allowed = seen(me, rows, last)
    heads = [((2 * pair + parity) // group, q_ref[...] * half_mask(parity, BF16)) for parity in range(2)]

    def span(unit):
        return pl.ds(unit * UNIT, UNIT)

    def scores(head, unit):
        return dot_nt(k_ref[head[0], span(unit), :], head[1])

    def weigh(head, unit, probs):
        return dot_nn(vt_ref[head[0], :, span(unit)], probs.astype(BF16))

    tops, probs = [], []
    for head in heads:
        s = jnp.where(allowed, scores(head, last), -1e30)
        tops.append(jnp.max(s, axis=0, keepdims=True))
        probs.append(jnp.exp(s - tops[-1]))
    start = tuple(
        (jnp.sum(p, axis=0, keepdims=True), weigh(head, last, p)) for head, p in zip(heads, probs)
    )

    def quick(unit, state):
        probs = [jnp.exp(scores(head, unit) - top) for head, top in zip(heads, tops)]
        return tuple(
            (total + jnp.sum(p, axis=0, keepdims=True), acc + weigh(head, unit, p))
            for head, (total, acc), p in zip(heads, state, probs)
        )

    def careful(unit, state):
        after = []
        for head, (top, total, acc) in zip(heads, state):
            s = scores(head, unit)
            new_top = jnp.maximum(top, jnp.max(s, axis=0, keepdims=True))
            shrink = jnp.exp(top - new_top)
            p = jnp.exp(s - new_top)
            total = total * shrink + jnp.sum(p, axis=0, keepdims=True)
            after.append((new_top, total, acc * shrink + weigh(head, unit, p)))
        return tuple(after)

    def store(state):
        for parity, (top, total, acc) in enumerate(state):
            lse_ref[0, parity : parity + 1, :] = top + jnp.log(total)
        both = jnp.concatenate([acc / total for top, total, acc in state], axis=0)
        o_ref[...] = jnp.transpose(both).astype(BF16)

    state = lax.fori_loop(0, last, quick, start)
    largest = jnp.max(jnp.maximum(state[0][0], state[1][0]))
    fine = largest < 1e30

    @pl.when(fine)
    def _():
        store([(top, total, acc) for top, (total, acc) in zip(tops, state)])

    @pl.when(jnp.logical_not(fine))
    def _():
        begin = tuple((top, total, acc) for top, (total, acc) in zip(tops, start))
        store(lax.fori_loop(0, last, careful, begin))


def attn_forward(me, q, k_twice, v_turned, first, pairs):
    rows = q.shape[0]
    length = k_twice.shape[1]
    blocks = length // rows
    scalars = jnp.concatenate([me, jnp.full((1,), first, jnp.int32)])
    return pl.pallas_call(
        attn_forward_kernel,
        grid_spec=pltpu.PrefetchScalarGridSpec(
            num_scalar_prefetch=1,
            grid=(pairs,),
            in_specs=[
                pl.BlockSpec((rows, LANES), lambda i, me: (0, first + i)),
                pl.BlockSpec((KV_HEADS, length, LANES), lambda i, me: (0, 0, 0)),
                pl.BlockSpec((KV_HEADS, HEAD, length), lambda i, me: (0, 0, 0)),
            ],
            out_specs=[
                pl.BlockSpec((rows, LANES), lambda i, me: (0, i)),
                pl.BlockSpec((1, 2, rows), lambda i, me: (i, 0, 0)),
            ],
        ),
        out_shape=[
            jax.ShapeDtypeStruct((rows, pairs * LANES), BF16),
            jax.ShapeDtypeStruct((pairs, 2, rows), F32),
        ],
        compiler_params=pltpu.CompilerParams(vmem_limit_bytes=VMEM_BYTES),
        cost_estimate=pl.CostEstimate(
            flops=32 * blocks * pairs * rows * rows * HEAD,
            bytes_accessed=4 * rows * pairs * LANES + 6 * length * LANES,
            transcendentals=blocks * 2 * pairs * rows * rows,
        ),
        name="attn_forward",
    )(scalars, q, k_twice, v_turned)


def attn_backward_kernel(spec, *refs):
    first, pairs, start, finish, carry_in, carry_out = spec
    refs = list(refs)
    me_ref, q_ref, k_ref, kt_ref, v_ref, o_ref, do_ref, lse_ref, cos_ref, sin_ref = refs[:10]
    at = 10
    if carry_in:
        raw_in = refs[at]
        at += 1
    dq_ref = refs[at]
    at += 1
    if finish is not None:
        folded = refs[at]
        at += 1
    if carry_out:
        raw_out = refs[at]
        at += 1
    acc, moved = refs[at:]
    step_index = pl.program_id(0)
    pair = step_index + first
    me = me_ref[0]
    rows = q_ref.shape[0]
    group = HEADS // KV_HEADS
    held = acc.shape[0]
    last = me * rows // UNIT
    allowed = seen(me, rows, last)

    @pl.when(step_index == 0)
    def _():
        if carry_in:
            pltpu.make_async_copy(raw_in, acc.at[0], moved.at[0]).start()
        else:
            acc[0] = jnp.zeros(acc.shape[1:], F32)
        for more in range(1, held):
            acc[more] = jnp.zeros(acc.shape[1:], F32)
        if carry_in:
            pltpu.make_async_copy(raw_in, acc.at[0], moved.at[0]).wait()

    products = do_ref[...].astype(F32) * o_ref[...].astype(F32)
    heads = []
    for parity in range(2):
        kv_head = (2 * pair + parity) // group
        mask = half_mask(parity, BF16)
        picks = jnp.broadcast_to(half_mask(parity, F32), (8, LANES))
        delta = lax.dot_general(
            picks,
            products,
            (((1,), (1,)), ((), ())),
            precision=lax.Precision.HIGHEST,
            preferred_element_type=F32,
        )[0:1, :]
        lse = lse_ref[0, parity : parity + 1, :]
        heads.append((kv_head, q_ref[...] * mask, do_ref[...] * mask, lse, delta))

    def unit_step(unit, dqs, masked):
        span = pl.ds(unit * UNIT, UNIT)
        probs, d_scores = [], []
        for kv_head, q_head, do_head, lse, delta in heads:
            p = jnp.exp(dot_nt(k_ref[kv_head, span, :], q_head) - lse)
            if masked:
                p = jnp.where(allowed, p, 0.0)
            d_p = dot_nt(v_ref[kv_head, span, :], do_head)
            probs.append(p.astype(BF16))
            d_scores.append((p * (d_p - delta)).astype(BF16))
        after = []
        for (kv_head, q_head, do_head, _, _), p, d_s, dq in zip(heads, probs, d_scores, dqs):
            place = kv_head - start
            acc[place, 1, span, :] += dot_nn(p, do_head)
            acc[place, 0, span, :] += dot_nn(d_s, q_head)
            after.append(dq + dot_nn(kt_ref[kv_head, :, span], d_s))
        return tuple(after)

    zero = jnp.zeros((HEAD, rows), F32)
    dqs = unit_step(last, (zero, zero), True)
    dqs = lax.fori_loop(0, last, lambda unit, dqs: unit_step(unit, dqs, False), dqs)
    dq = jnp.transpose(jnp.concatenate(dqs, axis=0)) * HEAD ** (-0.5)
    dq_ref[...] = (dq * cos_ref[...] + swap_halves(dq * sin_ref[...])).astype(BF16)

    @pl.when(step_index == pairs - 1)
    def _():
        if carry_out:
            leave = pltpu.make_async_copy(acc.at[held - 1], raw_out, moved.at[1])
            leave.start()
        if finish is not None:
            low = half_mask(0, jnp.int32) > 0

            def fold(block, carry):
                span = pl.ds(block * rows, rows)
                keys = acc[0, 0, span, :]
                values = acc[0, 1, span, :]
                keys = keys + pltpu.roll(keys, HEAD, 1)
                values = values + pltpu.roll(values, HEAD, 1)
                folded[span, :] = jnp.where(low, keys, values).astype(BF16)
                return carry

            lax.fori_loop(0, acc.shape[2] // rows, fold, 0)
        if carry_out:
            leave.wait()


def attn_backward(me, tensors, tables, first, pairs, raw=None):
    q, k_twice, k_turned, v_twice, o, d_o, lse = tensors
    rows = q.shape[0]
    length = k_twice.shape[1]
    blocks = length // rows
    group = HEADS // KV_HEADS
    start = 2 * first // group
    end = (2 * (first + pairs) - 1) // group
    finish = start if 2 * (first + pairs) >= group * (start + 1) else None
    carry_out = finish is None or end > start
    spec = (first, pairs, start, finish, raw is not None, carry_out)
    once = {"pipeline_mode": pl.Buffered(1)}
    whole = pl.BlockSpec((KV_HEADS, length, LANES), lambda i, me: (0, 0, 0), **once)
    turned = pl.BlockSpec((KV_HEADS, HEAD, length), lambda i, me: (0, 0, 0), **once)
    pair = pl.BlockSpec((rows, LANES), lambda i, me: (0, first + i))
    table = pl.BlockSpec((rows, LANES), lambda i, me: (0, 0))
    raw_shape = jax.ShapeDtypeStruct((2, length, LANES), F32)
    raw_spec = pl.BlockSpec(memory_space=pl.ANY)
    in_specs = [
        pair,
        whole,
        turned,
        whole,
        pair,
        pair,
        pl.BlockSpec((1, 2, rows), lambda i, me: (first + i, 0, 0)),
        table,
        table,
    ]
    operands = [q, k_twice, k_turned, v_twice, o, d_o, lse, *tables]
    if raw is not None:
        in_specs.append(raw_spec)
        operands.append(raw)
    out_specs = [pl.BlockSpec((rows, LANES), lambda i, me: (0, i))]
    out_shape = [jax.ShapeDtypeStruct((rows, pairs * LANES), BF16)]
    if finish is not None:
        out_specs.append(pl.BlockSpec((length, LANES), lambda i, me: (0, 0)))
        out_shape.append(jax.ShapeDtypeStruct((length, LANES), BF16))
    if carry_out:
        out_specs.append(raw_spec)
        out_shape.append(raw_shape)
    outs = pl.pallas_call(
        functools.partial(attn_backward_kernel, spec),
        grid_spec=pltpu.PrefetchScalarGridSpec(
            num_scalar_prefetch=1,
            grid=(pairs,),
            in_specs=in_specs,
            out_specs=out_specs,
            scratch_shapes=[
                pltpu.VMEM((end - start + 1, 2, length, LANES), F32),
                pltpu.SemaphoreType.DMA((2,)),
            ],
        ),
        out_shape=out_shape,
        compiler_params=pltpu.CompilerParams(vmem_limit_bytes=VMEM_BYTES),
        cost_estimate=pl.CostEstimate(
            flops=80 * blocks * pairs * rows * rows * HEAD,
            bytes_accessed=8 * rows * pairs * LANES + 16 * length * LANES,
            transcendentals=blocks * 2 * pairs * rows * rows,
        ),
        name="attn_backward",
    )(me, *operands)
    dq = outs[0]
    folded = outs[1] if finish is not None else None
    return dq, folded, outs[-1] if carry_out else None


def feed_kernel(spans, place_ref, ha_ref, hb_ref, ca_ref, cb_ref, *refs):
    pieces = refs[: len(spans)]
    outa_ref, outb_ref, dha_ref, dhb_ref, hid_ref, dg_ref, du_ref = refs[len(spans) : -2]
    w_ref, arrived = refs[-2:]
    tiles = FF_PART // FF_TILE
    step = pl.program_id(0)
    former = step < pl.num_programs(0) // 2

    def fetch(index):
        piece, (column, width) = pieces[index], spans[index]
        rows = piece.shape[0]
        start = pl.multiple_of(place_ref[index] * rows, 16)
        target = w_ref.at[pl.ds(start, rows), pl.ds(column, width)]
        return pltpu.make_async_copy(piece, target, arrived.at[index])

    @pl.when(step == 0)
    def _():
        for index in range(len(spans)):
            fetch(index).start()
        for index in range(len(spans)):
            fetch(index).wait()

    h = jnp.where(former, ha_ref[...], hb_ref[...])
    c = jnp.where(former, ca_ref[...], cb_ref[...])
    for t in range(tiles):

        def weights(m):
            start = m * FF_PART + t * FF_TILE
            return w_ref[:, start : start + FF_TILE]

        gate = dot_nn(h, weights(0))
        up = dot_nn(h, weights(1))
        d_hid = dot_nn(c, weights(2))
        sig = jax.nn.sigmoid(gate)
        silu = gate * sig
        span = slice(t * FF_TILE, (t + 1) * FF_TILE)
        hid_ref[:, span] = (silu * up).astype(BF16)
        dg_ref[:, span] = (d_hid * up * sig * (1.0 + gate * (1.0 - sig))).astype(BF16)
        du_ref[:, span] = (d_hid * silu).astype(BF16)
    gates = w_ref[:, :FF_PART]
    ups = w_ref[:, FF_PART : 2 * FF_PART]
    downs = w_ref[:, 2 * FF_PART :]
    d_h = (dot_nt(dg_ref[...], gates) + dot_nt(du_ref[...], ups)).astype(BF16)
    out = dot_nt(hid_ref[...], downs).astype(BF16)

    @pl.when(former)
    def _():
        dha_ref[...] = d_h
        outa_ref[...] = out

    @pl.when(jnp.logical_not(former))
    def _():
        dhb_ref[...] = d_h
        outb_ref[...] = out


def feed(h_pair, c_pair, pieces):
    count = h_pair[0].shape[0]
    rows = 256
    steps = count // rows
    one = pl.BlockSpec((rows, D), lambda i, place: (jnp.minimum(i, steps - 1), 0))
    two = pl.BlockSpec((rows, D), lambda i, place: (jnp.maximum(i - steps, 0), 0))
    hidden = pl.BlockSpec((rows, FF_PART), lambda i, place: (i, 0))
    spans = tuple((column, array.shape[1]) for array, _, column in pieces)
    places = jnp.stack([jnp.asarray(place, jnp.int32) for _, place, _ in pieces])
    return pl.pallas_call(
        functools.partial(feed_kernel, spans),
        grid_spec=pltpu.PrefetchScalarGridSpec(
            num_scalar_prefetch=1,
            grid=(2 * steps,),
            in_specs=[one, two, one, two] + [pl.BlockSpec(memory_space=pl.ANY)] * len(pieces),
            out_specs=[one, two, one, two, hidden, hidden, hidden],
            scratch_shapes=[
                pltpu.VMEM((D, 3 * FF_PART), BF16),
                pltpu.SemaphoreType.DMA((len(pieces),)),
            ],
        ),
        out_shape=[jax.ShapeDtypeStruct((count, D), BF16)] * 4
        + [jax.ShapeDtypeStruct((2 * count, FF_PART), BF16)] * 3,
        compiler_params=pltpu.CompilerParams(vmem_limit_bytes=VMEM_BYTES),
        cost_estimate=pl.CostEstimate(
            flops=40 * count * D * FF_PART,
            bytes_accessed=6 * D * FF_PART + 16 * count * D + 12 * count * FF_PART,
            transcendentals=2 * count * FF_PART,
        ),
        name="feed",
    )(places, *h_pair, *c_pair, *[array for array, _, _ in pieces])


def prepare_kernel(kv_ref, k_ref, v_ref, kt_ref, vt_ref):
    low = half_mask(0, jnp.int32) > 0
    for place, twice, turned in ((0, k_ref, kt_ref), (1, v_ref, vt_ref)):
        block = kv_ref[:, place * LANES : (place + 1) * LANES].astype(F32)
        other = pltpu.roll(block, HEAD, 1)
        twice[0] = jnp.where(low, block, other).astype(BF16)
        twice[1] = jnp.where(low, other, block).astype(BF16)
        across = jnp.transpose(block).astype(BF16)
        turned[0] = across[:HEAD]
        turned[1] = across[HEAD:]


def prepare(kv_whole):
    length = kv_whole.shape[0]
    rows = 512
    twice = pl.BlockSpec((KV_HEADS, rows, LANES), lambda i: (0, i, 0))
    turned = pl.BlockSpec((KV_HEADS, HEAD, rows), lambda i: (0, 0, i))
    return pl.pallas_call(
        prepare_kernel,
        grid=(length // rows,),
        in_specs=[pl.BlockSpec((rows, 2 * KW), lambda i: (i, 0))],
        out_specs=[twice, twice, turned, turned],
        out_shape=[jax.ShapeDtypeStruct((KV_HEADS, length, LANES), BF16)] * 2
        + [jax.ShapeDtypeStruct((KV_HEADS, HEAD, length), BF16)] * 2,
        cost_estimate=pl.CostEstimate(
            flops=8 * length * LANES, bytes_accessed=16 * length * LANES, transcendentals=0
        ),
        name="prepare",
    )(kv_whole)


def ring_order(place, count):
    up = 2 * place - 1
    down = 2 * (count - place)
    if isinstance(place, int):
        return 0 if place == 0 else up if place <= count // 2 else down
    return jnp.where(place == 0, 0, jnp.where(place <= count // 2, up, down))


class Ring:
    def __init__(self, count):
        order = [ring_order(place, count) for place in range(count)]
        self.count = count
        self.half = count // 2
        self.ahead = [(order[i], order[(i + 1) % count]) for i in range(count)]
        self.back = [(b, a) for a, b in self.ahead]
        mine = lax.axis_index("shard")
        self.place = jnp.where(mine % 2 == 1, (mine + 1) // 2, (count - mine // 2) % count)

    def owner(self, offset):
        return ring_order((self.place + self.count + offset) % self.count, self.count)

    def send(self, array, ahead):
        return lax.ppermute(array, "shard", self.ahead if ahead else self.back)


def tie(flows, *others):
    count = 2 * len(flows)
    sides = [side for flow in flows for side in (flow.right, flow.left)]
    tied = lax.optimization_barrier((*sides, *others))
    for index, flow in enumerate(flows):
        flow.right, flow.left = tied[2 * index : 2 * index + 2]
    others = tied[count:]
    return others[0] if len(others) == 1 else others


class Gather:
    def __init__(self, ring, array):
        self.ring = ring
        self.rows, self.cols = array.shape
        self.cut = (self.cols // (2 * LANES)) * LANES
        self.own = self.right = self.left = array
        self.done = 0
        self.pieces = [(array, 0, 0)]

    def step(self):
        self.done += 1
        if self.done < self.ring.half:
            self.right = self.ring.send(self.right, True)
            self.left = self.ring.send(self.left, False)
            self.pieces += [(self.right, -self.done, 0), (self.left, self.done, 0)]
        else:
            self.right = self.ring.send(self.right[:, : self.cut], True)
            self.left = self.ring.send(self.left[:, self.cut :], False)
            self.pieces += [(self.right, self.done, 0), (self.left, self.done, self.cut)]

    def placed(self):
        return [(piece, self.ring.owner(offset), column) for piece, offset, column in self.pieces]

    def result(self):
        whole = jnp.tile(self.own, (self.ring.count, 1))
        for piece, owner, column in self.placed()[1:]:
            whole = lax.dynamic_update_slice(whole, piece, (owner * self.rows, column))
        return whole

    def run(self):
        while self.done < self.ring.half:
            self.step()
        return self.result()


class ScatterSum:
    def __init__(self, ring, array):
        self.ring = ring
        self.array = array
        self.rows = array.shape[0] // ring.count
        self.cols = array.shape[1]
        self.cut = (self.cols // (2 * LANES)) * LANES
        self.done = 0
        far = self.chunk(ring.half)
        self.right = far[:, : self.cut]
        self.left = far[:, self.cut :]

    def chunk(self, offset):
        start = (self.ring.owner(offset) * self.rows, 0)
        return lax.dynamic_slice(self.array, start, (self.rows, self.cols))

    def add(self, offset, got, first, last):
        near = self.chunk(offset)
        part = (near[:, first:last].astype(F32) + got.astype(F32)).astype(BF16)
        return jnp.concatenate([near[:, :first], part, near[:, last:]], axis=1)

    def step(self):
        if self.done:
            offset = self.ring.half - self.done
            part = (0, self.cut, self.cols) if self.done == 1 else (0, self.cols, 0)
            self.right = self.add(offset, self.right, 0, part[1])
            self.left = self.add(-offset, self.left, part[1] if self.done == 1 else 0, self.cols)
        self.right = self.ring.send(self.right, True)
        self.left = self.ring.send(self.left, False)
        self.done += 1

    def result(self):
        return self.chunk(0).astype(F32) + self.right.astype(F32) + self.left.astype(F32)


def spread_sum(array):
    count = lax.axis_size("shard")
    arrived = lax.all_to_all(array, "shard", 0, 0, tiled=True)
    blocks = arrived.reshape(count, array.shape[0] // count, array.shape[1])
    return jnp.sum(blocks.astype(F32), axis=0)


def team_send(array, bit):
    return lax.ppermute(array, "rep", [(i, i ^ bit) for i in range(lax.axis_size("rep"))])


def team_sum(mine, core, cross, both):
    gathered = (cross.astype(F32) + team_send(both, 1).astype(F32)).astype(BF16)
    return (
        mine.astype(F32)
        + team_send(core, 1).astype(F32)
        + team_send(gathered, 2).astype(F32)
    )


def rope_tables(positions):
    half_width = HEAD // 2
    inverse = jnp.exp(
        jnp.arange(half_width, dtype=F32) * (-2.0 * math.log(ROPE_BASE) / HEAD)
    )
    angles = positions.astype(F32)[:, None] * inverse[None, :]
    cosine = jnp.cos(angles)
    sine = jnp.sin(angles)
    return (
        jnp.concatenate([cosine] * 4, axis=1),
        jnp.concatenate([-sine, sine, -sine, sine], axis=1),
    )


def rotate(source, cosine, sine):
    times = source.shape[1] // LANES
    return source * jnp.tile(cosine, (1, times)) + swap_halves(source) * jnp.tile(sine, (1, times))


def rotate_back(source, cosine, sine):
    times = source.shape[1] // LANES
    return source * jnp.tile(cosine, (1, times)) + swap_halves(source * jnp.tile(sine, (1, times)))


def norm_back(grad_normed, normed, inv_scale, gain_row):
    scaled = grad_normed * gain_row
    return inv_scale * (scaled - normed * jnp.mean(scaled * normed, axis=1, keepdims=True))


def body(
    hidden_in,
    cotangent,
    norm_gains,
    q_bias,
    kv_bias,
    q_weight,
    kv_weight,
    out_weight,
    gate_weight,
    up_weight,
    down_weight,
):
    tok_rows = hidden_in.shape[1]
    shard_count = lax.axis_size("shard")
    rep_count = lax.axis_size("rep")
    shard_place = lax.axis_index("shard")
    rep_place = lax.axis_index("rep")
    team_place = rep_place % TEAM
    row_share = D // shard_count
    kv_share = 2 * KW // shard_count
    ring = Ring(shard_count)
    core_place = rep_place % 2
    qkv_width = QW + 2 * KW
    teams = rep_count // TEAM
    across = [[t * TEAM + i for t in range(teams)] for i in range(TEAM)]

    small = jnp.concatenate([norm_gains[0], norm_gains[1], q_bias, kv_bias])
    spare = jnp.pad(small[None, :], ((0, 15), (0, qkv_width - small.shape[0])))
    qkv_piece = jnp.concatenate([jnp.concatenate([q_weight, kv_weight], axis=1), spare], axis=0)
    half_rows = (row_share + 16) // 2
    qkv_half = lax.dynamic_slice_in_dim(qkv_piece, core_place * half_rows, half_rows, 0)
    qkv_flow = Gather(ring, qkv_half)
    qkv_flow.step()
    gate_weight, up_weight, down_weight = tie([qkv_flow], gate_weight, up_weight, down_weight)

    def quarter(weight):
        padded = jnp.pad(weight, ((0, 0), (0, TEAM * FF_PART - FF)))
        return lax.dynamic_slice_in_dim(padded, team_place * FF_PART, FF_PART, 1)

    feed_piece = jnp.concatenate(
        [quarter(gate_weight), quarter(up_weight), quarter(down_weight)], axis=1
    )
    for _ in range(ring.half - 1):
        qkv_flow.step()
    feed_piece, out_weight = tie([qkv_flow], feed_piece, out_weight)
    mine = qkv_flow.result()
    other = team_send(mine, 1)
    halves = (jnp.where(core_place == 0, mine, other), jnp.where(core_place == 0, other, mine))
    qkv_all = jnp.concatenate(
        [half.reshape(shard_count, half_rows, qkv_width) for half in halves], axis=1
    )
    qkv_full = qkv_all[:, :row_share].reshape(D, qkv_width)
    smalls = qkv_all[:, row_share].astype(F32)
    gain_one = smalls[:, :row_share].reshape(D)
    gain_two = smalls[:, row_share : 2 * row_share].reshape(D)
    q_bias_all = smalls[:, 2 * row_share : 3 * row_share].reshape(QW)
    kv_bias_all = smalls[:, 3 * row_share : 3 * row_share + kv_share].reshape(2 * KW)
    q_full = qkv_full[:, :QW]
    kv_full = qkv_full[:, QW:]

    grad_out = cotangent[0]
    inputs = hidden_in[0].astype(F32)
    inv_one = lax.rsqrt(jnp.mean(inputs * inputs, axis=1, keepdims=True) + EPS)
    normed_one = inputs * inv_one
    h_one = (normed_one * gain_one).astype(BF16)
    positions = shard_place * tok_rows + jnp.arange(tok_rows, dtype=jnp.int32)
    cosine, sine = rope_tables(positions)
    keyvals = dot_nn(h_one, kv_full) + kv_bias_all
    kv_local = jnp.concatenate(
        [rotate(keyvals[:, :KW], cosine, sine), keyvals[:, KW:]], axis=1
    ).astype(BF16)

    feeding = Gather(ring, feed_piece)
    out_flow = Gather(ring, out_weight)
    flows = [feeding, out_flow]
    out_flow.step()
    feeding.step()
    kv_flow = Gather(ring, kv_local)
    kv_flow.step()
    grad_out = tie([kv_flow], grad_out)
    c_core = team_send(grad_out, 1)
    c_cross = team_send(grad_out, 2)
    kv_whole = kv_flow.run()
    queries = dot_nn(h_one, q_full) + q_bias_all
    q_scaled = rotate(queries, cosine, sine).astype(BF16) * jnp.asarray(HEAD ** (-0.5), BF16)
    me = shard_place.astype(jnp.int32).reshape(1)
    kv_whole = tie(flows, kv_whole)
    out_flow.step()
    feeding.step()
    k_twice, v_twice, k_turned, v_turned = prepare(kv_whole)
    attn_one, lse_one = attn_forward(me, q_scaled, k_twice, v_turned, 0, 3)
    attn_one, q_scaled = tie(flows, attn_one, q_scaled)
    out_flow.step()
    feeding.step()
    attn_two, lse_two = attn_forward(me, q_scaled, k_twice, v_turned, 3, 3)
    attn_two, q_scaled = tie(flows, attn_two, q_scaled)
    out_flow.step()
    feeding.step()
    attn_three, lse_three = attn_forward(me, q_scaled, k_twice, v_turned, 6, 1)
    attn_b = jnp.concatenate([attn_one, attn_two, attn_three], axis=1)
    lse = jnp.concatenate([lse_one, lse_two, lse_three], axis=0)
    out_full = out_flow.result()

    middle = inputs + dot_nt(attn_b, out_full)
    inv_two = lax.rsqrt(jnp.mean(middle * middle, axis=1, keepdims=True) + EPS)
    normed_two = middle * inv_two
    h_two = (normed_two * gain_two).astype(BF16)
    if row_share % 16:
        feed_pieces = [(feeding.result(), 0, 0)]
    else:
        feed_pieces = feeding.placed()

    c_both = team_send(c_cross, 1)
    h_core = team_send(h_two, 1)
    h_cross = team_send(h_two, 2)
    h_both = team_send(h_cross, 1)
    here = feed((h_two, h_core), (grad_out, c_core), feed_pieces)
    there = feed((h_cross, h_both), (c_cross, c_both), feed_pieces)
    out_parts = (here[0], here[1], there[0], there[1])
    dh_mine, dh_core, dh_cross, dh_both = here[2], here[3], there[2], there[3]

    dh_home = team_send(dh_core, 1)
    dh_away = (dh_cross.astype(F32) + team_send(dh_both, 1).astype(F32)).astype(BF16)
    dh_away, *hidden = lax.optimization_barrier((dh_away, *there[4:]))
    dh_back = team_send(dh_away, 2)
    h_sets = jnp.concatenate([h_two, h_core, h_cross, h_both], axis=0)
    c_sets = jnp.concatenate([grad_out, c_core, c_cross, c_both], axis=0)
    hid_sets, dg_sets, du_sets = (
        jnp.concatenate(pair, axis=0) for pair in zip(here[4:], hidden)
    )
    gate_grads = dot_tn(h_sets, dg_sets).astype(BF16)
    up_grads = dot_tn(h_sets, du_sets).astype(BF16)
    down_grads = dot_tn(c_sets, hid_sets).astype(BF16)
    feed_grads = jnp.concatenate([gate_grads, up_grads, down_grads], axis=1)
    dh_back, feed_grads, *out_parts = lax.optimization_barrier((dh_back, feed_grads, *out_parts))
    grad_h_two = dh_mine.astype(F32) + dh_home.astype(F32) + dh_back.astype(F32)
    feed_sum = ScatterSum(ring, feed_grads)
    feed_sum.step()

    gain_two_grad = jnp.sum(grad_h_two * normed_two, axis=0)
    grad_middle = grad_out.astype(F32) + norm_back(grad_h_two, normed_two, inv_two, gain_two)
    grad_branch_b = grad_middle.astype(BF16)
    grad_attn = dot_nn(grad_branch_b, out_full).astype(BF16)
    out_sum_flow = ScatterSum(ring, dot_tn(grad_branch_b, attn_b).astype(BF16))

    tables = (cosine, sine)

    def backward(first, pairs, raw):
        tensors = (q_scaled, k_twice, k_turned, v_twice, attn_b, grad_attn, lse)
        return attn_backward(me, tensors, tables, first, pairs, raw)

    flows = [feed_sum, out_sum_flow]
    grad_attn = tie([feed_sum], grad_attn)
    feed_sum.step()
    out_sum_flow.step()
    out_sum = team_sum(*out_parts)
    output = middle + out_sum
    dq_one, _, raw = backward(0, 2, None)
    dq_one, raw, grad_attn, output = tie(flows, dq_one, raw, grad_attn, output)
    out_sum_flow.step()
    feed_sum.step()
    dq_two, dkv_zero, raw = backward(2, 2, raw)
    dkv_zero, raw, grad_attn = tie(flows, dkv_zero, raw, grad_attn)
    out_sum_flow.step()
    feed_sum.step()
    zero_sum = spread_sum(dkv_zero)
    dq_three, _, raw = backward(4, 2, raw)
    dq_three, raw, grad_attn, zero_sum = tie(flows, dq_three, raw, grad_attn, zero_sum)
    out_sum_flow.step()
    feed_rows = feed_sum.result().astype(BF16)
    feed_core = team_send(feed_rows, 1)
    feed_cross = team_send(feed_rows, 2)
    dq_early = jnp.concatenate([dq_one, dq_two, dq_three], axis=1)
    early_sum = spread_sum(dot_tn(h_one, dq_early).astype(BF16)).astype(BF16)
    dq_four, dkv_one, _ = backward(6, 1, raw)
    early_sum, dkv_one, feed_cross = tie([out_sum_flow], early_sum, dkv_one, feed_cross)
    one_sum = spread_sum(dkv_one)
    grad_q_b = jnp.concatenate([dq_early, dq_four], axis=1)

    def team_total(rows):
        rows = (rows.astype(F32) + team_send(rows, 1).astype(F32)).astype(BF16)
        rows = rows.astype(F32) + team_send(rows, 2).astype(F32)
        if teams > 1:
            rows = lax.psum(rows.astype(BF16), "rep", axis_index_groups=across).astype(F32)
        return rows

    q_bias_sum = jnp.sum(grad_q_b.astype(F32), axis=0)
    grad_h_q = dot_nt(grad_q_b, q_full)
    early_rows = team_total(early_sum)

    grad_k = jnp.concatenate([zero_sum[:, :HEAD], one_sum[:, :HEAD]], axis=1)
    grad_v = jnp.concatenate([zero_sum[:, HEAD:], one_sum[:, HEAD:]], axis=1)
    grad_kv_b = jnp.concatenate([rotate_back(grad_k, cosine, sine), grad_v], axis=1).astype(BF16)
    kv_bias_sum = jnp.sum(grad_kv_b.astype(F32), axis=0)
    grad_h_one = grad_h_q + dot_nt(grad_kv_b, kv_full)
    gain_one_grad = jnp.sum(grad_h_one * normed_one, axis=0)
    input_grad = (grad_middle + norm_back(grad_h_one, normed_one, inv_one, gain_one)).astype(BF16)

    late = jnp.concatenate([grad_kv_b, dq_four], axis=1)
    width = late.shape[1]
    late_weight = dot_tn(h_one, late).reshape(shard_count, row_share, width)
    smalls = jnp.concatenate(
        [
            one.reshape(shard_count, -1)
            for one in (gain_one_grad, gain_two_grad, q_bias_sum, kv_bias_sum)
        ],
        axis=1,
    )
    smalls = jnp.pad(smalls, ((0, 0), (0, 16 * width - smalls.shape[1])))
    last_sum = jnp.concatenate([late_weight, smalls.reshape(shard_count, 16, width)], axis=1)
    last_sum = spread_sum(last_sum.reshape(-1, width).astype(BF16))
    last_rows = team_total(last_sum.astype(BF16))
    kv_rows = last_rows[:row_share, : 2 * KW]
    q_rows = jnp.concatenate([early_rows, last_rows[:row_share, 2 * KW :]], axis=1)
    smalls = last_rows[row_share:].reshape(-1)
    gains_grad = smalls[: 2 * row_share].reshape(2, row_share)
    q_bias_grad = smalls[2 * row_share : 3 * row_share]
    kv_bias_grad = smalls[3 * row_share : 3 * row_share + kv_share]

    out_rows = team_total(out_sum_flow.result().astype(BF16))
    feed_parts = [feed_rows, feed_core, feed_cross, team_send(feed_cross, 1)]
    if teams > 1:
        feed_parts = [lax.psum(part, "rep", axis_index_groups=across) for part in feed_parts]

    def columns(matrix):
        whole = jnp.zeros((row_share, TEAM * FF_PART), F32)
        for bit, part in enumerate(feed_parts):
            part = part[:, matrix * FF_PART : (matrix + 1) * FF_PART].astype(F32)
            whole = lax.dynamic_update_slice(whole, part, (0, (team_place ^ bit) * FF_PART))
        return whole[:, :FF]

    gate_grad, up_grad, down_grad = (columns(matrix) for matrix in range(3))
    return (
        output.astype(BF16)[None],
        input_grad[None],
        gains_grad,
        q_bias_grad,
        kv_bias_grad,
        q_rows,
        kv_rows,
        out_rows,
        gate_grad,
        up_grad,
        down_grad,
    )


def solution(mesh):
    tokens = P("rep", "shard", None)
    rows = P("shard", None)
    placed = (tokens, tokens, P(None, "shard"), P("shard"), P("shard")) + (rows,) * 6
    return jax.shard_map(body, mesh=mesh, in_specs=placed, out_specs=placed, check_vma=False)
```

```python
import functools
import math

import jax
import jax.numpy as jnp
from jax import lax
from jax.experimental import pallas as pl
from jax.experimental.pallas import tpu as pltpu
from jax.sharding import PartitionSpec as P

D = 896
HEADS = 14
KV_HEADS = 2
HEAD = 64
FF = 4864
QW = 896
KW = 128
LANES = 128
TEAM = 4
FF_PART = 1280
FF_TILE = 256
UNIT = 1024

EPS = 1e-06
ROPE_BASE = 1000000.0
F32 = jnp.float32
BF16 = jnp.bfloat16
VMEM_BYTES = 56 * 1024 * 1024


def dot_nt(left, right):
    return lax.dot_general(left, right, (((1,), (1,)), ((), ())), preferred_element_type=F32)


def dot_tn(left, right):
    return lax.dot_general(left, right, (((0,), (0,)), ((), ())), preferred_element_type=F32)


def dot_nn(left, right):
    return jnp.dot(left, right, preferred_element_type=F32)


def half_mask(parity, kind):
    lane = lax.broadcasted_iota(jnp.int32, (1, LANES), 1)
    return ((lane // HEAD) == parity).astype(kind)


def swap_halves(source):
    lane = lax.broadcasted_iota(jnp.int32, source.shape, 1)
    ahead = jnp.roll(source, -(HEAD // 2), axis=1)
    behind = jnp.roll(source, HEAD // 2, axis=1)
    return jnp.where(lane % HEAD < HEAD // 2, ahead, behind)


def seen(me, rows, unit):
    base = (me * rows // UNIT) * UNIT
    key = lax.broadcasted_iota(jnp.int32, (UNIT, rows), 0) + base
    query = lax.broadcasted_iota(jnp.int32, (UNIT, rows), 1) + me * rows
    return key <= query


def attn_forward_kernel(me_ref, q_ref, k_ref, vt_ref, o_ref, lse_ref):
    pair = pl.program_id(0) + me_ref[1]
    me = me_ref[0]
    rows = q_ref.shape[0]
    group = HEADS // KV_HEADS
    last = me * rows // UNIT
    allowed = seen(me, rows, last)
    heads = [((2 * pair + parity) // group, q_ref[...] * half_mask(parity, BF16)) for parity in range(2)]

    def span(unit):
        return pl.ds(unit * UNIT, UNIT)

    def scores(head, unit):
        return dot_nt(k_ref[head[0], span(unit), :], head[1])

    def weigh(head, unit, probs):
        return dot_nn(vt_ref[head[0], :, span(unit)], probs.astype(BF16))

    tops, probs = [], []
    for head in heads:
        s = jnp.where(allowed, scores(head, last), -1e30)
        tops.append(jnp.max(s, axis=0, keepdims=True))
        probs.append(jnp.exp(s - tops[-1]))
    start = tuple(
        (jnp.sum(p, axis=0, keepdims=True), weigh(head, last, p)) for head, p in zip(heads, probs)
    )

    def quick(unit, state):
        probs = [jnp.exp(scores(head, unit) - top) for head, top in zip(heads, tops)]
        return tuple(
            (total + jnp.sum(p, axis=0, keepdims=True), acc + weigh(head, unit, p))
            for head, (total, acc), p in zip(heads, state, probs)
        )

    def careful(unit, state):
        after = []
        for head, (top, total, acc) in zip(heads, state):
            s = scores(head, unit)
            new_top = jnp.maximum(top, jnp.max(s, axis=0, keepdims=True))
            shrink = jnp.exp(top - new_top)
            p = jnp.exp(s - new_top)
            total = total * shrink + jnp.sum(p, axis=0, keepdims=True)
            after.append((new_top, total, acc * shrink + weigh(head, unit, p)))
        return tuple(after)

    def store(state):
        for parity, (top, total, acc) in enumerate(state):
            lse_ref[0, parity : parity + 1, :] = top + jnp.log(total)
        both = jnp.concatenate([acc / total for top, total, acc in state], axis=0)
        o_ref[...] = jnp.transpose(both).astype(BF16)

    state = lax.fori_loop(0, last, quick, start)
    largest = jnp.max(jnp.maximum(state[0][0], state[1][0]))
    fine = largest < 1e30

    @pl.when(fine)
    def _():
        store([(top, total, acc) for top, (total, acc) in zip(tops, state)])

    @pl.when(jnp.logical_not(fine))
    def _():
        begin = tuple((top, total, acc) for top, (total, acc) in zip(tops, start))
        store(lax.fori_loop(0, last, careful, begin))


def attn_forward(me, q, k_twice, v_turned, first, pairs):
    rows = q.shape[0]
    length = k_twice.shape[1]
    blocks = length // rows
    scalars = jnp.concatenate([me, jnp.full((1,), first, jnp.int32)])
    return pl.pallas_call(
        attn_forward_kernel,
        grid_spec=pltpu.PrefetchScalarGridSpec(
            num_scalar_prefetch=1,
            grid=(pairs,),
            in_specs=[
                pl.BlockSpec((rows, LANES), lambda i, me: (0, first + i)),
                pl.BlockSpec((KV_HEADS, length, LANES), lambda i, me: (0, 0, 0)),
                pl.BlockSpec((KV_HEADS, HEAD, length), lambda i, me: (0, 0, 0)),
            ],
            out_specs=[
                pl.BlockSpec((rows, LANES), lambda i, me: (0, i)),
                pl.BlockSpec((1, 2, rows), lambda i, me: (i, 0, 0)),
            ],
        ),
        out_shape=[
            jax.ShapeDtypeStruct((rows, pairs * LANES), BF16),
            jax.ShapeDtypeStruct((pairs, 2, rows), F32),
        ],
        compiler_params=pltpu.CompilerParams(vmem_limit_bytes=VMEM_BYTES),
        cost_estimate=pl.CostEstimate(
            flops=32 * blocks * pairs * rows * rows * HEAD,
            bytes_accessed=4 * rows * pairs * LANES + 6 * length * LANES,
            transcendentals=blocks * 2 * pairs * rows * rows,
        ),
        name="attn_forward",
    )(scalars, q, k_twice, v_turned)


def attn_backward_kernel(spec, *refs):
    first, pairs, start, finish, carry_in, carry_out = spec
    refs = list(refs)
    me_ref, q_ref, k_ref, kt_ref, v_ref, o_ref, do_ref, lse_ref, cos_ref, sin_ref = refs[:10]
    at = 10
    if carry_in:
        raw_in = refs[at]
        at += 1
    dq_ref = refs[at]
    at += 1
    if finish is not None:
        folded = refs[at]
        at += 1
    if carry_out:
        raw_out = refs[at]
        at += 1
    acc, moved = refs[at:]
    step_index = pl.program_id(0)
    pair = step_index + first
    me = me_ref[0]
    rows = q_ref.shape[0]
    group = HEADS // KV_HEADS
    held = acc.shape[0]
    last = me * rows // UNIT
    allowed = seen(me, rows, last)

    @pl.when(step_index == 0)
    def _():
        if carry_in:
            pltpu.make_async_copy(raw_in, acc.at[0], moved.at[0]).start()
        else:
            acc[0] = jnp.zeros(acc.shape[1:], F32)
        for more in range(1, held):
            acc[more] = jnp.zeros(acc.shape[1:], F32)
        if carry_in:
            pltpu.make_async_copy(raw_in, acc.at[0], moved.at[0]).wait()

    products = do_ref[...].astype(F32) * o_ref[...].astype(F32)
    heads = []
    for parity in range(2):
        kv_head = (2 * pair + parity) // group
        mask = half_mask(parity, BF16)
        picks = jnp.broadcast_to(half_mask(parity, F32), (8, LANES))
        delta = lax.dot_general(
            picks,
            products,
            (((1,), (1,)), ((), ())),
            precision=lax.Precision.HIGHEST,
            preferred_element_type=F32,
        )[0:1, :]
        lse = lse_ref[0, parity : parity + 1, :]
        heads.append((kv_head, q_ref[...] * mask, do_ref[...] * mask, lse, delta))

    def unit_step(unit, dqs, masked):
        span = pl.ds(unit * UNIT, UNIT)
        probs, d_scores = [], []
        for kv_head, q_head, do_head, lse, delta in heads:
            p = jnp.exp(dot_nt(k_ref[kv_head, span, :], q_head) - lse)
            if masked:
                p = jnp.where(allowed, p, 0.0)
            d_p = dot_nt(v_ref[kv_head, span, :], do_head)
            probs.append(p.astype(BF16))
            d_scores.append((p * (d_p - delta)).astype(BF16))
        after = []
        for (kv_head, q_head, do_head, _, _), p, d_s, dq in zip(heads, probs, d_scores, dqs):
            place = kv_head - start
            acc[place, 1, span, :] += dot_nn(p, do_head)
            acc[place, 0, span, :] += dot_nn(d_s, q_head)
            after.append(dq + dot_nn(kt_ref[kv_head, :, span], d_s))
        return tuple(after)

    zero = jnp.zeros((HEAD, rows), F32)
    dqs = unit_step(last, (zero, zero), True)
    dqs = lax.fori_loop(0, last, lambda unit, dqs: unit_step(unit, dqs, False), dqs)
    dq = jnp.transpose(jnp.concatenate(dqs, axis=0)) * HEAD ** (-0.5)
    dq_ref[...] = (dq * cos_ref[...] + swap_halves(dq * sin_ref[...])).astype(BF16)

    @pl.when(step_index == pairs - 1)
    def _():
        if carry_out:
            leave = pltpu.make_async_copy(acc.at[held - 1], raw_out, moved.at[1])
            leave.start()
        if finish is not None:
            low = half_mask(0, jnp.int32) > 0

            def fold(block, carry):
                span = pl.ds(block * rows, rows)
                keys = acc[0, 0, span, :]
                values = acc[0, 1, span, :]
                keys = keys + pltpu.roll(keys, HEAD, 1)
                values = values + pltpu.roll(values, HEAD, 1)
                folded[span, :] = jnp.where(low, keys, values).astype(BF16)
                return carry

            lax.fori_loop(0, acc.shape[2] // rows, fold, 0)
        if carry_out:
            leave.wait()


def attn_backward(me, tensors, tables, first, pairs, raw=None):
    q, k_twice, k_turned, v_twice, o, d_o, lse = tensors
    rows = q.shape[0]
    length = k_twice.shape[1]
    blocks = length // rows
    group = HEADS // KV_HEADS
    start = 2 * first // group
    end = (2 * (first + pairs) - 1) // group
    finish = start if 2 * (first + pairs) >= group * (start + 1) else None
    carry_out = finish is None or end > start
    spec = (first, pairs, start, finish, raw is not None, carry_out)
    once = {"pipeline_mode": pl.Buffered(1)}
    whole = pl.BlockSpec((KV_HEADS, length, LANES), lambda i, me: (0, 0, 0), **once)
    turned = pl.BlockSpec((KV_HEADS, HEAD, length), lambda i, me: (0, 0, 0), **once)
    pair = pl.BlockSpec((rows, LANES), lambda i, me: (0, first + i))
    table = pl.BlockSpec((rows, LANES), lambda i, me: (0, 0))
    raw_shape = jax.ShapeDtypeStruct((2, length, LANES), F32)
    raw_spec = pl.BlockSpec(memory_space=pl.ANY)
    in_specs = [
        pair,
        whole,
        turned,
        whole,
        pair,
        pair,
        pl.BlockSpec((1, 2, rows), lambda i, me: (first + i, 0, 0)),
        table,
        table,
    ]
    operands = [q, k_twice, k_turned, v_twice, o, d_o, lse, *tables]
    if raw is not None:
        in_specs.append(raw_spec)
        operands.append(raw)
    out_specs = [pl.BlockSpec((rows, LANES), lambda i, me: (0, i))]
    out_shape = [jax.ShapeDtypeStruct((rows, pairs * LANES), BF16)]
    if finish is not None:
        out_specs.append(pl.BlockSpec((length, LANES), lambda i, me: (0, 0)))
        out_shape.append(jax.ShapeDtypeStruct((length, LANES), BF16))
    if carry_out:
        out_specs.append(raw_spec)
        out_shape.append(raw_shape)
    outs = pl.pallas_call(
        functools.partial(attn_backward_kernel, spec),
        grid_spec=pltpu.PrefetchScalarGridSpec(
            num_scalar_prefetch=1,
            grid=(pairs,),
            in_specs=in_specs,
            out_specs=out_specs,
            scratch_shapes=[
                pltpu.VMEM((end - start + 1, 2, length, LANES), F32),
                pltpu.SemaphoreType.DMA((2,)),
            ],
        ),
        out_shape=out_shape,
        compiler_params=pltpu.CompilerParams(vmem_limit_bytes=VMEM_BYTES),
        cost_estimate=pl.CostEstimate(
            flops=80 * blocks * pairs * rows * rows * HEAD,
            bytes_accessed=8 * rows * pairs * LANES + 16 * length * LANES,
            transcendentals=blocks * 2 * pairs * rows * rows,
        ),
        name="attn_backward",
    )(me, *operands)
    dq = outs[0]
    folded = outs[1] if finish is not None else None
    return dq, folded, outs[-1] if carry_out else None


def feed_kernel(sets, spans, place_ref, *refs):
    h_refs, c_refs, refs = refs[:sets], refs[sets : 2 * sets], refs[2 * sets :]
    pieces, refs = refs[: len(spans)], refs[len(spans) :]
    out_refs, dh_refs, refs = refs[:sets], refs[sets : 2 * sets], refs[2 * sets :]
    hid_ref, dg_ref, du_ref, w_ref, arrived = refs
    tiles = FF_PART // FF_TILE
    step = pl.program_id(0)
    former = step < pl.num_programs(0) // sets

    def fetch(index):
        piece, (column, width) = pieces[index], spans[index]
        rows = piece.shape[0]
        start = pl.multiple_of(place_ref[index] * rows, 16)
        source = piece.at[:, pl.ds(0, width)]
        target = w_ref.at[pl.ds(start, rows), pl.ds(column, width)]
        return pltpu.make_async_copy(source, target, arrived.at[index])

    @pl.when(step == 0)
    def _():
        for index in range(len(spans)):
            fetch(index).start()
        for index in range(len(spans)):
            fetch(index).wait()

    if sets == 1:
        h, c = h_refs[0][...], c_refs[0][...]
    else:
        h = jnp.where(former, h_refs[0][...], h_refs[1][...])
        c = jnp.where(former, c_refs[0][...], c_refs[1][...])
    for t in range(tiles):

        def weights(m):
            start = m * FF_PART + t * FF_TILE
            return w_ref[:, start : start + FF_TILE]

        gate = dot_nn(h, weights(0))
        up = dot_nn(h, weights(1))
        d_hid = dot_nn(c, weights(2))
        sig = jax.nn.sigmoid(gate)
        silu = gate * sig
        span = slice(t * FF_TILE, (t + 1) * FF_TILE)
        hid_ref[:, span] = (silu * up).astype(BF16)
        dg_ref[:, span] = (d_hid * up * sig * (1.0 + gate * (1.0 - sig))).astype(BF16)
        du_ref[:, span] = (d_hid * silu).astype(BF16)
    gates = w_ref[:, :FF_PART]
    ups = w_ref[:, FF_PART : 2 * FF_PART]
    downs = w_ref[:, 2 * FF_PART :]
    d_h = (dot_nt(dg_ref[...], gates) + dot_nt(du_ref[...], ups)).astype(BF16)
    out = dot_nt(hid_ref[...], downs).astype(BF16)

    @pl.when(former)
    def _():
        dh_refs[0][...] = d_h
        out_refs[0][...] = out

    @pl.when(jnp.logical_not(former))
    def _():
        dh_refs[-1][...] = d_h
        out_refs[-1][...] = out


def feed(h_sets, c_sets, pieces, places):
    sets = len(h_sets)
    count = h_sets[0].shape[0]
    rows = 256
    steps = count // rows
    one = pl.BlockSpec((rows, D), lambda i, place: (jnp.minimum(i, steps - 1), 0))
    two = pl.BlockSpec((rows, D), lambda i, place: (jnp.maximum(i - steps, 0), 0))
    token_specs = [one, two][:sets]
    hidden = pl.BlockSpec((rows, FF_PART), lambda i, place: (i, 0))
    spans = tuple(
        (column, min(array.shape[1], 3 * FF_PART - column)) for array, column in pieces
    )
    return pl.pallas_call(
        functools.partial(feed_kernel, sets, spans),
        grid_spec=pltpu.PrefetchScalarGridSpec(
            num_scalar_prefetch=1,
            grid=(sets * steps,),
            in_specs=token_specs * 2 + [pl.BlockSpec(memory_space=pl.ANY)] * len(pieces),
            out_specs=token_specs * 2 + [hidden, hidden, hidden],
            scratch_shapes=[
                pltpu.VMEM((D, 3 * FF_PART), BF16),
                pltpu.SemaphoreType.DMA((len(pieces),)),
            ],
        ),
        out_shape=[jax.ShapeDtypeStruct((count, D), BF16)] * (2 * sets)
        + [jax.ShapeDtypeStruct((sets * count, FF_PART), BF16)] * 3,
        compiler_params=pltpu.CompilerParams(vmem_limit_bytes=VMEM_BYTES),
        cost_estimate=pl.CostEstimate(
            flops=20 * sets * count * D * FF_PART,
            bytes_accessed=6 * D * FF_PART + sets * count * (8 * D + 6 * FF_PART),
            transcendentals=sets * count * FF_PART,
        ),
        name="feed",
    )(places, *h_sets, *c_sets, *[array for array, _ in pieces])


def columns_kernel(team_ref, *refs):
    parts, outs = refs[:TEAM], refs[TEAM:]
    team = team_ref[0]
    for place in range(TEAM):
        bit = team ^ place
        width = min(FF_PART, FF - place * FF_PART)
        for matrix, out in enumerate(outs):
            span = slice(matrix * FF_PART, matrix * FF_PART + width)
            low = jnp.where(bit == 0, parts[0][:, span].astype(F32), parts[1][:, span].astype(F32))
            high = jnp.where(bit == 2, parts[2][:, span].astype(F32), parts[3][:, span].astype(F32))
            out[:, place * FF_PART : place * FF_PART + width] = jnp.where(bit < 2, low, high)


def columns(team_place, parts):
    rows = parts[0].shape[0]
    return pl.pallas_call(
        columns_kernel,
        grid_spec=pltpu.PrefetchScalarGridSpec(
            num_scalar_prefetch=1,
            grid=(1,),
            in_specs=[pl.BlockSpec((rows, 3 * FF_PART), lambda i, team: (0, 0))] * TEAM,
            out_specs=[pl.BlockSpec((rows, FF), lambda i, team: (0, 0))] * 3,
        ),
        out_shape=[jax.ShapeDtypeStruct((rows, FF), F32)] * 3,
        compiler_params=pltpu.CompilerParams(vmem_limit_bytes=VMEM_BYTES),
        cost_estimate=pl.CostEstimate(
            flops=rows * FF, bytes_accessed=20 * rows * FF, transcendentals=0
        ),
        name="columns",
    )(team_place.astype(jnp.int32).reshape(1), *parts)


def project_kernel(first, h_ref, w_ref, b_ref, cos_ref, sin_ref, out_ref):
    block = pl.program_id(0) + first
    flat = dot_nn(h_ref[...], w_ref[...]) + b_ref[...]
    turned = flat * cos_ref[...] + swap_halves(flat) * sin_ref[...]
    kept = jnp.where(block < (QW + KW) // LANES, turned, flat)
    scale = jnp.where(block < QW // LANES, HEAD ** (-0.5), 1.0)
    out_ref[...] = (kept * scale).astype(BF16)


def project(h, weights, bias, cosine, sine, first, count):
    rows = h.shape[0]
    table = pl.BlockSpec((rows, LANES), lambda i: (0, 0))
    return pl.pallas_call(
        functools.partial(project_kernel, first),
        grid=(count,),
        in_specs=[
            pl.BlockSpec((rows, D), lambda i: (0, 0)),
            pl.BlockSpec((D, LANES), lambda i: (0, first + i)),
            pl.BlockSpec((1, LANES), lambda i: (0, first + i)),
            table,
            table,
        ],
        out_specs=pl.BlockSpec((rows, LANES), lambda i: (0, i)),
        out_shape=jax.ShapeDtypeStruct((rows, count * LANES), BF16),
        cost_estimate=pl.CostEstimate(
            flops=2 * rows * D * count * LANES,
            bytes_accessed=2 * (D * count * LANES + rows * D),
            transcendentals=0,
        ),
        name="project",
    )(h, weights, bias, cosine, sine)


def prepare_kernel(kv_ref, k_ref, v_ref, kt_ref, vt_ref):
    low = half_mask(0, jnp.int32) > 0
    for place, twice, turned in ((0, k_ref, kt_ref), (1, v_ref, vt_ref)):
        block = kv_ref[:, place * LANES : (place + 1) * LANES].astype(F32)
        other = pltpu.roll(block, HEAD, 1)
        twice[0] = jnp.where(low, block, other).astype(BF16)
        twice[1] = jnp.where(low, other, block).astype(BF16)
        across = jnp.transpose(block).astype(BF16)
        turned[0] = across[:HEAD]
        turned[1] = across[HEAD:]


def prepare(kv_whole):
    length = kv_whole.shape[0]
    rows = 512
    twice = pl.BlockSpec((KV_HEADS, rows, LANES), lambda i: (0, i, 0))
    turned = pl.BlockSpec((KV_HEADS, HEAD, rows), lambda i: (0, 0, i))
    return pl.pallas_call(
        prepare_kernel,
        grid=(length // rows,),
        in_specs=[pl.BlockSpec((rows, 2 * KW), lambda i: (i, 0))],
        out_specs=[twice, twice, turned, turned],
        out_shape=[jax.ShapeDtypeStruct((KV_HEADS, length, LANES), BF16)] * 2
        + [jax.ShapeDtypeStruct((KV_HEADS, HEAD, length), BF16)] * 2,
        cost_estimate=pl.CostEstimate(
            flops=8 * length * LANES, bytes_accessed=16 * length * LANES, transcendentals=0
        ),
        name="prepare",
    )(kv_whole)


def ring_order(place, count):
    up = 2 * place - 1
    down = 2 * (count - place)
    if isinstance(place, int):
        return 0 if place == 0 else up if place <= count // 2 else down
    return jnp.where(place == 0, 0, jnp.where(place <= count // 2, up, down))


class Ring:
    def __init__(self, count):
        order = [ring_order(place, count) for place in range(count)]
        self.count = count
        self.half = count // 2
        self.ahead = [(order[i], order[(i + 1) % count]) for i in range(count)]
        self.back = [(b, a) for a, b in self.ahead]
        mine = lax.axis_index("shard")
        self.place = jnp.where(mine % 2 == 1, (mine + 1) // 2, (count - mine // 2) % count)

    def owner(self, offset):
        return ring_order((self.place + self.count + offset) % self.count, self.count)

    def send(self, array, ahead):
        return lax.ppermute(array, "shard", self.ahead if ahead else self.back)


def tie(flows, *others):
    count = 2 * len(flows)
    sides = [side for flow in flows for side in (flow.right, flow.left)]
    tied = lax.optimization_barrier((*sides, *others))
    for index, flow in enumerate(flows):
        flow.right, flow.left = tied[2 * index : 2 * index + 2]
    others = tied[count:]
    return others[0] if len(others) == 1 else others


class Gather:
    def __init__(self, ring, array):
        self.ring = ring
        self.rows, self.cols = array.shape
        self.cut = (self.cols // (2 * LANES)) * LANES
        self.own = self.right = self.left = array
        self.done = 0
        self.pieces = [(array, 0, 0)]

    def step(self):
        self.done += 1
        if self.done < self.ring.half:
            self.right = self.ring.send(self.right, True)
            self.left = self.ring.send(self.left, False)
            self.pieces += [(self.right, -self.done, 0), (self.left, self.done, 0)]
        else:
            self.right = self.ring.send(self.right[:, : self.cut], True)
            self.left = self.ring.send(self.left[:, self.cut :], False)
            self.pieces += [(self.right, self.done, 0), (self.left, self.done, self.cut)]

    def owners(self):
        index = jnp.arange(len(self.pieces), dtype=jnp.int32)
        offset = (index + 1) // 2
        return self.ring.owner(jnp.where(index % 2 == 1, -offset, offset))

    def result(self, first=0):
        count = self.ring.count
        cols = self.cols - first
        whole = jnp.broadcast_to(self.own[None, :, first:], (count, self.rows, cols))
        for piece, offset, column in self.pieces[1:]:
            skip = max(first - column, 0)
            if skip < piece.shape[1]:
                start = (self.ring.owner(offset), 0, column + skip - first)
                whole = lax.dynamic_update_slice(whole, piece[None, :, skip:], start)
        return whole.reshape(count * self.rows, cols)

    def run(self):
        while self.done < self.ring.half:
            self.step()
        return self.result()


class ScatterSum:
    def __init__(self, ring, arrays):
        self.ring = ring
        self.rows = arrays[0].shape[0] // ring.count
        self.cols = sum(array.shape[1] for array in arrays)
        self.arrays = [array.reshape(ring.count, self.rows, -1) for array in arrays]
        self.cut = (self.cols // (2 * LANES)) * LANES
        self.done = 0
        far = self.chunk(ring.half)
        self.right = far[:, : self.cut]
        self.left = far[:, self.cut :]

    def chunk(self, offset):
        owner = self.ring.owner(offset)
        return jnp.concatenate(
            [lax.dynamic_index_in_dim(array, owner, 0, keepdims=False) for array in self.arrays],
            axis=1,
        )

    def add(self, offset, got, first, last):
        near = self.chunk(offset)
        part = (near[:, first:last].astype(F32) + got.astype(F32)).astype(BF16)
        return jnp.concatenate([near[:, :first], part, near[:, last:]], axis=1)

    def step(self):
        if self.done:
            offset = self.ring.half - self.done
            part = (0, self.cut, self.cols) if self.done == 1 else (0, self.cols, 0)
            self.right = self.add(offset, self.right, 0, part[1])
            self.left = self.add(-offset, self.left, part[1] if self.done == 1 else 0, self.cols)
        self.right = self.ring.send(self.right, True)
        self.left = self.ring.send(self.left, False)
        self.done += 1

    def result(self):
        return self.chunk(0).astype(F32) + self.right.astype(F32) + self.left.astype(F32)


def spread_sum(array):
    count = lax.axis_size("shard")
    arrived = lax.all_to_all(array, "shard", 0, 0, tiled=True)
    blocks = arrived.reshape(count, array.shape[0] // count, array.shape[1])
    return jnp.sum(blocks.astype(F32), axis=0)


def team_send(array, bit):
    return lax.ppermute(array, "rep", [(i, i ^ bit) for i in range(lax.axis_size("rep"))])


def team_sum(mine, core, cross, both):
    gathered = (cross.astype(F32) + team_send(both, 1).astype(F32)).astype(BF16)
    return (
        mine.astype(F32)
        + team_send(core, 1).astype(F32)
        + team_send(gathered, 2).astype(F32)
    )


def rope_tables(positions):
    half_width = HEAD // 2
    inverse = jnp.exp(
        jnp.arange(half_width, dtype=F32) * (-2.0 * math.log(ROPE_BASE) / HEAD)
    )
    angles = positions.astype(F32)[:, None] * inverse[None, :]
    cosine = jnp.cos(angles)
    sine = jnp.sin(angles)
    return (
        jnp.concatenate([cosine] * 4, axis=1),
        jnp.concatenate([-sine, sine, -sine, sine], axis=1),
    )


def rotate(source, cosine, sine):
    times = source.shape[1] // LANES
    return source * jnp.tile(cosine, (1, times)) + swap_halves(source) * jnp.tile(sine, (1, times))


def rotate_back(source, cosine, sine):
    times = source.shape[1] // LANES
    return source * jnp.tile(cosine, (1, times)) + swap_halves(source * jnp.tile(sine, (1, times)))


def norm_back(grad_normed, normed, inv_scale, gain_row):
    scaled = grad_normed * gain_row
    return inv_scale * (scaled - normed * jnp.mean(scaled * normed, axis=1, keepdims=True))


def body(
    hidden_in,
    cotangent,
    norm_gains,
    q_bias,
    kv_bias,
    q_weight,
    kv_weight,
    out_weight,
    gate_weight,
    up_weight,
    down_weight,
):
    tok_rows = hidden_in.shape[1]
    shard_count = lax.axis_size("shard")
    rep_count = lax.axis_size("rep")
    shard_place = lax.axis_index("shard")
    rep_place = lax.axis_index("rep")
    team_place = rep_place % TEAM
    row_share = D // shard_count
    kv_share = 2 * KW // shard_count
    ring = Ring(shard_count)
    core_place = rep_place % 2
    qkv_width = QW + 2 * KW
    teams = rep_count // TEAM
    across = [[t * TEAM + i for t in range(teams)] for i in range(TEAM)]

    small = jnp.concatenate([norm_gains[0], norm_gains[1], q_bias, kv_bias])
    spare = jnp.pad(small[None, :], ((0, 15), (0, qkv_width - small.shape[0])))
    qkv_piece = jnp.concatenate([jnp.concatenate([q_weight, kv_weight], axis=1), spare], axis=0)
    half_rows = (row_share + 16) // 2
    qkv_half = lax.dynamic_slice_in_dim(qkv_piece, core_place * half_rows, half_rows, 0)
    grad_out = cotangent[0]
    qkv_flow = Gather(ring, qkv_half)
    qkv_flow.step()
    c_cross = team_send(grad_out, 2)
    gate_weight, up_weight, down_weight, out_weight = tie(
        [qkv_flow], gate_weight, up_weight, down_weight, out_weight
    )

    def quarter(weight):
        padded = jnp.pad(weight, ((0, 0), (0, TEAM * FF_PART - FF)))
        return lax.dynamic_slice_in_dim(padded, team_place * FF_PART, FF_PART, 1)

    feed_piece = jnp.concatenate(
        [quarter(gate_weight), quarter(up_weight), quarter(down_weight), out_weight], axis=1
    )
    for _ in range(ring.half - 1):
        qkv_flow.step()
    feed_piece, c_cross = tie([qkv_flow], feed_piece, c_cross)
    mine = qkv_flow.result()
    other = team_send(mine, 1)
    halves = (jnp.where(core_place == 0, mine, other), jnp.where(core_place == 0, other, mine))
    qkv_all = jnp.concatenate(
        [half.reshape(shard_count, half_rows, qkv_width) for half in halves], axis=1
    )
    qkv_full = qkv_all[:, :row_share].reshape(D, qkv_width)
    smalls = qkv_all[:, row_share].astype(F32)
    gain_one = smalls[:, :row_share].reshape(D)
    gain_two = smalls[:, row_share : 2 * row_share].reshape(D)
    q_bias_all = smalls[:, 2 * row_share : 3 * row_share].reshape(QW)
    kv_bias_all = smalls[:, 3 * row_share : 3 * row_share + kv_share].reshape(2 * KW)
    bias = jnp.concatenate([q_bias_all, kv_bias_all])[None, :]
    q_full = qkv_full[:, :QW]
    kv_full = qkv_full[:, QW:]

    inputs = hidden_in[0].astype(F32)
    inv_one = lax.rsqrt(jnp.mean(inputs * inputs, axis=1, keepdims=True) + EPS)
    normed_one = inputs * inv_one
    h_one = (normed_one * gain_one).astype(BF16)
    positions = shard_place * tok_rows + jnp.arange(tok_rows, dtype=jnp.int32)
    cosine, sine = rope_tables(positions)
    kv_local = project(h_one, qkv_full, bias, cosine, sine, QW // LANES, 2 * KW // LANES)

    feeding = Gather(ring, feed_piece)
    flows = [feeding]
    feeding.step()
    kv_flow = Gather(ring, kv_local)
    kv_flow.step()
    late_out = tie([kv_flow], grad_out)
    c_both = team_send(late_out, 3)
    kv_whole = kv_flow.run()
    q_scaled = project(h_one, qkv_full, bias, cosine, sine, 0, QW // LANES)
    me = shard_place.astype(jnp.int32).reshape(1)
    kv_whole, late_out = tie(flows, kv_whole, late_out)
    c_core = team_send(late_out, 1)
    feeding.step()
    k_twice, v_twice, k_turned, v_turned = prepare(kv_whole)
    attn_one, lse_one = attn_forward(me, q_scaled, k_twice, v_turned, 0, 3)
    attn_one, q_scaled, c_core, c_both = tie(flows, attn_one, q_scaled, c_core, c_both)
    feeding.step()
    attn_two, lse_two = attn_forward(me, q_scaled, k_twice, v_turned, 3, 3)
    attn_two, q_scaled = tie(flows, attn_two, q_scaled)
    feeding.step()
    attn_three, lse_three = attn_forward(me, q_scaled, k_twice, v_turned, 6, 1)
    attn_three = tie(flows, attn_three)
    attn_b = jnp.concatenate([attn_one, attn_two, attn_three], axis=1)
    lse = jnp.concatenate([lse_one, lse_two, lse_three], axis=0)
    out_full = feeding.result(3 * FF_PART)

    middle = inputs + dot_nt(attn_b, out_full)
    inv_two = lax.rsqrt(jnp.mean(middle * middle, axis=1, keepdims=True) + EPS)
    normed_two = middle * inv_two
    h_two = (normed_two * gain_two).astype(BF16)
    if row_share % 16:
        feed_pieces = [(feeding.result(), 0)]
        feed_places = jnp.zeros((1,), jnp.int32)
    else:
        feed_pieces = [(piece, column) for piece, _, column in feeding.pieces]
        feed_places = feeding.owners()

    h_core = team_send(h_two, 1)
    h_cross = team_send(h_two, 2)
    here = feed((h_two, h_core), (grad_out, c_core), feed_pieces, feed_places)
    h_cross, *here = lax.optimization_barrier((h_cross, *here))
    h_both = team_send(h_cross, 1)
    cross = feed((h_cross,), (c_cross,), feed_pieces, feed_places)
    h_both, *cross = lax.optimization_barrier((h_both, *cross))
    both = feed((h_both,), (c_both,), feed_pieces, feed_places)
    out_parts = (here[0], here[1], cross[0], both[0])
    dh_mine, dh_core, dh_cross, dh_both = here[2], here[3], cross[1], both[1]

    dh_home = team_send(dh_core, 1)
    dh_away = (dh_cross.astype(F32) + team_send(dh_both, 1).astype(F32)).astype(BF16)
    dh_away, *hidden = lax.optimization_barrier((dh_away, *both[2:]))
    dh_back = team_send(dh_away, 2)
    h_sets = jnp.concatenate([h_two, h_core, h_cross, h_both], axis=0)
    c_sets = jnp.concatenate([grad_out, c_core, c_cross, c_both], axis=0)
    hid_sets, dg_sets, du_sets = (
        jnp.concatenate(parts, axis=0) for parts in zip(here[4:], cross[2:], hidden)
    )
    gate_grads = dot_tn(h_sets, dg_sets).astype(BF16)
    up_grads = dot_tn(h_sets, du_sets).astype(BF16)
    down_grads = dot_tn(c_sets, hid_sets).astype(BF16)
    dh_back, gate_grads, up_grads, down_grads = lax.optimization_barrier(
        (dh_back, gate_grads, up_grads, down_grads)
    )
    grad_h_two = dh_mine.astype(F32) + dh_home.astype(F32) + dh_back.astype(F32)

    gain_two_grad = jnp.sum(grad_h_two * normed_two, axis=0)
    grad_middle = grad_out.astype(F32) + norm_back(grad_h_two, normed_two, inv_two, gain_two)
    grad_branch_b = grad_middle.astype(BF16)
    grad_attn = dot_nn(grad_branch_b, out_full).astype(BF16)
    out_grads = dot_tn(grad_branch_b, attn_b).astype(BF16)
    row_sum = ScatterSum(ring, [gate_grads, up_grads, down_grads, out_grads])
    row_sum.step()

    tables = (cosine, sine)

    def backward(first, pairs, raw):
        tensors = (q_scaled, k_twice, k_turned, v_twice, attn_b, grad_attn, lse)
        return attn_backward(me, tensors, tables, first, pairs, raw)

    flows = [row_sum]
    grad_attn = tie(flows, grad_attn)
    row_sum.step()
    dq_one, _, raw = backward(0, 2, None)
    dq_one, raw, grad_attn = tie(flows, dq_one, raw, grad_attn)
    row_sum.step()
    dq_two, dkv_zero, raw = backward(2, 2, raw)
    dkv_zero, raw, grad_attn = tie(flows, dkv_zero, raw, grad_attn)
    row_sum.step()
    zero_sum = spread_sum(dkv_zero)
    dq_three, dkv_one, _ = backward(4, 3, raw)
    dq_three, dkv_one, zero_sum, *out_parts = tie(flows, dq_three, dkv_one, zero_sum, *out_parts)
    one_sum = spread_sum(dkv_one)
    mine = row_sum.result().astype(BF16)
    core = team_send(mine, 1)
    cross = team_send(mine, 2)
    output = middle + team_sum(*out_parts)
    one_sum, dq_three = lax.optimization_barrier((one_sum, dq_three))
    grad_q_b = jnp.concatenate([dq_one, dq_two, dq_three], axis=1)

    def team_total(rows):
        core, cross, both = (team_send(rows, bit).astype(F32) for bit in (1, 2, 3))
        rows = (rows.astype(F32) + core) + (cross + both)
        if teams > 1:
            rows = lax.psum(rows.astype(BF16), "rep", axis_index_groups=across).astype(F32)
        return rows

    q_bias_sum = jnp.sum(grad_q_b.astype(F32), axis=0)
    grad_h_q = dot_nt(grad_q_b, q_full)
    q_grads = dot_tn(h_one, grad_q_b).astype(BF16)
    q_grads = q_grads.reshape(shard_count, 2, 2, row_share // TEAM, QW)

    def halve(array, axis, place, bit):
        keep = lax.dynamic_index_in_dim(array, place, axis, keepdims=False)
        give = lax.dynamic_index_in_dim(array, 1 - place, axis, keepdims=False)
        return (keep.astype(F32) + team_send(give, bit).astype(F32)).astype(BF16)

    q_grads = halve(halve(q_grads, 2, core_place, 1), 1, team_place // 2, 2)
    q_part = spread_sum(q_grads.reshape(-1, QW))

    grad_k = jnp.concatenate([zero_sum[:, :HEAD], one_sum[:, :HEAD]], axis=1)
    grad_v = jnp.concatenate([zero_sum[:, HEAD:], one_sum[:, HEAD:]], axis=1)
    grad_kv_b = jnp.concatenate([rotate_back(grad_k, cosine, sine), grad_v], axis=1).astype(BF16)
    kv_bias_sum = jnp.sum(grad_kv_b.astype(F32), axis=0)
    grad_h_one = grad_h_q + dot_nt(grad_kv_b, kv_full)
    gain_one_grad = jnp.sum(grad_h_one * normed_one, axis=0)
    input_grad = (grad_middle + norm_back(grad_h_one, normed_one, inv_one, gain_one)).astype(BF16)

    width = 2 * KW
    late_weight = dot_tn(h_one, grad_kv_b).reshape(shard_count, row_share, width)
    smalls = jnp.concatenate(
        [
            one.reshape(shard_count, -1)
            for one in (gain_one_grad, gain_two_grad, q_bias_sum, kv_bias_sum)
        ],
        axis=1,
    )
    smalls = jnp.pad(smalls, ((0, 0), (0, 16 * width - smalls.shape[1])))
    last_sum = jnp.concatenate([late_weight, smalls.reshape(shard_count, 16, width)], axis=1)
    last_sum = spread_sum(last_sum.reshape(-1, width).astype(BF16))
    last_rows = team_total(last_sum.astype(BF16))
    kv_rows = last_rows[:row_share]
    smalls = last_rows[row_share:].reshape(-1)
    gains_grad = smalls[: 2 * row_share].reshape(2, row_share)
    q_bias_grad = smalls[2 * row_share : 3 * row_share]
    kv_bias_grad = smalls[3 * row_share : 3 * row_share + kv_share]

    if teams > 1:
        q_part = lax.psum(q_part.astype(BF16), "rep", axis_index_groups=across)
    q_part = q_part.astype(BF16)
    q_parts = [q_part] + [team_send(q_part, bit) for bit in (1, 2, 3)]

    def quarter_at(place):
        bit = team_place ^ place
        low = jnp.where(bit == 0, q_parts[0], q_parts[1])
        return jnp.where(bit < 2, low, jnp.where(bit == 2, q_parts[2], q_parts[3]))

    q_rows = jnp.concatenate([quarter_at(place) for place in range(TEAM)], axis=0).astype(F32)
    parts = [mine, core, cross, team_send(cross, 1)]
    if teams > 1:
        parts = [lax.psum(part, "rep", axis_index_groups=across) for part in parts]
    outs = [part[:, 3 * FF_PART :].astype(F32) for part in parts]
    out_rows = (outs[0] + outs[1]) + (outs[2] + outs[3])
    gate_grad, up_grad, down_grad = columns(team_place, parts)
    return (
        output.astype(BF16)[None],
        input_grad[None],
        gains_grad,
        q_bias_grad,
        kv_bias_grad,
        q_rows,
        kv_rows,
        out_rows,
        gate_grad,
        up_grad,
        down_grad,
    )


def solution(mesh):
    tokens = P("rep", "shard", None)
    rows = P("shard", None)
    placed = (tokens, tokens, P(None, "shard"), P("shard"), P("shard")) + (rows,) * 6
    return jax.shard_map(body, mesh=mesh, in_specs=placed, out_specs=placed, check_vma=False)
```

```python
import functools
import math

import jax
import jax.numpy as jnp
from jax import lax
from jax.experimental import pallas as pl
from jax.experimental.pallas import tpu as pltpu
from jax.sharding import PartitionSpec as P

D = 896
HEADS = 14
KV_HEADS = 2
HEAD = 64
FF = 4864
QW = 896
KW = 128
LANES = 128
TEAM = 4
FF_PART = 1280
FF_TILE = 256
UNIT = 1024

EPS = 1e-06
ROPE_BASE = 1000000.0
F32 = jnp.float32
BF16 = jnp.bfloat16
VMEM_BYTES = 56 * 1024 * 1024


def dot_nt(left, right):
    return lax.dot_general(left, right, (((1,), (1,)), ((), ())), preferred_element_type=F32)


def dot_tn(left, right):
    return lax.dot_general(left, right, (((0,), (0,)), ((), ())), preferred_element_type=F32)


def dot_nn(left, right):
    return jnp.dot(left, right, preferred_element_type=F32)


def half_mask(parity, kind):
    lane = lax.broadcasted_iota(jnp.int32, (1, LANES), 1)
    return ((lane // HEAD) == parity).astype(kind)


def swap_halves(source):
    lane = lax.broadcasted_iota(jnp.int32, source.shape, 1)
    ahead = jnp.roll(source, -(HEAD // 2), axis=1)
    behind = jnp.roll(source, HEAD // 2, axis=1)
    return jnp.where(lane % HEAD < HEAD // 2, ahead, behind)


def seen(me, rows, unit):
    base = (me * rows // UNIT) * UNIT
    key = lax.broadcasted_iota(jnp.int32, (UNIT, rows), 0) + base
    query = lax.broadcasted_iota(jnp.int32, (UNIT, rows), 1) + me * rows
    return key <= query


def attn_forward_kernel(me_ref, q_ref, k_ref, vt_ref, o_ref, lse_ref):
    pair = pl.program_id(0) + me_ref[1]
    me = me_ref[0]
    rows = q_ref.shape[0]
    group = HEADS // KV_HEADS
    last = me * rows // UNIT
    allowed = seen(me, rows, last)
    heads = [((2 * pair + parity) // group, q_ref[...] * half_mask(parity, BF16)) for parity in range(2)]

    def span(unit):
        return pl.ds(unit * UNIT, UNIT)

    def scores(head, unit):
        return dot_nt(k_ref[head[0], span(unit), :], head[1])

    def weigh(head, unit, probs):
        return dot_nn(vt_ref[head[0], :, span(unit)], probs.astype(BF16))

    tops, probs = [], []
    for head in heads:
        s = jnp.where(allowed, scores(head, last), -1e30)
        tops.append(jnp.max(s, axis=0, keepdims=True))
        probs.append(jnp.exp(s - tops[-1]))
    start = tuple(
        (jnp.sum(p, axis=0, keepdims=True), weigh(head, last, p)) for head, p in zip(heads, probs)
    )

    def quick(unit, state):
        probs = [jnp.exp(scores(head, unit) - top) for head, top in zip(heads, tops)]
        return tuple(
            (total + jnp.sum(p, axis=0, keepdims=True), acc + weigh(head, unit, p))
            for head, (total, acc), p in zip(heads, state, probs)
        )

    def careful(unit, state):
        after = []
        for head, (top, total, acc) in zip(heads, state):
            s = scores(head, unit)
            new_top = jnp.maximum(top, jnp.max(s, axis=0, keepdims=True))
            shrink = jnp.exp(top - new_top)
            p = jnp.exp(s - new_top)
            total = total * shrink + jnp.sum(p, axis=0, keepdims=True)
            after.append((new_top, total, acc * shrink + weigh(head, unit, p)))
        return tuple(after)

    def store(state):
        for parity, (top, total, acc) in enumerate(state):
            lse_ref[0, parity : parity + 1, :] = top + jnp.log(total)
        both = jnp.concatenate([acc / total for top, total, acc in state], axis=0)
        o_ref[...] = jnp.transpose(both).astype(BF16)

    state = lax.fori_loop(0, last, quick, start)
    largest = jnp.max(jnp.maximum(state[0][0], state[1][0]))
    fine = largest < 1e30

    @pl.when(fine)
    def _():
        store([(top, total, acc) for top, (total, acc) in zip(tops, state)])

    @pl.when(jnp.logical_not(fine))
    def _():
        begin = tuple((top, total, acc) for top, (total, acc) in zip(tops, start))
        store(lax.fori_loop(0, last, careful, begin))


def attn_forward(me, q, k_twice, v_turned, first, pairs):
    rows = q.shape[0]
    length = k_twice.shape[1]
    blocks = length // rows
    scalars = jnp.concatenate([me, jnp.full((1,), first, jnp.int32)])
    return pl.pallas_call(
        attn_forward_kernel,
        grid_spec=pltpu.PrefetchScalarGridSpec(
            num_scalar_prefetch=1,
            grid=(pairs,),
            in_specs=[
                pl.BlockSpec((rows, LANES), lambda i, me: (0, first + i)),
                pl.BlockSpec((KV_HEADS, length, LANES), lambda i, me: (0, 0, 0)),
                pl.BlockSpec((KV_HEADS, HEAD, length), lambda i, me: (0, 0, 0)),
            ],
            out_specs=[
                pl.BlockSpec((rows, LANES), lambda i, me: (0, i)),
                pl.BlockSpec((1, 2, rows), lambda i, me: (i, 0, 0)),
            ],
        ),
        out_shape=[
            jax.ShapeDtypeStruct((rows, pairs * LANES), BF16),
            jax.ShapeDtypeStruct((pairs, 2, rows), F32),
        ],
        compiler_params=pltpu.CompilerParams(vmem_limit_bytes=VMEM_BYTES),
        cost_estimate=pl.CostEstimate(
            flops=32 * blocks * pairs * rows * rows * HEAD,
            bytes_accessed=4 * rows * pairs * LANES + 6 * length * LANES,
            transcendentals=blocks * 2 * pairs * rows * rows,
        ),
        name="attn_forward",
    )(scalars, q, k_twice, v_turned)


def attn_backward_kernel(spec, *refs):
    first, pairs, start, finish, carry_in, carry_out = spec
    refs = list(refs)
    me_ref, q_ref, k_ref, kt_ref, v_ref, o_ref, do_ref, lse_ref, cos_ref, sin_ref = refs[:10]
    at = 10
    if carry_in:
        raw_in = refs[at]
        at += 1
    dq_ref = refs[at]
    at += 1
    if finish is not None:
        folded = refs[at]
        at += 1
    if carry_out:
        raw_out = refs[at]
        at += 1
    acc, moved = refs[at:]
    step_index = pl.program_id(0)
    pair = step_index + first
    me = me_ref[0]
    rows = q_ref.shape[0]
    group = HEADS // KV_HEADS
    held = acc.shape[0]
    last = me * rows // UNIT
    allowed = seen(me, rows, last)

    @pl.when(step_index == 0)
    def _():
        if carry_in:
            pltpu.make_async_copy(raw_in, acc.at[0], moved.at[0]).start()
        else:
            acc[0] = jnp.zeros(acc.shape[1:], F32)
        for more in range(1, held):
            acc[more] = jnp.zeros(acc.shape[1:], F32)
        if carry_in:
            pltpu.make_async_copy(raw_in, acc.at[0], moved.at[0]).wait()

    products = do_ref[...].astype(F32) * o_ref[...].astype(F32)
    heads = []
    for parity in range(2):
        kv_head = (2 * pair + parity) // group
        mask = half_mask(parity, BF16)
        picks = jnp.broadcast_to(half_mask(parity, F32), (8, LANES))
        delta = lax.dot_general(
            picks,
            products,
            (((1,), (1,)), ((), ())),
            precision=lax.Precision.HIGHEST,
            preferred_element_type=F32,
        )[0:1, :]
        lse = lse_ref[0, parity : parity + 1, :]
        heads.append((kv_head, q_ref[...] * mask, do_ref[...] * mask, lse, delta))

    def unit_step(unit, dqs, masked):
        span = pl.ds(unit * UNIT, UNIT)
        probs, d_scores = [], []
        for kv_head, q_head, do_head, lse, delta in heads:
            p = jnp.exp(dot_nt(k_ref[kv_head, span, :], q_head) - lse)
            if masked:
                p = jnp.where(allowed, p, 0.0)
            d_p = dot_nt(v_ref[kv_head, span, :], do_head)
            probs.append(p.astype(BF16))
            d_scores.append((p * (d_p - delta)).astype(BF16))
        after = []
        for (kv_head, q_head, do_head, _, _), p, d_s, dq in zip(heads, probs, d_scores, dqs):
            place = kv_head - start
            acc[place, 1, span, :] += dot_nn(p, do_head)
            acc[place, 0, span, :] += dot_nn(d_s, q_head)
            after.append(dq + dot_nn(kt_ref[kv_head, :, span], d_s))
        return tuple(after)

    zero = jnp.zeros((HEAD, rows), F32)
    dqs = unit_step(last, (zero, zero), True)
    dqs = lax.fori_loop(0, last, lambda unit, dqs: unit_step(unit, dqs, False), dqs)
    dq = jnp.transpose(jnp.concatenate(dqs, axis=0)) * HEAD ** (-0.5)
    dq_ref[...] = (dq * cos_ref[...] + swap_halves(dq * sin_ref[...])).astype(BF16)

    @pl.when(step_index == pairs - 1)
    def _():
        if carry_out:
            leave = pltpu.make_async_copy(acc.at[held - 1], raw_out, moved.at[1])
            leave.start()
        if finish is not None:
            low = half_mask(0, jnp.int32) > 0

            def fold(block, carry):
                span = pl.ds(block * rows, rows)
                keys = acc[0, 0, span, :]
                values = acc[0, 1, span, :]
                keys = keys + pltpu.roll(keys, HEAD, 1)
                values = values + pltpu.roll(values, HEAD, 1)
                folded[span, :] = jnp.where(low, keys, values).astype(BF16)
                return carry

            lax.fori_loop(0, acc.shape[2] // rows, fold, 0)
        if carry_out:
            leave.wait()


def attn_backward(me, tensors, tables, first, pairs, raw=None):
    q, k_twice, k_turned, v_twice, o, d_o, lse = tensors
    rows = q.shape[0]
    length = k_twice.shape[1]
    blocks = length // rows
    group = HEADS // KV_HEADS
    start = 2 * first // group
    end = (2 * (first + pairs) - 1) // group
    finish = start if 2 * (first + pairs) >= group * (start + 1) else None
    carry_out = finish is None or end > start
    spec = (first, pairs, start, finish, raw is not None, carry_out)
    once = {"pipeline_mode": pl.Buffered(1)}
    whole = pl.BlockSpec((KV_HEADS, length, LANES), lambda i, me: (0, 0, 0), **once)
    turned = pl.BlockSpec((KV_HEADS, HEAD, length), lambda i, me: (0, 0, 0), **once)
    pair = pl.BlockSpec((rows, LANES), lambda i, me: (0, first + i))
    table = pl.BlockSpec((rows, LANES), lambda i, me: (0, 0))
    raw_shape = jax.ShapeDtypeStruct((2, length, LANES), F32)
    raw_spec = pl.BlockSpec(memory_space=pl.ANY)
    in_specs = [
        pair,
        whole,
        turned,
        whole,
        pair,
        pair,
        pl.BlockSpec((1, 2, rows), lambda i, me: (first + i, 0, 0)),
        table,
        table,
    ]
    operands = [q, k_twice, k_turned, v_twice, o, d_o, lse, *tables]
    if raw is not None:
        in_specs.append(raw_spec)
        operands.append(raw)
    out_specs = [pl.BlockSpec((rows, LANES), lambda i, me: (0, i))]
    out_shape = [jax.ShapeDtypeStruct((rows, pairs * LANES), BF16)]
    if finish is not None:
        out_specs.append(pl.BlockSpec((length, LANES), lambda i, me: (0, 0)))
        out_shape.append(jax.ShapeDtypeStruct((length, LANES), BF16))
    if carry_out:
        out_specs.append(raw_spec)
        out_shape.append(raw_shape)
    outs = pl.pallas_call(
        functools.partial(attn_backward_kernel, spec),
        grid_spec=pltpu.PrefetchScalarGridSpec(
            num_scalar_prefetch=1,
            grid=(pairs,),
            in_specs=in_specs,
            out_specs=out_specs,
            scratch_shapes=[
                pltpu.VMEM((end - start + 1, 2, length, LANES), F32),
                pltpu.SemaphoreType.DMA((2,)),
            ],
        ),
        out_shape=out_shape,
        compiler_params=pltpu.CompilerParams(vmem_limit_bytes=VMEM_BYTES),
        cost_estimate=pl.CostEstimate(
            flops=80 * blocks * pairs * rows * rows * HEAD,
            bytes_accessed=8 * rows * pairs * LANES + 16 * length * LANES,
            transcendentals=blocks * 2 * pairs * rows * rows,
        ),
        name="attn_backward",
    )(me, *operands)
    dq = outs[0]
    folded = outs[1] if finish is not None else None
    return dq, folded, outs[-1] if carry_out else None


def feed_kernel(sets, spans, place_ref, *refs):
    h_refs, c_refs, refs = refs[:sets], refs[sets : 2 * sets], refs[2 * sets :]
    pieces, refs = refs[: len(spans)], refs[len(spans) :]
    out_refs, dh_refs, refs = refs[:sets], refs[sets : 2 * sets], refs[2 * sets :]
    hid_ref, dg_ref, du_ref, w_ref, arrived = refs
    tiles = FF_PART // FF_TILE
    step = pl.program_id(0)
    former = step < pl.num_programs(0) // sets

    def fetch(index):
        piece, (column, width) = pieces[index], spans[index]
        rows = piece.shape[0]
        start = pl.multiple_of(place_ref[index] * rows, 16)
        source = piece.at[:, pl.ds(0, width)]
        target = w_ref.at[pl.ds(start, rows), pl.ds(column, width)]
        return pltpu.make_async_copy(source, target, arrived.at[index])

    @pl.when(step == 0)
    def _():
        for index in range(len(spans)):
            fetch(index).start()
        for index in range(len(spans)):
            fetch(index).wait()

    if sets == 1:
        h, c = h_refs[0][...], c_refs[0][...]
    else:
        h = jnp.where(former, h_refs[0][...], h_refs[1][...])
        c = jnp.where(former, c_refs[0][...], c_refs[1][...])
    for t in range(tiles):

        def weights(m):
            start = m * FF_PART + t * FF_TILE
            return w_ref[:, start : start + FF_TILE]

        gate = dot_nn(h, weights(0))
        up = dot_nn(h, weights(1))
        d_hid = dot_nn(c, weights(2))
        sig = jax.nn.sigmoid(gate)
        silu = gate * sig
        span = slice(t * FF_TILE, (t + 1) * FF_TILE)
        hid_ref[:, span] = (silu * up).astype(BF16)
        dg_ref[:, span] = (d_hid * up * sig * (1.0 + gate * (1.0 - sig))).astype(BF16)
        du_ref[:, span] = (d_hid * silu).astype(BF16)
    gates = w_ref[:, :FF_PART]
    ups = w_ref[:, FF_PART : 2 * FF_PART]
    downs = w_ref[:, 2 * FF_PART :]
    d_h = (dot_nt(dg_ref[...], gates) + dot_nt(du_ref[...], ups)).astype(BF16)
    out = dot_nt(hid_ref[...], downs).astype(BF16)

    @pl.when(former)
    def _():
        dh_refs[0][...] = d_h
        out_refs[0][...] = out

    @pl.when(jnp.logical_not(former))
    def _():
        dh_refs[-1][...] = d_h
        out_refs[-1][...] = out


def feed(h_sets, c_sets, pieces, places):
    sets = len(h_sets)
    count = h_sets[0].shape[0]
    rows = 256
    steps = count // rows
    one = pl.BlockSpec((rows, D), lambda i, place: (jnp.minimum(i, steps - 1), 0))
    two = pl.BlockSpec((rows, D), lambda i, place: (jnp.maximum(i - steps, 0), 0))
    token_specs = [one, two][:sets]
    hidden = pl.BlockSpec((rows, FF_PART), lambda i, place: (i, 0))
    spans = tuple(
        (column, min(array.shape[1], 3 * FF_PART - column)) for array, column in pieces
    )
    return pl.pallas_call(
        functools.partial(feed_kernel, sets, spans),
        grid_spec=pltpu.PrefetchScalarGridSpec(
            num_scalar_prefetch=1,
            grid=(sets * steps,),
            in_specs=token_specs * 2 + [pl.BlockSpec(memory_space=pl.ANY)] * len(pieces),
            out_specs=token_specs * 2 + [hidden, hidden, hidden],
            scratch_shapes=[
                pltpu.VMEM((D, 3 * FF_PART), BF16),
                pltpu.SemaphoreType.DMA((len(pieces),)),
            ],
        ),
        out_shape=[jax.ShapeDtypeStruct((count, D), BF16)] * (2 * sets)
        + [jax.ShapeDtypeStruct((sets * count, FF_PART), BF16)] * 3,
        compiler_params=pltpu.CompilerParams(vmem_limit_bytes=VMEM_BYTES),
        cost_estimate=pl.CostEstimate(
            flops=20 * sets * count * D * FF_PART,
            bytes_accessed=6 * D * FF_PART + sets * count * (8 * D + 6 * FF_PART),
            transcendentals=sets * count * FF_PART,
        ),
        name="feed",
    )(places, *h_sets, *c_sets, *[array for array, _ in pieces])


def columns_kernel(team_ref, *refs):
    parts, outs = refs[:TEAM], refs[TEAM:]
    team = team_ref[0]
    for place in range(TEAM):
        bit = team ^ place
        width = min(FF_PART, FF - place * FF_PART)
        for matrix, out in enumerate(outs):
            span = slice(matrix * FF_PART, matrix * FF_PART + width)
            low = jnp.where(bit == 0, parts[0][:, span].astype(F32), parts[1][:, span].astype(F32))
            high = jnp.where(bit == 2, parts[2][:, span].astype(F32), parts[3][:, span].astype(F32))
            out[:, place * FF_PART : place * FF_PART + width] = jnp.where(bit < 2, low, high)


def columns(team_place, parts):
    rows = parts[0].shape[0]
    return pl.pallas_call(
        columns_kernel,
        grid_spec=pltpu.PrefetchScalarGridSpec(
            num_scalar_prefetch=1,
            grid=(1,),
            in_specs=[pl.BlockSpec((rows, 3 * FF_PART), lambda i, team: (0, 0))] * TEAM,
            out_specs=[pl.BlockSpec((rows, FF), lambda i, team: (0, 0))] * 3,
        ),
        out_shape=[jax.ShapeDtypeStruct((rows, FF), F32)] * 3,
        compiler_params=pltpu.CompilerParams(vmem_limit_bytes=VMEM_BYTES),
        cost_estimate=pl.CostEstimate(
            flops=rows * FF, bytes_accessed=20 * rows * FF, transcendentals=0
        ),
        name="columns",
    )(team_place.astype(jnp.int32).reshape(1), *parts)


def project_kernel(first, h_ref, w_ref, b_ref, cos_ref, sin_ref, out_ref):
    block = pl.program_id(0) + first
    flat = dot_nn(h_ref[...], w_ref[...]) + b_ref[...]
    turned = flat * cos_ref[...] + swap_halves(flat) * sin_ref[...]
    kept = jnp.where(block < (QW + KW) // LANES, turned, flat)
    scale = jnp.where(block < QW // LANES, HEAD ** (-0.5), 1.0)
    out_ref[...] = (kept * scale).astype(BF16)


def project(h, weights, bias, cosine, sine, first, count):
    rows = h.shape[0]
    table = pl.BlockSpec((rows, LANES), lambda i: (0, 0))
    return pl.pallas_call(
        functools.partial(project_kernel, first),
        grid=(count,),
        in_specs=[
            pl.BlockSpec((rows, D), lambda i: (0, 0)),
            pl.BlockSpec((D, LANES), lambda i: (0, first + i)),
            pl.BlockSpec((1, LANES), lambda i: (0, first + i)),
            table,
            table,
        ],
        out_specs=pl.BlockSpec((rows, LANES), lambda i: (0, i)),
        out_shape=jax.ShapeDtypeStruct((rows, count * LANES), BF16),
        cost_estimate=pl.CostEstimate(
            flops=2 * rows * D * count * LANES,
            bytes_accessed=2 * (D * count * LANES + rows * D),
            transcendentals=0,
        ),
        name="project",
    )(h, weights, bias, cosine, sine)


def prepare_kernel(kv_ref, k_ref, v_ref, kt_ref, vt_ref):
    low = half_mask(0, jnp.int32) > 0
    for place, twice, turned in ((0, k_ref, kt_ref), (1, v_ref, vt_ref)):
        block = kv_ref[:, place * LANES : (place + 1) * LANES].astype(F32)
        other = pltpu.roll(block, HEAD, 1)
        twice[0] = jnp.where(low, block, other).astype(BF16)
        twice[1] = jnp.where(low, other, block).astype(BF16)
        across = jnp.transpose(block).astype(BF16)
        turned[0] = across[:HEAD]
        turned[1] = across[HEAD:]


def prepare(kv_whole):
    length = kv_whole.shape[0]
    rows = 512
    twice = pl.BlockSpec((KV_HEADS, rows, LANES), lambda i: (0, i, 0))
    turned = pl.BlockSpec((KV_HEADS, HEAD, rows), lambda i: (0, 0, i))
    return pl.pallas_call(
        prepare_kernel,
        grid=(length // rows,),
        in_specs=[pl.BlockSpec((rows, 2 * KW), lambda i: (i, 0))],
        out_specs=[twice, twice, turned, turned],
        out_shape=[jax.ShapeDtypeStruct((KV_HEADS, length, LANES), BF16)] * 2
        + [jax.ShapeDtypeStruct((KV_HEADS, HEAD, length), BF16)] * 2,
        cost_estimate=pl.CostEstimate(
            flops=8 * length * LANES, bytes_accessed=16 * length * LANES, transcendentals=0
        ),
        name="prepare",
    )(kv_whole)


def ring_order(place, count):
    up = 2 * place - 1
    down = 2 * (count - place)
    if isinstance(place, int):
        return 0 if place == 0 else up if place <= count // 2 else down
    return jnp.where(place == 0, 0, jnp.where(place <= count // 2, up, down))


class Ring:
    def __init__(self, count):
        order = [ring_order(place, count) for place in range(count)]
        self.count = count
        self.half = count // 2
        self.ahead = [(order[i], order[(i + 1) % count]) for i in range(count)]
        self.back = [(b, a) for a, b in self.ahead]
        mine = lax.axis_index("shard")
        self.place = jnp.where(mine % 2 == 1, (mine + 1) // 2, (count - mine // 2) % count)

    def owner(self, offset):
        return ring_order((self.place + self.count + offset) % self.count, self.count)

    def send(self, array, ahead):
        return lax.ppermute(array, "shard", self.ahead if ahead else self.back)


def tie(flows, *others):
    count = 2 * len(flows)
    sides = [side for flow in flows for side in (flow.right, flow.left)]
    tied = lax.optimization_barrier((*sides, *others))
    for index, flow in enumerate(flows):
        flow.right, flow.left = tied[2 * index : 2 * index + 2]
    others = tied[count:]
    return others[0] if len(others) == 1 else others


class Gather:
    def __init__(self, ring, array):
        self.ring = ring
        self.rows, self.cols = array.shape
        self.cut = (self.cols // (2 * LANES)) * LANES
        self.own = self.right = self.left = array
        self.done = 0
        self.pieces = [(array, 0, 0)]

    def step(self):
        self.done += 1
        if self.done < self.ring.half:
            self.right = self.ring.send(self.right, True)
            self.left = self.ring.send(self.left, False)
            self.pieces += [(self.right, -self.done, 0), (self.left, self.done, 0)]
        else:
            self.right = self.ring.send(self.right[:, : self.cut], True)
            self.left = self.ring.send(self.left[:, self.cut :], False)
            self.pieces += [(self.right, self.done, 0), (self.left, self.done, self.cut)]

    def owners(self):
        index = jnp.arange(len(self.pieces), dtype=jnp.int32)
        offset = (index + 1) // 2
        return self.ring.owner(jnp.where(index % 2 == 1, -offset, offset))

    def result(self, first=0):
        count = self.ring.count
        cols = self.cols - first
        whole = jnp.broadcast_to(self.own[None, :, first:], (count, self.rows, cols))
        for piece, offset, column in self.pieces[1:]:
            skip = max(first - column, 0)
            if skip < piece.shape[1]:
                start = (self.ring.owner(offset), 0, column + skip - first)
                whole = lax.dynamic_update_slice(whole, piece[None, :, skip:], start)
        return whole.reshape(count * self.rows, cols)

    def run(self):
        while self.done < self.ring.half:
            self.step()
        return self.result()


class ScatterSum:
    def __init__(self, ring, arrays):
        self.ring = ring
        self.rows = arrays[0].shape[0] // ring.count
        self.cols = sum(array.shape[1] for array in arrays)
        self.arrays = [array.reshape(ring.count, self.rows, -1) for array in arrays]
        self.cut = (self.cols // (2 * LANES)) * LANES
        self.done = 0
        far = self.chunk(ring.half)
        self.right = far[:, : self.cut]
        self.left = far[:, self.cut :]

    def chunk(self, offset):
        owner = self.ring.owner(offset)
        return jnp.concatenate(
            [lax.dynamic_index_in_dim(array, owner, 0, keepdims=False) for array in self.arrays],
            axis=1,
        )

    def add(self, offset, got, first, last):
        near = self.chunk(offset)
        part = (near[:, first:last].astype(F32) + got.astype(F32)).astype(BF16)
        return jnp.concatenate([near[:, :first], part, near[:, last:]], axis=1)

    def step(self):
        if self.done:
            offset = self.ring.half - self.done
            part = (0, self.cut, self.cols) if self.done == 1 else (0, self.cols, 0)
            self.right = self.add(offset, self.right, 0, part[1])
            self.left = self.add(-offset, self.left, part[1] if self.done == 1 else 0, self.cols)
        self.right = self.ring.send(self.right, True)
        self.left = self.ring.send(self.left, False)
        self.done += 1

    def result(self):
        return self.chunk(0).astype(F32) + self.right.astype(F32) + self.left.astype(F32)


def spread_sum(array):
    count = lax.axis_size("shard")
    arrived = lax.all_to_all(array, "shard", 0, 0, tiled=True)
    blocks = arrived.reshape(count, array.shape[0] // count, array.shape[1])
    return jnp.sum(blocks.astype(F32), axis=0)


def team_send(array, bit):
    return lax.ppermute(array, "rep", [(i, i ^ bit) for i in range(lax.axis_size("rep"))])


def team_sum(mine, core, cross, both):
    gathered = (cross.astype(F32) + team_send(both, 1).astype(F32)).astype(BF16)
    return (
        mine.astype(F32)
        + team_send(core, 1).astype(F32)
        + team_send(gathered, 2).astype(F32)
    )


def rope_tables(positions):
    half_width = HEAD // 2
    inverse = jnp.exp(
        jnp.arange(half_width, dtype=F32) * (-2.0 * math.log(ROPE_BASE) / HEAD)
    )
    angles = positions.astype(F32)[:, None] * inverse[None, :]
    cosine = jnp.cos(angles)
    sine = jnp.sin(angles)
    return (
        jnp.concatenate([cosine] * 4, axis=1),
        jnp.concatenate([-sine, sine, -sine, sine], axis=1),
    )


def rotate(source, cosine, sine):
    times = source.shape[1] // LANES
    return source * jnp.tile(cosine, (1, times)) + swap_halves(source) * jnp.tile(sine, (1, times))


def rotate_back(source, cosine, sine):
    times = source.shape[1] // LANES
    return source * jnp.tile(cosine, (1, times)) + swap_halves(source * jnp.tile(sine, (1, times)))


def norm_back(grad_normed, normed, inv_scale, gain_row):
    scaled = grad_normed * gain_row
    return inv_scale * (scaled - normed * jnp.mean(scaled * normed, axis=1, keepdims=True))


def body(
    hidden_in,
    cotangent,
    norm_gains,
    q_bias,
    kv_bias,
    q_weight,
    kv_weight,
    out_weight,
    gate_weight,
    up_weight,
    down_weight,
):
    tok_rows = hidden_in.shape[1]
    shard_count = lax.axis_size("shard")
    rep_count = lax.axis_size("rep")
    shard_place = lax.axis_index("shard")
    rep_place = lax.axis_index("rep")
    team_place = rep_place % TEAM
    row_share = D // shard_count
    kv_share = 2 * KW // shard_count
    ring = Ring(shard_count)
    core_place = rep_place % 2
    qkv_width = QW + 2 * KW
    teams = rep_count // TEAM
    across = [[t * TEAM + i for t in range(teams)] for i in range(TEAM)]

    small = jnp.concatenate([norm_gains[0], norm_gains[1], q_bias, kv_bias])
    spare = jnp.pad(small[None, :], ((0, 15), (0, qkv_width - small.shape[0])))
    qkv_piece = jnp.concatenate([jnp.concatenate([q_weight, kv_weight], axis=1), spare], axis=0)
    half_rows = (row_share + 16) // 2
    qkv_half = lax.dynamic_slice_in_dim(qkv_piece, core_place * half_rows, half_rows, 0)
    grad_out = cotangent[0]
    qkv_flow = Gather(ring, qkv_half)
    qkv_flow.step()
    c_cross = team_send(grad_out, 2)
    gate_weight, up_weight, down_weight, out_weight = tie(
        [qkv_flow], gate_weight, up_weight, down_weight, out_weight
    )

    def quarter(weight):
        padded = jnp.pad(weight, ((0, 0), (0, TEAM * FF_PART - FF)))
        return lax.dynamic_slice_in_dim(padded, team_place * FF_PART, FF_PART, 1)

    feed_piece = jnp.concatenate(
        [quarter(gate_weight), quarter(up_weight), quarter(down_weight), out_weight], axis=1
    )
    for _ in range(ring.half - 1):
        qkv_flow.step()
    feed_piece = tie([qkv_flow], feed_piece)
    mine = qkv_flow.result()
    other = team_send(mine, 1)
    halves = (jnp.where(core_place == 0, mine, other), jnp.where(core_place == 0, other, mine))
    qkv_all = jnp.concatenate(
        [half.reshape(shard_count, half_rows, qkv_width) for half in halves], axis=1
    )
    qkv_full = qkv_all[:, :row_share].reshape(D, qkv_width)
    smalls = qkv_all[:, row_share].astype(F32)
    gain_one = smalls[:, :row_share].reshape(D)
    gain_two = smalls[:, row_share : 2 * row_share].reshape(D)
    q_bias_all = smalls[:, 2 * row_share : 3 * row_share].reshape(QW)
    kv_bias_all = smalls[:, 3 * row_share : 3 * row_share + kv_share].reshape(2 * KW)
    bias = jnp.concatenate([q_bias_all, kv_bias_all])[None, :]
    q_full = qkv_full[:, :QW]
    kv_full = qkv_full[:, QW:]

    inputs = hidden_in[0].astype(F32)
    inv_one = lax.rsqrt(jnp.mean(inputs * inputs, axis=1, keepdims=True) + EPS)
    normed_one = inputs * inv_one
    h_one = (normed_one * gain_one).astype(BF16)
    positions = shard_place * tok_rows + jnp.arange(tok_rows, dtype=jnp.int32)
    cosine, sine = rope_tables(positions)
    kv_local = project(h_one, qkv_full, bias, cosine, sine, QW // LANES, 2 * KW // LANES)

    feeding = Gather(ring, feed_piece)
    flows = [feeding]
    feeding.step()
    kv_flow = Gather(ring, kv_local)
    kv_flow.step()
    late_out, c_cross = tie([kv_flow], grad_out, c_cross)
    c_both = team_send(late_out, 3)
    kv_whole = kv_flow.run()
    q_scaled = project(h_one, qkv_full, bias, cosine, sine, 0, QW // LANES)
    me = shard_place.astype(jnp.int32).reshape(1)
    kv_whole, late_out = tie(flows, kv_whole, late_out)
    c_core = team_send(late_out, 1)
    feeding.step()
    k_twice, v_twice, k_turned, v_turned = prepare(kv_whole)
    attn_one, lse_one = attn_forward(me, q_scaled, k_twice, v_turned, 0, 3)
    attn_one, q_scaled, c_core, c_both = tie(flows, attn_one, q_scaled, c_core, c_both)
    feeding.step()
    attn_two, lse_two = attn_forward(me, q_scaled, k_twice, v_turned, 3, 3)
    attn_two, q_scaled = tie(flows, attn_two, q_scaled)
    feeding.step()
    attn_three, lse_three = attn_forward(me, q_scaled, k_twice, v_turned, 6, 1)
    attn_three = tie(flows, attn_three)
    attn_b = jnp.concatenate([attn_one, attn_two, attn_three], axis=1)
    lse = jnp.concatenate([lse_one, lse_two, lse_three], axis=0)
    out_full = feeding.result(3 * FF_PART)

    middle = inputs + dot_nt(attn_b, out_full)
    inv_two = lax.rsqrt(jnp.mean(middle * middle, axis=1, keepdims=True) + EPS)
    normed_two = middle * inv_two
    h_two = (normed_two * gain_two).astype(BF16)
    if row_share % 16:
        feed_pieces = [(feeding.result(), 0)]
        feed_places = jnp.zeros((1,), jnp.int32)
    else:
        feed_pieces = [(piece, column) for piece, _, column in feeding.pieces]
        feed_places = feeding.owners()

    h_core = team_send(h_two, 1)
    h_cross = team_send(h_two, 2)
    here = feed((h_two, h_core), (grad_out, c_core), feed_pieces, feed_places)
    h_cross, *here = lax.optimization_barrier((h_cross, *here))
    h_both = team_send(h_cross, 1)
    cross = feed((h_cross,), (c_cross,), feed_pieces, feed_places)
    h_both, *cross = lax.optimization_barrier((h_both, *cross))
    both = feed((h_both,), (c_both,), feed_pieces, feed_places)
    out_parts = (here[0], here[1], cross[0], both[0])
    dh_mine, dh_core, dh_cross, dh_both = here[2], here[3], cross[1], both[1]

    dh_home = team_send(dh_core, 1)
    dh_away = (dh_cross.astype(F32) + team_send(dh_both, 1).astype(F32)).astype(BF16)
    dh_away, *hidden = lax.optimization_barrier((dh_away, *both[2:]))
    dh_back = team_send(dh_away, 2)
    h_sets = jnp.concatenate([h_two, h_core, h_cross, h_both], axis=0)
    c_sets = jnp.concatenate([grad_out, c_core, c_cross, c_both], axis=0)
    hid_sets, dg_sets, du_sets = (
        jnp.concatenate(parts, axis=0) for parts in zip(here[4:], cross[2:], hidden)
    )
    gate_grads = dot_tn(h_sets, dg_sets).astype(BF16)
    up_grads = dot_tn(h_sets, du_sets).astype(BF16)
    down_grads = dot_tn(c_sets, hid_sets).astype(BF16)
    dh_back, gate_grads, up_grads, down_grads = lax.optimization_barrier(
        (dh_back, gate_grads, up_grads, down_grads)
    )
    grad_h_two = dh_mine.astype(F32) + dh_home.astype(F32) + dh_back.astype(F32)

    gain_two_grad = jnp.sum(grad_h_two * normed_two, axis=0)
    grad_middle = grad_out.astype(F32) + norm_back(grad_h_two, normed_two, inv_two, gain_two)
    grad_branch_b = grad_middle.astype(BF16)
    grad_attn = dot_nn(grad_branch_b, out_full).astype(BF16)
    out_grads = dot_tn(grad_branch_b, attn_b).astype(BF16)
    row_sum = ScatterSum(ring, [gate_grads, up_grads, down_grads, out_grads])
    row_sum.step()

    tables = (cosine, sine)

    def backward(first, pairs, raw):
        tensors = (q_scaled, k_twice, k_turned, v_twice, attn_b, grad_attn, lse)
        return attn_backward(me, tensors, tables, first, pairs, raw)

    flows = [row_sum]
    grad_attn = tie(flows, grad_attn)
    row_sum.step()
    dq_one, _, raw = backward(0, 2, None)
    dq_one, raw, grad_attn = tie(flows, dq_one, raw, grad_attn)
    row_sum.step()
    dq_two, dkv_zero, raw = backward(2, 2, raw)
    dkv_zero, raw, grad_attn = tie(flows, dkv_zero, raw, grad_attn)
    row_sum.step()
    zero_sum = spread_sum(dkv_zero)
    dq_three, dkv_one, _ = backward(4, 3, raw)
    dq_three, dkv_one, zero_sum, *out_parts = tie(flows, dq_three, dkv_one, zero_sum, *out_parts)
    one_sum = spread_sum(dkv_one)
    mine, dq_three = lax.optimization_barrier((row_sum.result().astype(BF16), dq_three))
    cross = team_send(mine, 2)
    core = team_send(mine, 1)
    output = middle + team_sum(*out_parts)
    grad_q_b = jnp.concatenate([dq_one, dq_two, dq_three], axis=1)

    def team_total(rows):
        core, cross, both = (team_send(rows, bit).astype(F32) for bit in (1, 2, 3))
        rows = (rows.astype(F32) + core) + (cross + both)
        if teams > 1:
            rows = lax.psum(rows.astype(BF16), "rep", axis_index_groups=across).astype(F32)
        return rows

    q_bias_sum = jnp.sum(grad_q_b.astype(F32), axis=0)
    grad_h_q = dot_nt(grad_q_b, q_full)
    q_grads = dot_tn(h_one, grad_q_b).astype(BF16)
    q_grads = q_grads.reshape(shard_count, 2, 2, row_share // TEAM, QW)
    one_sum, q_grads = lax.optimization_barrier((one_sum, q_grads))

    def halve(array, axis, place, bit):
        keep = lax.dynamic_index_in_dim(array, place, axis, keepdims=False)
        give = lax.dynamic_index_in_dim(array, 1 - place, axis, keepdims=False)
        return (keep.astype(F32) + team_send(give, bit).astype(F32)).astype(BF16)

    q_grads = halve(halve(q_grads, 2, core_place, 1), 1, team_place // 2, 2)

    grad_k = jnp.concatenate([zero_sum[:, :HEAD], one_sum[:, :HEAD]], axis=1)
    grad_v = jnp.concatenate([zero_sum[:, HEAD:], one_sum[:, HEAD:]], axis=1)
    grad_kv_b = jnp.concatenate([rotate_back(grad_k, cosine, sine), grad_v], axis=1).astype(BF16)
    kv_bias_sum = jnp.sum(grad_kv_b.astype(F32), axis=0)
    grad_h_one = grad_h_q + dot_nt(grad_kv_b, kv_full)
    gain_one_grad = jnp.sum(grad_h_one * normed_one, axis=0)
    input_grad = (grad_middle + norm_back(grad_h_one, normed_one, inv_one, gain_one)).astype(BF16)

    width = 2 * KW
    late_weight = dot_tn(h_one, grad_kv_b).reshape(shard_count, row_share, width)
    smalls = jnp.concatenate(
        [
            one.reshape(shard_count, -1)
            for one in (gain_one_grad, gain_two_grad, q_bias_sum, kv_bias_sum)
        ],
        axis=1,
    )
    smalls = jnp.pad(smalls, ((0, 0), (0, 16 * width - smalls.shape[1])))
    last_sum = jnp.concatenate([late_weight, smalls.reshape(shard_count, 16, width)], axis=1)
    last_sum, cross, q_grads = lax.optimization_barrier(
        (last_sum.reshape(-1, width).astype(BF16), cross, q_grads)
    )
    both = team_send(cross, 1)
    last_sum = spread_sum(last_sum)
    q_part = spread_sum(q_grads.reshape(-1, QW))
    last_rows = team_total(last_sum.astype(BF16))
    kv_rows = last_rows[:row_share]
    smalls = last_rows[row_share:].reshape(-1)
    gains_grad = smalls[: 2 * row_share].reshape(2, row_share)
    q_bias_grad = smalls[2 * row_share : 3 * row_share]
    kv_bias_grad = smalls[3 * row_share : 3 * row_share + kv_share]

    if teams > 1:
        q_part = lax.psum(q_part.astype(BF16), "rep", axis_index_groups=across)
    q_part = q_part.astype(BF16)
    q_parts = [q_part] + [team_send(q_part, bit) for bit in (1, 2, 3)]

    def quarter_at(place):
        bit = team_place ^ place
        low = jnp.where(bit == 0, q_parts[0], q_parts[1])
        return jnp.where(bit < 2, low, jnp.where(bit == 2, q_parts[2], q_parts[3]))

    q_rows = jnp.concatenate([quarter_at(place) for place in range(TEAM)], axis=0).astype(F32)
    parts = [mine, core, cross, both]
    if teams > 1:
        parts = [lax.psum(part, "rep", axis_index_groups=across) for part in parts]
    outs = [part[:, 3 * FF_PART :].astype(F32) for part in parts]
    out_rows = (outs[0] + outs[1]) + (outs[2] + outs[3])
    gate_grad, up_grad, down_grad = columns(team_place, parts)
    return (
        output.astype(BF16)[None],
        input_grad[None],
        gains_grad,
        q_bias_grad,
        kv_bias_grad,
        q_rows,
        kv_rows,
        out_rows,
        gate_grad,
        up_grad,
        down_grad,
    )


def solution(mesh):
    tokens = P("rep", "shard", None)
    rows = P("shard", None)
    placed = (tokens, tokens, P(None, "shard"), P("shard"), P("shard")) + (rows,) * 6
    return jax.shard_map(body, mesh=mesh, in_specs=placed, out_specs=placed, check_vma=False)
```

```python
import functools
import math

import jax
import jax.numpy as jnp
from jax import lax
from jax.experimental import pallas as pl
from jax.experimental.pallas import tpu as pltpu
from jax.sharding import PartitionSpec as P

D = 896
HEADS = 14
KV_HEADS = 2
HEAD = 64
FF = 4864
QW = 896
KW = 128
LANES = 128
TEAM = 4
FF_PART = 1280
FF_TILE = 256
UNIT = 1024

EPS = 1e-06
ROPE_BASE = 1000000.0
F32 = jnp.float32
BF16 = jnp.bfloat16
VMEM_BYTES = 56 * 1024 * 1024


def dot_nt(left, right):
    return lax.dot_general(left, right, (((1,), (1,)), ((), ())), preferred_element_type=F32)


def dot_tn(left, right):
    return lax.dot_general(left, right, (((0,), (0,)), ((), ())), preferred_element_type=F32)


def dot_nn(left, right):
    return jnp.dot(left, right, preferred_element_type=F32)


def half_mask(parity, kind):
    lane = lax.broadcasted_iota(jnp.int32, (1, LANES), 1)
    return ((lane // HEAD) == parity).astype(kind)


def swap_halves(source):
    lane = lax.broadcasted_iota(jnp.int32, source.shape, 1)
    ahead = jnp.roll(source, -(HEAD // 2), axis=1)
    behind = jnp.roll(source, HEAD // 2, axis=1)
    return jnp.where(lane % HEAD < HEAD // 2, ahead, behind)


def seen(me, rows, unit):
    base = (me * rows // UNIT) * UNIT
    key = lax.broadcasted_iota(jnp.int32, (UNIT, rows), 0) + base
    query = lax.broadcasted_iota(jnp.int32, (UNIT, rows), 1) + me * rows
    return key <= query


def attn_forward_kernel(me_ref, q_ref, k_ref, vt_ref, o_ref, lse_ref):
    pair = pl.program_id(0) + me_ref[1]
    me = me_ref[0]
    rows = q_ref.shape[0]
    group = HEADS // KV_HEADS
    last = me * rows // UNIT
    allowed = seen(me, rows, last)
    heads = [((2 * pair + parity) // group, q_ref[...] * half_mask(parity, BF16)) for parity in range(2)]

    def span(unit):
        return pl.ds(unit * UNIT, UNIT)

    def scores(head, unit):
        return dot_nt(k_ref[head[0], span(unit), :], head[1])

    def weigh(head, unit, probs):
        return dot_nn(vt_ref[head[0], :, span(unit)], probs.astype(BF16))

    tops, probs = [], []
    for head in heads:
        s = jnp.where(allowed, scores(head, last), -1e30)
        tops.append(jnp.max(s, axis=0, keepdims=True))
        probs.append(jnp.exp(s - tops[-1]))
    start = tuple(
        (jnp.sum(p, axis=0, keepdims=True), weigh(head, last, p)) for head, p in zip(heads, probs)
    )

    def quick(unit, state):
        probs = [jnp.exp(scores(head, unit) - top) for head, top in zip(heads, tops)]
        return tuple(
            (total + jnp.sum(p, axis=0, keepdims=True), acc + weigh(head, unit, p))
            for head, (total, acc), p in zip(heads, state, probs)
        )

    def careful(unit, state):
        after = []
        for head, (top, total, acc) in zip(heads, state):
            s = scores(head, unit)
            new_top = jnp.maximum(top, jnp.max(s, axis=0, keepdims=True))
            shrink = jnp.exp(top - new_top)
            p = jnp.exp(s - new_top)
            total = total * shrink + jnp.sum(p, axis=0, keepdims=True)
            after.append((new_top, total, acc * shrink + weigh(head, unit, p)))
        return tuple(after)

    def store(state):
        for parity, (top, total, acc) in enumerate(state):
            lse_ref[0, parity : parity + 1, :] = top + jnp.log(total)
        both = jnp.concatenate([acc / total for top, total, acc in state], axis=0)
        o_ref[...] = jnp.transpose(both).astype(BF16)

    state = lax.fori_loop(0, last, quick, start)
    largest = jnp.max(jnp.maximum(state[0][0], state[1][0]))
    fine = largest < 1e30

    @pl.when(fine)
    def _():
        store([(top, total, acc) for top, (total, acc) in zip(tops, state)])

    @pl.when(jnp.logical_not(fine))
    def _():
        begin = tuple((top, total, acc) for top, (total, acc) in zip(tops, start))
        store(lax.fori_loop(0, last, careful, begin))


def attn_forward(me, q, k_twice, v_turned, first, pairs):
    rows = q.shape[0]
    length = k_twice.shape[1]
    blocks = length // rows
    scalars = jnp.concatenate([me, jnp.full((1,), first, jnp.int32)])
    return pl.pallas_call(
        attn_forward_kernel,
        grid_spec=pltpu.PrefetchScalarGridSpec(
            num_scalar_prefetch=1,
            grid=(pairs,),
            in_specs=[
                pl.BlockSpec((rows, LANES), lambda i, me: (0, first + i)),
                pl.BlockSpec((KV_HEADS, length, LANES), lambda i, me: (0, 0, 0)),
                pl.BlockSpec((KV_HEADS, HEAD, length), lambda i, me: (0, 0, 0)),
            ],
            out_specs=[
                pl.BlockSpec((rows, LANES), lambda i, me: (0, i)),
                pl.BlockSpec((1, 2, rows), lambda i, me: (i, 0, 0)),
            ],
        ),
        out_shape=[
            jax.ShapeDtypeStruct((rows, pairs * LANES), BF16),
            jax.ShapeDtypeStruct((pairs, 2, rows), F32),
        ],
        compiler_params=pltpu.CompilerParams(vmem_limit_bytes=VMEM_BYTES),
        cost_estimate=pl.CostEstimate(
            flops=32 * blocks * pairs * rows * rows * HEAD,
            bytes_accessed=4 * rows * pairs * LANES + 6 * length * LANES,
            transcendentals=blocks * 2 * pairs * rows * rows,
        ),
        name="attn_forward",
    )(scalars, q, k_twice, v_turned)


def attn_backward_kernel(spec, *refs):
    first, pairs, start, finish, carry_in, carry_out = spec
    refs = list(refs)
    me_ref, q_ref, k_ref, kt_ref, v_ref, o_ref, do_ref, lse_ref, cos_ref, sin_ref = refs[:10]
    at = 10
    if carry_in:
        raw_in = refs[at]
        at += 1
    dq_ref = refs[at]
    at += 1
    if finish is not None:
        folded = refs[at]
        at += 1
    if carry_out:
        raw_out = refs[at]
        at += 1
    acc, moved = refs[at:]
    step_index = pl.program_id(0)
    pair = step_index + first
    me = me_ref[0]
    rows = q_ref.shape[0]
    group = HEADS // KV_HEADS
    held = acc.shape[0]
    last = me * rows // UNIT
    allowed = seen(me, rows, last)

    @pl.when(step_index == 0)
    def _():
        if carry_in:
            pltpu.make_async_copy(raw_in, acc.at[0], moved.at[0]).start()
        else:
            acc[0] = jnp.zeros(acc.shape[1:], F32)
        for more in range(1, held):
            acc[more] = jnp.zeros(acc.shape[1:], F32)
        if carry_in:
            pltpu.make_async_copy(raw_in, acc.at[0], moved.at[0]).wait()

    products = do_ref[...].astype(F32) * o_ref[...].astype(F32)
    heads = []
    for parity in range(2):
        kv_head = (2 * pair + parity) // group
        mask = half_mask(parity, BF16)
        picks = jnp.broadcast_to(half_mask(parity, F32), (8, LANES))
        delta = lax.dot_general(
            picks,
            products,
            (((1,), (1,)), ((), ())),
            precision=lax.Precision.HIGHEST,
            preferred_element_type=F32,
        )[0:1, :]
        lse = lse_ref[0, parity : parity + 1, :]
        heads.append((kv_head, q_ref[...] * mask, do_ref[...] * mask, lse, delta))

    def unit_step(unit, dqs, masked):
        span = pl.ds(unit * UNIT, UNIT)
        probs, d_scores = [], []
        for kv_head, q_head, do_head, lse, delta in heads:
            p = jnp.exp(dot_nt(k_ref[kv_head, span, :], q_head) - lse)
            if masked:
                p = jnp.where(allowed, p, 0.0)
            d_p = dot_nt(v_ref[kv_head, span, :], do_head)
            probs.append(p.astype(BF16))
            d_scores.append((p * (d_p - delta)).astype(BF16))
        after = []
        for (kv_head, q_head, do_head, _, _), p, d_s, dq in zip(heads, probs, d_scores, dqs):
            place = kv_head - start
            acc[place, 1, span, :] += dot_nn(p, do_head)
            acc[place, 0, span, :] += dot_nn(d_s, q_head)
            after.append(dq + dot_nn(kt_ref[kv_head, :, span], d_s))
        return tuple(after)

    zero = jnp.zeros((HEAD, rows), F32)
    dqs = unit_step(last, (zero, zero), True)
    dqs = lax.fori_loop(0, last, lambda unit, dqs: unit_step(unit, dqs, False), dqs)
    dq = jnp.transpose(jnp.concatenate(dqs, axis=0)) * HEAD ** (-0.5)
    dq_ref[...] = (dq * cos_ref[...] + swap_halves(dq * sin_ref[...])).astype(BF16)

    @pl.when(step_index == pairs - 1)
    def _():
        if carry_out:
            leave = pltpu.make_async_copy(acc.at[held - 1], raw_out, moved.at[1])
            leave.start()
        if finish is not None:
            low = half_mask(0, jnp.int32) > 0

            def fold(block, carry):
                span = pl.ds(block * rows, rows)
                keys = acc[0, 0, span, :]
                values = acc[0, 1, span, :]
                keys = keys + pltpu.roll(keys, HEAD, 1)
                values = values + pltpu.roll(values, HEAD, 1)
                folded[span, :] = jnp.where(low, keys, values).astype(BF16)
                return carry

            lax.fori_loop(0, acc.shape[2] // rows, fold, 0)
        if carry_out:
            leave.wait()


def attn_backward(me, tensors, tables, first, pairs, raw=None):
    q, k_twice, k_turned, v_twice, o, d_o, lse = tensors
    rows = q.shape[0]
    length = k_twice.shape[1]
    blocks = length // rows
    group = HEADS // KV_HEADS
    start = 2 * first // group
    end = (2 * (first + pairs) - 1) // group
    finish = start if 2 * (first + pairs) >= group * (start + 1) else None
    carry_out = finish is None or end > start
    spec = (first, pairs, start, finish, raw is not None, carry_out)
    once = {"pipeline_mode": pl.Buffered(1)}
    whole = pl.BlockSpec((KV_HEADS, length, LANES), lambda i, me: (0, 0, 0), **once)
    turned = pl.BlockSpec((KV_HEADS, HEAD, length), lambda i, me: (0, 0, 0), **once)
    pair = pl.BlockSpec((rows, LANES), lambda i, me: (0, first + i))
    table = pl.BlockSpec((rows, LANES), lambda i, me: (0, 0))
    raw_shape = jax.ShapeDtypeStruct((2, length, LANES), F32)
    raw_spec = pl.BlockSpec(memory_space=pl.ANY)
    in_specs = [
        pair,
        whole,
        turned,
        whole,
        pair,
        pair,
        pl.BlockSpec((1, 2, rows), lambda i, me: (first + i, 0, 0)),
        table,
        table,
    ]
    operands = [q, k_twice, k_turned, v_twice, o, d_o, lse, *tables]
    if raw is not None:
        in_specs.append(raw_spec)
        operands.append(raw)
    out_specs = [pl.BlockSpec((rows, LANES), lambda i, me: (0, i))]
    out_shape = [jax.ShapeDtypeStruct((rows, pairs * LANES), BF16)]
    if finish is not None:
        out_specs.append(pl.BlockSpec((length, LANES), lambda i, me: (0, 0)))
        out_shape.append(jax.ShapeDtypeStruct((length, LANES), BF16))
    if carry_out:
        out_specs.append(raw_spec)
        out_shape.append(raw_shape)
    outs = pl.pallas_call(
        functools.partial(attn_backward_kernel, spec),
        grid_spec=pltpu.PrefetchScalarGridSpec(
            num_scalar_prefetch=1,
            grid=(pairs,),
            in_specs=in_specs,
            out_specs=out_specs,
            scratch_shapes=[
                pltpu.VMEM((end - start + 1, 2, length, LANES), F32),
                pltpu.SemaphoreType.DMA((2,)),
            ],
        ),
        out_shape=out_shape,
        compiler_params=pltpu.CompilerParams(vmem_limit_bytes=VMEM_BYTES),
        cost_estimate=pl.CostEstimate(
            flops=80 * blocks * pairs * rows * rows * HEAD,
            bytes_accessed=8 * rows * pairs * LANES + 16 * length * LANES,
            transcendentals=blocks * 2 * pairs * rows * rows,
        ),
        name="attn_backward",
    )(me, *operands)
    dq = outs[0]
    folded = outs[1] if finish is not None else None
    return dq, folded, outs[-1] if carry_out else None


def feed_kernel(sets, spans, place_ref, *refs):
    h_refs, c_refs, refs = refs[:sets], refs[sets : 2 * sets], refs[2 * sets :]
    pieces, refs = refs[: len(spans)], refs[len(spans) :]
    out_refs, dh_refs, refs = refs[:sets], refs[sets : 2 * sets], refs[2 * sets :]
    hid_ref, dg_ref, du_ref, w_ref, arrived = refs
    tiles = FF_PART // FF_TILE
    step = pl.program_id(0)
    former = step < pl.num_programs(0) // sets

    def fetch(index):
        piece, (column, width) = pieces[index], spans[index]
        rows = piece.shape[0]
        start = pl.multiple_of(place_ref[index] * rows, 16)
        source = piece.at[:, pl.ds(0, width)]
        target = w_ref.at[pl.ds(start, rows), pl.ds(column, width)]
        return pltpu.make_async_copy(source, target, arrived.at[index])

    @pl.when(step == 0)
    def _():
        for index in range(len(spans)):
            fetch(index).start()
        for index in range(len(spans)):
            fetch(index).wait()

    if sets == 1:
        h, c = h_refs[0][...], c_refs[0][...]
    else:
        h = jnp.where(former, h_refs[0][...], h_refs[1][...])
        c = jnp.where(former, c_refs[0][...], c_refs[1][...])
    for t in range(tiles):

        def weights(m):
            start = m * FF_PART + t * FF_TILE
            return w_ref[:, start : start + FF_TILE]

        gate = dot_nn(h, weights(0))
        up = dot_nn(h, weights(1))
        d_hid = dot_nn(c, weights(2))
        sig = jax.nn.sigmoid(gate)
        silu = gate * sig
        span = slice(t * FF_TILE, (t + 1) * FF_TILE)
        hid_ref[:, span] = (silu * up).astype(BF16)
        dg_ref[:, span] = (d_hid * up * sig * (1.0 + gate * (1.0 - sig))).astype(BF16)
        du_ref[:, span] = (d_hid * silu).astype(BF16)
    gates = w_ref[:, :FF_PART]
    ups = w_ref[:, FF_PART : 2 * FF_PART]
    downs = w_ref[:, 2 * FF_PART :]
    d_h = (dot_nt(dg_ref[...], gates) + dot_nt(du_ref[...], ups)).astype(BF16)
    out = dot_nt(hid_ref[...], downs).astype(BF16)

    @pl.when(former)
    def _():
        dh_refs[0][...] = d_h
        out_refs[0][...] = out

    @pl.when(jnp.logical_not(former))
    def _():
        dh_refs[-1][...] = d_h
        out_refs[-1][...] = out


def feed(h_sets, c_sets, pieces, places):
    sets = len(h_sets)
    count = h_sets[0].shape[0]
    rows = 256
    steps = count // rows
    one = pl.BlockSpec((rows, D), lambda i, place: (jnp.minimum(i, steps - 1), 0))
    two = pl.BlockSpec((rows, D), lambda i, place: (jnp.maximum(i - steps, 0), 0))
    token_specs = [one, two][:sets]
    hidden = pl.BlockSpec((rows, FF_PART), lambda i, place: (i, 0))
    spans = tuple(
        (column, min(array.shape[1], 3 * FF_PART - column)) for array, column in pieces
    )
    return pl.pallas_call(
        functools.partial(feed_kernel, sets, spans),
        grid_spec=pltpu.PrefetchScalarGridSpec(
            num_scalar_prefetch=1,
            grid=(sets * steps,),
            in_specs=token_specs * 2 + [pl.BlockSpec(memory_space=pl.ANY)] * len(pieces),
            out_specs=token_specs * 2 + [hidden, hidden, hidden],
            scratch_shapes=[
                pltpu.VMEM((D, 3 * FF_PART), BF16),
                pltpu.SemaphoreType.DMA((len(pieces),)),
            ],
        ),
        out_shape=[jax.ShapeDtypeStruct((count, D), BF16)] * (2 * sets)
        + [jax.ShapeDtypeStruct((sets * count, FF_PART), BF16)] * 3,
        compiler_params=pltpu.CompilerParams(vmem_limit_bytes=VMEM_BYTES),
        cost_estimate=pl.CostEstimate(
            flops=20 * sets * count * D * FF_PART,
            bytes_accessed=6 * D * FF_PART + sets * count * (8 * D + 6 * FF_PART),
            transcendentals=sets * count * FF_PART,
        ),
        name="feed",
    )(places, *h_sets, *c_sets, *[array for array, _ in pieces])


def columns_kernel(team_ref, *refs):
    parts, outs = refs[:TEAM], refs[TEAM:]
    team = team_ref[0]
    for place in range(TEAM):
        bit = team ^ place
        width = min(FF_PART, FF - place * FF_PART)
        for matrix, out in enumerate(outs):
            span = slice(matrix * FF_PART, matrix * FF_PART + width)
            low = jnp.where(bit == 0, parts[0][:, span].astype(F32), parts[1][:, span].astype(F32))
            high = jnp.where(bit == 2, parts[2][:, span].astype(F32), parts[3][:, span].astype(F32))
            out[:, place * FF_PART : place * FF_PART + width] = jnp.where(bit < 2, low, high)


def columns(team_place, parts):
    rows = parts[0].shape[0]
    return pl.pallas_call(
        columns_kernel,
        grid_spec=pltpu.PrefetchScalarGridSpec(
            num_scalar_prefetch=1,
            grid=(1,),
            in_specs=[pl.BlockSpec((rows, 3 * FF_PART), lambda i, team: (0, 0))] * TEAM,
            out_specs=[pl.BlockSpec((rows, FF), lambda i, team: (0, 0))] * 3,
        ),
        out_shape=[jax.ShapeDtypeStruct((rows, FF), F32)] * 3,
        compiler_params=pltpu.CompilerParams(vmem_limit_bytes=VMEM_BYTES),
        cost_estimate=pl.CostEstimate(
            flops=rows * FF, bytes_accessed=20 * rows * FF, transcendentals=0
        ),
        name="columns",
    )(team_place.astype(jnp.int32).reshape(1), *parts)


def project_kernel(first, h_ref, w_ref, b_ref, cos_ref, sin_ref, out_ref):
    block = pl.program_id(0) + first
    flat = dot_nn(h_ref[...], w_ref[...]) + b_ref[...]
    turned = flat * cos_ref[...] + swap_halves(flat) * sin_ref[...]
    kept = jnp.where(block < (QW + KW) // LANES, turned, flat)
    scale = jnp.where(block < QW // LANES, HEAD ** (-0.5), 1.0)
    out_ref[...] = (kept * scale).astype(BF16)


def project(h, weights, bias, cosine, sine, first, count):
    rows = h.shape[0]
    table = pl.BlockSpec((rows, LANES), lambda i: (0, 0))
    return pl.pallas_call(
        functools.partial(project_kernel, first),
        grid=(count,),
        in_specs=[
            pl.BlockSpec((rows, D), lambda i: (0, 0)),
            pl.BlockSpec((D, LANES), lambda i: (0, first + i)),
            pl.BlockSpec((1, LANES), lambda i: (0, first + i)),
            table,
            table,
        ],
        out_specs=pl.BlockSpec((rows, LANES), lambda i: (0, i)),
        out_shape=jax.ShapeDtypeStruct((rows, count * LANES), BF16),
        cost_estimate=pl.CostEstimate(
            flops=2 * rows * D * count * LANES,
            bytes_accessed=2 * (D * count * LANES + rows * D),
            transcendentals=0,
        ),
        name="project",
    )(h, weights, bias, cosine, sine)


def prepare_kernel(kv_ref, k_ref, v_ref, kt_ref, vt_ref):
    low = half_mask(0, jnp.int32) > 0
    for place, twice, turned in ((0, k_ref, kt_ref), (1, v_ref, vt_ref)):
        block = kv_ref[:, place * LANES : (place + 1) * LANES].astype(F32)
        other = pltpu.roll(block, HEAD, 1)
        twice[0] = jnp.where(low, block, other).astype(BF16)
        twice[1] = jnp.where(low, other, block).astype(BF16)
        across = jnp.transpose(block).astype(BF16)
        turned[0] = across[:HEAD]
        turned[1] = across[HEAD:]


def prepare(kv_whole):
    length = kv_whole.shape[0]
    rows = 512
    twice = pl.BlockSpec((KV_HEADS, rows, LANES), lambda i: (0, i, 0))
    turned = pl.BlockSpec((KV_HEADS, HEAD, rows), lambda i: (0, 0, i))
    return pl.pallas_call(
        prepare_kernel,
        grid=(length // rows,),
        in_specs=[pl.BlockSpec((rows, 2 * KW), lambda i: (i, 0))],
        out_specs=[twice, twice, turned, turned],
        out_shape=[jax.ShapeDtypeStruct((KV_HEADS, length, LANES), BF16)] * 2
        + [jax.ShapeDtypeStruct((KV_HEADS, HEAD, length), BF16)] * 2,
        cost_estimate=pl.CostEstimate(
            flops=8 * length * LANES, bytes_accessed=16 * length * LANES, transcendentals=0
        ),
        name="prepare",
    )(kv_whole)


def ring_order(place, count):
    up = 2 * place - 1
    down = 2 * (count - place)
    if isinstance(place, int):
        return 0 if place == 0 else up if place <= count // 2 else down
    return jnp.where(place == 0, 0, jnp.where(place <= count // 2, up, down))


class Ring:
    def __init__(self, count):
        order = [ring_order(place, count) for place in range(count)]
        self.count = count
        self.half = count // 2
        self.ahead = [(order[i], order[(i + 1) % count]) for i in range(count)]
        self.back = [(b, a) for a, b in self.ahead]
        mine = lax.axis_index("shard")
        self.place = jnp.where(mine % 2 == 1, (mine + 1) // 2, (count - mine // 2) % count)

    def owner(self, offset):
        return ring_order((self.place + self.count + offset) % self.count, self.count)

    def send(self, array, ahead):
        return lax.ppermute(array, "shard", self.ahead if ahead else self.back)


def tie(flows, *others):
    count = 2 * len(flows)
    sides = [side for flow in flows for side in (flow.right, flow.left)]
    tied = lax.optimization_barrier((*sides, *others))
    for index, flow in enumerate(flows):
        flow.right, flow.left = tied[2 * index : 2 * index + 2]
    others = tied[count:]
    return others[0] if len(others) == 1 else others


class Gather:
    def __init__(self, ring, array):
        self.ring = ring
        self.rows, self.cols = array.shape
        self.cut = (self.cols // (2 * LANES)) * LANES
        self.own = self.right = self.left = array
        self.done = 0
        self.pieces = [(array, 0, 0)]

    def step(self):
        self.done += 1
        if self.done < self.ring.half:
            self.right = self.ring.send(self.right, True)
            self.left = self.ring.send(self.left, False)
            self.pieces += [(self.right, -self.done, 0), (self.left, self.done, 0)]
        else:
            self.right = self.ring.send(self.right[:, : self.cut], True)
            self.left = self.ring.send(self.left[:, self.cut :], False)
            self.pieces += [(self.right, self.done, 0), (self.left, self.done, self.cut)]

    def owners(self):
        index = jnp.arange(len(self.pieces), dtype=jnp.int32)
        offset = (index + 1) // 2
        return self.ring.owner(jnp.where(index % 2 == 1, -offset, offset))

    def result(self, first=0):
        count = self.ring.count
        cols = self.cols - first
        whole = jnp.broadcast_to(self.own[None, :, first:], (count, self.rows, cols))
        for piece, offset, column in self.pieces[1:]:
            skip = max(first - column, 0)
            if skip < piece.shape[1]:
                start = (self.ring.owner(offset), 0, column + skip - first)
                whole = lax.dynamic_update_slice(whole, piece[None, :, skip:], start)
        return whole.reshape(count * self.rows, cols)

    def run(self):
        while self.done < self.ring.half:
            self.step()
        return self.result()


class ScatterSum:
    def __init__(self, ring, arrays):
        self.ring = ring
        self.rows = arrays[0].shape[0] // ring.count
        self.cols = sum(array.shape[1] for array in arrays)
        self.arrays = [array.reshape(ring.count, self.rows, -1) for array in arrays]
        self.cut = (self.cols // (2 * LANES)) * LANES
        self.done = 0
        far = self.chunk(ring.half)
        self.right = far[:, : self.cut]
        self.left = far[:, self.cut :]

    def chunk(self, offset):
        owner = self.ring.owner(offset)
        return jnp.concatenate(
            [lax.dynamic_index_in_dim(array, owner, 0, keepdims=False) for array in self.arrays],
            axis=1,
        )

    def add(self, offset, got, first, last):
        near = self.chunk(offset)
        part = (near[:, first:last].astype(F32) + got.astype(F32)).astype(BF16)
        return jnp.concatenate([near[:, :first], part, near[:, last:]], axis=1)

    def step(self):
        if self.done:
            offset = self.ring.half - self.done
            part = (0, self.cut, self.cols) if self.done == 1 else (0, self.cols, 0)
            self.right = self.add(offset, self.right, 0, part[1])
            self.left = self.add(-offset, self.left, part[1] if self.done == 1 else 0, self.cols)
        self.right = self.ring.send(self.right, True)
        self.left = self.ring.send(self.left, False)
        self.done += 1

    def result(self):
        return self.chunk(0).astype(F32) + self.right.astype(F32) + self.left.astype(F32)


def spread_sum(array):
    count = lax.axis_size("shard")
    arrived = lax.all_to_all(array, "shard", 0, 0, tiled=True)
    blocks = arrived.reshape(count, array.shape[0] // count, array.shape[1])
    return jnp.sum(blocks.astype(F32), axis=0)


def team_send(array, bit):
    return lax.ppermute(array, "rep", [(i, i ^ bit) for i in range(lax.axis_size("rep"))])


def team_sum(mine, core, cross, both):
    gathered = (cross.astype(F32) + team_send(both, 1).astype(F32)).astype(BF16)
    return (
        mine.astype(F32)
        + team_send(core, 1).astype(F32)
        + team_send(gathered, 2).astype(F32)
    )


def rope_tables(positions):
    half_width = HEAD // 2
    inverse = jnp.exp(
        jnp.arange(half_width, dtype=F32) * (-2.0 * math.log(ROPE_BASE) / HEAD)
    )
    angles = positions.astype(F32)[:, None] * inverse[None, :]
    cosine = jnp.cos(angles)
    sine = jnp.sin(angles)
    return (
        jnp.concatenate([cosine] * 4, axis=1),
        jnp.concatenate([-sine, sine, -sine, sine], axis=1),
    )


def rotate(source, cosine, sine):
    times = source.shape[1] // LANES
    return source * jnp.tile(cosine, (1, times)) + swap_halves(source) * jnp.tile(sine, (1, times))


def rotate_back(source, cosine, sine):
    times = source.shape[1] // LANES
    return source * jnp.tile(cosine, (1, times)) + swap_halves(source * jnp.tile(sine, (1, times)))


def norm_back(grad_normed, normed, inv_scale, gain_row):
    scaled = grad_normed * gain_row
    return inv_scale * (scaled - normed * jnp.mean(scaled * normed, axis=1, keepdims=True))


def body(
    hidden_in,
    cotangent,
    norm_gains,
    q_bias,
    kv_bias,
    q_weight,
    kv_weight,
    out_weight,
    gate_weight,
    up_weight,
    down_weight,
):
    tok_rows = hidden_in.shape[1]
    shard_count = lax.axis_size("shard")
    rep_count = lax.axis_size("rep")
    shard_place = lax.axis_index("shard")
    rep_place = lax.axis_index("rep")
    team_place = rep_place % TEAM
    row_share = D // shard_count
    kv_share = 2 * KW // shard_count
    ring = Ring(shard_count)
    core_place = rep_place % 2
    qkv_width = QW + 2 * KW
    teams = rep_count // TEAM
    across = [[t * TEAM + i for t in range(teams)] for i in range(TEAM)]

    small = jnp.concatenate([norm_gains[0], norm_gains[1], q_bias, kv_bias])
    spare = jnp.pad(small[None, :], ((0, 15), (0, qkv_width - small.shape[0])))
    qkv_piece = jnp.concatenate([jnp.concatenate([q_weight, kv_weight], axis=1), spare], axis=0)
    half_rows = (row_share + 16) // 2
    qkv_half = lax.dynamic_slice_in_dim(qkv_piece, core_place * half_rows, half_rows, 0)
    grad_out = cotangent[0]
    qkv_flow = Gather(ring, qkv_half)
    qkv_flow.step()
    c_cross = team_send(grad_out, 2)
    gate_weight, up_weight, down_weight, out_weight = tie(
        [qkv_flow], gate_weight, up_weight, down_weight, out_weight
    )

    def quarter(weight):
        padded = jnp.pad(weight, ((0, 0), (0, TEAM * FF_PART - FF)))
        return lax.dynamic_slice_in_dim(padded, team_place * FF_PART, FF_PART, 1)

    feed_piece = jnp.concatenate(
        [quarter(gate_weight), quarter(up_weight), quarter(down_weight), out_weight], axis=1
    )
    for _ in range(ring.half - 1):
        qkv_flow.step()
    feed_piece, c_cross = tie([qkv_flow], feed_piece, c_cross)
    mine = qkv_flow.result()
    other = team_send(mine, 1)
    halves = (jnp.where(core_place == 0, mine, other), jnp.where(core_place == 0, other, mine))
    qkv_all = jnp.concatenate(
        [half.reshape(shard_count, half_rows, qkv_width) for half in halves], axis=1
    )
    qkv_full = qkv_all[:, :row_share].reshape(D, qkv_width)
    smalls = qkv_all[:, row_share].astype(F32)
    gain_one = smalls[:, :row_share].reshape(D)
    gain_two = smalls[:, row_share : 2 * row_share].reshape(D)
    q_bias_all = smalls[:, 2 * row_share : 3 * row_share].reshape(QW)
    kv_bias_all = smalls[:, 3 * row_share : 3 * row_share + kv_share].reshape(2 * KW)
    bias = jnp.concatenate([q_bias_all, kv_bias_all])[None, :]
    q_full = qkv_full[:, :QW]
    kv_full = qkv_full[:, QW:]

    inputs = hidden_in[0].astype(F32)
    inv_one = lax.rsqrt(jnp.mean(inputs * inputs, axis=1, keepdims=True) + EPS)
    normed_one = inputs * inv_one
    h_one = (normed_one * gain_one).astype(BF16)
    positions = shard_place * tok_rows + jnp.arange(tok_rows, dtype=jnp.int32)
    cosine, sine = rope_tables(positions)
    kv_local = project(h_one, qkv_full, bias, cosine, sine, QW // LANES, 2 * KW // LANES)

    feeding = Gather(ring, feed_piece)
    flows = [feeding]
    feeding.step()
    kv_flow = Gather(ring, kv_local)
    kv_flow.step()
    late_out = tie([kv_flow], grad_out)
    c_both = team_send(late_out, 3)
    kv_whole = kv_flow.run()
    q_scaled = project(h_one, qkv_full, bias, cosine, sine, 0, QW // LANES)
    me = shard_place.astype(jnp.int32).reshape(1)
    kv_whole, late_out = tie(flows, kv_whole, late_out)
    c_core = team_send(late_out, 1)
    feeding.step()
    k_twice, v_twice, k_turned, v_turned = prepare(kv_whole)
    attn_one, lse_one = attn_forward(me, q_scaled, k_twice, v_turned, 0, 3)
    attn_one, q_scaled, c_core, c_both = tie(flows, attn_one, q_scaled, c_core, c_both)
    feeding.step()
    attn_two, lse_two = attn_forward(me, q_scaled, k_twice, v_turned, 3, 3)
    attn_two, q_scaled = tie(flows, attn_two, q_scaled)
    feeding.step()
    attn_three, lse_three = attn_forward(me, q_scaled, k_twice, v_turned, 6, 1)
    attn_three = tie(flows, attn_three)
    attn_b = jnp.concatenate([attn_one, attn_two, attn_three], axis=1)
    lse = jnp.concatenate([lse_one, lse_two, lse_three], axis=0)
    out_full = feeding.result(3 * FF_PART)

    middle = inputs + dot_nt(attn_b, out_full)
    inv_two = lax.rsqrt(jnp.mean(middle * middle, axis=1, keepdims=True) + EPS)
    normed_two = middle * inv_two
    h_two = (normed_two * gain_two).astype(BF16)
    if row_share % 16:
        feed_pieces = [(feeding.result(), 0)]
        feed_places = jnp.zeros((1,), jnp.int32)
    else:
        feed_pieces = [(piece, column) for piece, _, column in feeding.pieces]
        feed_places = feeding.owners()

    h_core = team_send(h_two, 1)
    h_cross = team_send(h_two, 2)
    here = feed((h_two, h_core), (grad_out, c_core), feed_pieces, feed_places)
    h_cross, *here = lax.optimization_barrier((h_cross, *here))
    h_both = team_send(h_cross, 1)
    cross = feed((h_cross,), (c_cross,), feed_pieces, feed_places)
    h_both, *cross = lax.optimization_barrier((h_both, *cross))
    both = feed((h_both,), (c_both,), feed_pieces, feed_places)
    out_parts = (here[0], here[1], cross[0], both[0])
    dh_mine, dh_core, dh_cross, dh_both = here[2], here[3], cross[1], both[1]

    dh_home = team_send(dh_core, 1)
    dh_away = (dh_cross.astype(F32) + team_send(dh_both, 1).astype(F32)).astype(BF16)
    dh_away, *hidden = lax.optimization_barrier((dh_away, *both[2:]))
    dh_back = team_send(dh_away, 2)
    h_sets = jnp.concatenate([h_two, h_core, h_cross, h_both], axis=0)
    c_sets = jnp.concatenate([grad_out, c_core, c_cross, c_both], axis=0)
    hid_sets, dg_sets, du_sets = (
        jnp.concatenate(parts, axis=0) for parts in zip(here[4:], cross[2:], hidden)
    )
    gate_grads = dot_tn(h_sets, dg_sets).astype(BF16)
    up_grads = dot_tn(h_sets, du_sets).astype(BF16)
    down_grads = dot_tn(c_sets, hid_sets).astype(BF16)
    dh_back, gate_grads, up_grads, down_grads = lax.optimization_barrier(
        (dh_back, gate_grads, up_grads, down_grads)
    )
    grad_h_two = dh_mine.astype(F32) + dh_home.astype(F32) + dh_back.astype(F32)

    gain_two_grad = jnp.sum(grad_h_two * normed_two, axis=0)
    grad_middle = grad_out.astype(F32) + norm_back(grad_h_two, normed_two, inv_two, gain_two)
    grad_branch_b = grad_middle.astype(BF16)
    grad_attn = dot_nn(grad_branch_b, out_full).astype(BF16)
    out_grads = dot_tn(grad_branch_b, attn_b).astype(BF16)
    row_sum = ScatterSum(ring, [gate_grads, up_grads, down_grads, out_grads])
    row_sum.step()

    tables = (cosine, sine)

    def backward(first, pairs, raw):
        tensors = (q_scaled, k_twice, k_turned, v_twice, attn_b, grad_attn, lse)
        return attn_backward(me, tensors, tables, first, pairs, raw)

    flows = [row_sum]
    grad_attn = tie(flows, grad_attn)
    row_sum.step()
    dq_one, _, raw = backward(0, 2, None)
    dq_one, raw, grad_attn = tie(flows, dq_one, raw, grad_attn)
    row_sum.step()
    dq_two, dkv_zero, raw = backward(2, 2, raw)
    dkv_zero, raw, grad_attn = tie(flows, dkv_zero, raw, grad_attn)
    row_sum.step()
    zero_sum = spread_sum(dkv_zero)
    dq_three, dkv_one, _ = backward(4, 3, raw)
    dq_three, dkv_one, zero_sum, *out_parts = tie(flows, dq_three, dkv_one, zero_sum, *out_parts)
    one_sum = spread_sum(dkv_one)
    mine, dq_three = lax.optimization_barrier((row_sum.result().astype(BF16), dq_three))
    cross = team_send(mine, 2)
    core = team_send(mine, 1)
    output = middle + team_sum(*out_parts)
    grad_q_b = jnp.concatenate([dq_one, dq_two, dq_three], axis=1)

    def team_total(rows):
        core, cross, both = (team_send(rows, bit).astype(F32) for bit in (1, 2, 3))
        rows = (rows.astype(F32) + core) + (cross + both)
        if teams > 1:
            rows = lax.psum(rows.astype(BF16), "rep", axis_index_groups=across).astype(F32)
        return rows

    q_bias_sum = jnp.sum(grad_q_b.astype(F32), axis=0)
    grad_h_q = dot_nt(grad_q_b, q_full)
    q_grads = dot_tn(h_one, grad_q_b).astype(BF16)
    q_grads = q_grads.reshape(shard_count, 2, 2, row_share // TEAM, QW)
    one_sum, q_grads = lax.optimization_barrier((one_sum, q_grads))

    def halve(array, axis, place, bit):
        keep = lax.dynamic_index_in_dim(array, place, axis, keepdims=False)
        give = lax.dynamic_index_in_dim(array, 1 - place, axis, keepdims=False)
        return (keep.astype(F32) + team_send(give, bit).astype(F32)).astype(BF16)

    q_grads = halve(halve(q_grads, 2, core_place, 1), 1, team_place // 2, 2)

    grad_k = jnp.concatenate([zero_sum[:, :HEAD], one_sum[:, :HEAD]], axis=1)
    grad_v = jnp.concatenate([zero_sum[:, HEAD:], one_sum[:, HEAD:]], axis=1)
    grad_kv_b = jnp.concatenate([rotate_back(grad_k, cosine, sine), grad_v], axis=1).astype(BF16)
    kv_bias_sum = jnp.sum(grad_kv_b.astype(F32), axis=0)
    grad_h_one = grad_h_q + dot_nt(grad_kv_b, kv_full)
    gain_one_grad = jnp.sum(grad_h_one * normed_one, axis=0)
    input_grad = (grad_middle + norm_back(grad_h_one, normed_one, inv_one, gain_one)).astype(BF16)

    width = 2 * KW
    late_weight = dot_tn(h_one, grad_kv_b).reshape(shard_count, row_share, width)
    smalls = jnp.concatenate(
        [
            one.reshape(shard_count, -1)
            for one in (gain_one_grad, gain_two_grad, q_bias_sum, kv_bias_sum)
        ],
        axis=1,
    )
    smalls = jnp.pad(smalls, ((0, 0), (0, 16 * width - smalls.shape[1])))
    last_sum = jnp.concatenate([late_weight, smalls.reshape(shard_count, 16, width)], axis=1)
    last_sum, cross = lax.optimization_barrier(
        (last_sum.reshape(-1, width).astype(BF16), cross)
    )
    both = team_send(cross, 1)
    last_sum, q_grads, both = lax.optimization_barrier((spread_sum(last_sum), q_grads, both))
    q_part = spread_sum(q_grads.reshape(-1, QW))
    last_rows = team_total(last_sum.astype(BF16))
    kv_rows = last_rows[:row_share]
    smalls = last_rows[row_share:].reshape(-1)
    gains_grad = smalls[: 2 * row_share].reshape(2, row_share)
    q_bias_grad = smalls[2 * row_share : 3 * row_share]
    kv_bias_grad = smalls[3 * row_share : 3 * row_share + kv_share]

    parts = [mine, core, cross, both]
    if teams > 1:
        parts = [lax.psum(part, "rep", axis_index_groups=across) for part in parts]
    outs = [part[:, 3 * FF_PART :].astype(F32) for part in parts]
    out_rows = (outs[0] + outs[1]) + (outs[2] + outs[3])
    gate_grad, up_grad, down_grad = columns(team_place, parts)
    gate_grad, up_grad, down_grad, q_part = lax.optimization_barrier(
        (gate_grad, up_grad, down_grad, q_part)
    )
    if teams > 1:
        q_part = lax.psum(q_part.astype(BF16), "rep", axis_index_groups=across)
    q_part = q_part.astype(BF16)
    q_parts = [q_part] + [team_send(q_part, bit) for bit in (1, 2, 3)]

    def quarter_at(place):
        bit = team_place ^ place
        low = jnp.where(bit == 0, q_parts[0], q_parts[1])
        return jnp.where(bit < 2, low, jnp.where(bit == 2, q_parts[2], q_parts[3]))

    q_rows = jnp.concatenate([quarter_at(place) for place in range(TEAM)], axis=0).astype(F32)
    return (
        output.astype(BF16)[None],
        input_grad[None],
        gains_grad,
        q_bias_grad,
        kv_bias_grad,
        q_rows,
        kv_rows,
        out_rows,
        gate_grad,
        up_grad,
        down_grad,
    )


def solution(mesh):
    tokens = P("rep", "shard", None)
    rows = P("shard", None)
    placed = (tokens, tokens, P(None, "shard"), P("shard"), P("shard")) + (rows,) * 6
    return jax.shard_map(body, mesh=mesh, in_specs=placed, out_specs=placed, check_vma=False)
```

```python
import functools
import math

import jax
import jax.numpy as jnp
from jax import lax
from jax.experimental import pallas as pl
from jax.experimental.pallas import tpu as pltpu
from jax.sharding import PartitionSpec as P

D = 896
HEADS = 14
KV_HEADS = 2
HEAD = 64
FF = 4864
QW = 896
KW = 128
LANES = 128
TEAM = 4
FF_PART = 1280
FF_TILE = 256
UNIT = 1024

EPS = 1e-06
ROPE_BASE = 1000000.0
F32 = jnp.float32
BF16 = jnp.bfloat16
VMEM_BYTES = 56 * 1024 * 1024


def dot_nt(left, right):
    return lax.dot_general(left, right, (((1,), (1,)), ((), ())), preferred_element_type=F32)


def dot_tn(left, right):
    return lax.dot_general(left, right, (((0,), (0,)), ((), ())), preferred_element_type=F32)


def dot_nn(left, right):
    return jnp.dot(left, right, preferred_element_type=F32)


def half_mask(parity, kind):
    lane = lax.broadcasted_iota(jnp.int32, (1, LANES), 1)
    return ((lane // HEAD) == parity).astype(kind)


def swap_halves(source):
    lane = lax.broadcasted_iota(jnp.int32, source.shape, 1)
    ahead = jnp.roll(source, -(HEAD // 2), axis=1)
    behind = jnp.roll(source, HEAD // 2, axis=1)
    return jnp.where(lane % HEAD < HEAD // 2, ahead, behind)


def seen(me, rows, unit):
    base = (me * rows // UNIT) * UNIT
    key = lax.broadcasted_iota(jnp.int32, (UNIT, rows), 0) + base
    query = lax.broadcasted_iota(jnp.int32, (UNIT, rows), 1) + me * rows
    return key <= query


def attn_forward_kernel(me_ref, q_ref, k_ref, vt_ref, o_ref, lse_ref):
    pair = pl.program_id(0) + me_ref[1]
    me = me_ref[0]
    rows = q_ref.shape[0]
    group = HEADS // KV_HEADS
    last = me * rows // UNIT
    allowed = seen(me, rows, last)
    heads = [((2 * pair + parity) // group, q_ref[...] * half_mask(parity, BF16)) for parity in range(2)]

    def span(unit):
        return pl.ds(unit * UNIT, UNIT)

    def scores(head, unit):
        return dot_nt(k_ref[head[0], span(unit), :], head[1])

    def weigh(head, unit, probs):
        return dot_nn(vt_ref[head[0], :, span(unit)], probs.astype(BF16))

    tops, probs = [], []
    for head in heads:
        s = jnp.where(allowed, scores(head, last), -1e30)
        tops.append(jnp.max(s, axis=0, keepdims=True))
        probs.append(jnp.exp(s - tops[-1]))
    start = tuple(
        (jnp.sum(p, axis=0, keepdims=True), weigh(head, last, p)) for head, p in zip(heads, probs)
    )

    def quick(unit, state):
        probs = [jnp.exp(scores(head, unit) - top) for head, top in zip(heads, tops)]
        return tuple(
            (total + jnp.sum(p, axis=0, keepdims=True), acc + weigh(head, unit, p))
            for head, (total, acc), p in zip(heads, state, probs)
        )

    def careful(unit, state):
        after = []
        for head, (top, total, acc) in zip(heads, state):
            s = scores(head, unit)
            new_top = jnp.maximum(top, jnp.max(s, axis=0, keepdims=True))
            shrink = jnp.exp(top - new_top)
            p = jnp.exp(s - new_top)
            total = total * shrink + jnp.sum(p, axis=0, keepdims=True)
            after.append((new_top, total, acc * shrink + weigh(head, unit, p)))
        return tuple(after)

    def store(state):
        for parity, (top, total, acc) in enumerate(state):
            lse_ref[0, parity : parity + 1, :] = top + jnp.log(total)
        both = jnp.concatenate([acc / total for top, total, acc in state], axis=0)
        o_ref[...] = jnp.transpose(both).astype(BF16)

    state = lax.fori_loop(0, last, quick, start)
    largest = jnp.max(jnp.maximum(state[0][0], state[1][0]))
    fine = largest < 1e30

    @pl.when(fine)
    def _():
        store([(top, total, acc) for top, (total, acc) in zip(tops, state)])

    @pl.when(jnp.logical_not(fine))
    def _():
        begin = tuple((top, total, acc) for top, (total, acc) in zip(tops, start))
        store(lax.fori_loop(0, last, careful, begin))


def attn_forward(me, q, k_twice, v_turned, first, pairs):
    rows = q.shape[0]
    length = k_twice.shape[1]
    blocks = length // rows
    scalars = jnp.concatenate([me, jnp.full((1,), first, jnp.int32)])
    return pl.pallas_call(
        attn_forward_kernel,
        grid_spec=pltpu.PrefetchScalarGridSpec(
            num_scalar_prefetch=1,
            grid=(pairs,),
            in_specs=[
                pl.BlockSpec((rows, LANES), lambda i, me: (0, first + i)),
                pl.BlockSpec((KV_HEADS, length, LANES), lambda i, me: (0, 0, 0)),
                pl.BlockSpec((KV_HEADS, HEAD, length), lambda i, me: (0, 0, 0)),
            ],
            out_specs=[
                pl.BlockSpec((rows, LANES), lambda i, me: (0, i)),
                pl.BlockSpec((1, 2, rows), lambda i, me: (i, 0, 0)),
            ],
        ),
        out_shape=[
            jax.ShapeDtypeStruct((rows, pairs * LANES), BF16),
            jax.ShapeDtypeStruct((pairs, 2, rows), F32),
        ],
        compiler_params=pltpu.CompilerParams(vmem_limit_bytes=VMEM_BYTES),
        cost_estimate=pl.CostEstimate(
            flops=32 * blocks * pairs * rows * rows * HEAD,
            bytes_accessed=4 * rows * pairs * LANES + 6 * length * LANES,
            transcendentals=blocks * 2 * pairs * rows * rows,
        ),
        name="attn_forward",
    )(scalars, q, k_twice, v_turned)


def attn_backward_kernel(spec, *refs):
    first, pairs, start, finish, carry_in, carry_out = spec
    refs = list(refs)
    me_ref, q_ref, k_ref, kt_ref, v_ref, o_ref, do_ref, lse_ref, cos_ref, sin_ref = refs[:10]
    at = 10
    if carry_in:
        raw_in = refs[at]
        at += 1
    dq_ref = refs[at]
    at += 1
    if finish is not None:
        folded = refs[at]
        at += 1
    if carry_out:
        raw_out = refs[at]
        at += 1
    acc, moved = refs[at:]
    step_index = pl.program_id(0)
    pair = step_index + first
    me = me_ref[0]
    rows = q_ref.shape[0]
    group = HEADS // KV_HEADS
    held = acc.shape[0]
    last = me * rows // UNIT
    allowed = seen(me, rows, last)

    @pl.when(step_index == 0)
    def _():
        if carry_in:
            pltpu.make_async_copy(raw_in, acc.at[0], moved.at[0]).start()
        else:
            acc[0] = jnp.zeros(acc.shape[1:], F32)
        for more in range(1, held):
            acc[more] = jnp.zeros(acc.shape[1:], F32)
        if carry_in:
            pltpu.make_async_copy(raw_in, acc.at[0], moved.at[0]).wait()

    products = do_ref[...].astype(F32) * o_ref[...].astype(F32)
    heads = []
    for parity in range(2):
        kv_head = (2 * pair + parity) // group
        mask = half_mask(parity, BF16)
        picks = jnp.broadcast_to(half_mask(parity, F32), (8, LANES))
        delta = lax.dot_general(
            picks,
            products,
            (((1,), (1,)), ((), ())),
            precision=lax.Precision.HIGHEST,
            preferred_element_type=F32,
        )[0:1, :]
        lse = lse_ref[0, parity : parity + 1, :]
        heads.append((kv_head, q_ref[...] * mask, do_ref[...] * mask, lse, delta))

    def unit_step(unit, dqs, masked):
        span = pl.ds(unit * UNIT, UNIT)
        probs, d_scores = [], []
        for kv_head, q_head, do_head, lse, delta in heads:
            p = jnp.exp(dot_nt(k_ref[kv_head, span, :], q_head) - lse)
            if masked:
                p = jnp.where(allowed, p, 0.0)
            d_p = dot_nt(v_ref[kv_head, span, :], do_head)
            probs.append(p.astype(BF16))
            d_scores.append((p * (d_p - delta)).astype(BF16))
        after = []
        for (kv_head, q_head, do_head, _, _), p, d_s, dq in zip(heads, probs, d_scores, dqs):
            place = kv_head - start
            acc[place, 1, span, :] += dot_nn(p, do_head)
            acc[place, 0, span, :] += dot_nn(d_s, q_head)
            after.append(dq + dot_nn(kt_ref[kv_head, :, span], d_s))
        return tuple(after)

    zero = jnp.zeros((HEAD, rows), F32)
    dqs = unit_step(last, (zero, zero), True)
    dqs = lax.fori_loop(0, last, lambda unit, dqs: unit_step(unit, dqs, False), dqs)
    dq = jnp.transpose(jnp.concatenate(dqs, axis=0)) * HEAD ** (-0.5)
    dq_ref[...] = (dq * cos_ref[...] + swap_halves(dq * sin_ref[...])).astype(BF16)

    @pl.when(step_index == pairs - 1)
    def _():
        if carry_out:
            leave = pltpu.make_async_copy(acc.at[held - 1], raw_out, moved.at[1])
            leave.start()
        if finish is not None:
            low = half_mask(0, jnp.int32) > 0

            def fold(block, carry):
                span = pl.ds(block * rows, rows)
                keys = acc[0, 0, span, :]
                values = acc[0, 1, span, :]
                keys = keys + pltpu.roll(keys, HEAD, 1)
                values = values + pltpu.roll(values, HEAD, 1)
                folded[span, :] = jnp.where(low, keys, values).astype(BF16)
                return carry

            lax.fori_loop(0, acc.shape[2] // rows, fold, 0)
        if carry_out:
            leave.wait()


def attn_backward(me, tensors, tables, first, pairs, raw=None):
    q, k_twice, k_turned, v_twice, o, d_o, lse = tensors
    rows = q.shape[0]
    length = k_twice.shape[1]
    blocks = length // rows
    group = HEADS // KV_HEADS
    start = 2 * first // group
    end = (2 * (first + pairs) - 1) // group
    finish = start if 2 * (first + pairs) >= group * (start + 1) else None
    carry_out = finish is None or end > start
    spec = (first, pairs, start, finish, raw is not None, carry_out)
    once = {"pipeline_mode": pl.Buffered(1)}
    whole = pl.BlockSpec((KV_HEADS, length, LANES), lambda i, me: (0, 0, 0), **once)
    turned = pl.BlockSpec((KV_HEADS, HEAD, length), lambda i, me: (0, 0, 0), **once)
    pair = pl.BlockSpec((rows, LANES), lambda i, me: (0, first + i))
    table = pl.BlockSpec((rows, LANES), lambda i, me: (0, 0))
    raw_shape = jax.ShapeDtypeStruct((2, length, LANES), F32)
    raw_spec = pl.BlockSpec(memory_space=pl.ANY)
    in_specs = [
        pair,
        whole,
        turned,
        whole,
        pair,
        pair,
        pl.BlockSpec((1, 2, rows), lambda i, me: (first + i, 0, 0)),
        table,
        table,
    ]
    operands = [q, k_twice, k_turned, v_twice, o, d_o, lse, *tables]
    if raw is not None:
        in_specs.append(raw_spec)
        operands.append(raw)
    out_specs = [pl.BlockSpec((rows, LANES), lambda i, me: (0, i))]
    out_shape = [jax.ShapeDtypeStruct((rows, pairs * LANES), BF16)]
    if finish is not None:
        out_specs.append(pl.BlockSpec((length, LANES), lambda i, me: (0, 0)))
        out_shape.append(jax.ShapeDtypeStruct((length, LANES), BF16))
    if carry_out:
        out_specs.append(raw_spec)
        out_shape.append(raw_shape)
    outs = pl.pallas_call(
        functools.partial(attn_backward_kernel, spec),
        grid_spec=pltpu.PrefetchScalarGridSpec(
            num_scalar_prefetch=1,
            grid=(pairs,),
            in_specs=in_specs,
            out_specs=out_specs,
            scratch_shapes=[
                pltpu.VMEM((end - start + 1, 2, length, LANES), F32),
                pltpu.SemaphoreType.DMA((2,)),
            ],
        ),
        out_shape=out_shape,
        compiler_params=pltpu.CompilerParams(vmem_limit_bytes=VMEM_BYTES),
        cost_estimate=pl.CostEstimate(
            flops=80 * blocks * pairs * rows * rows * HEAD,
            bytes_accessed=8 * rows * pairs * LANES + 16 * length * LANES,
            transcendentals=blocks * 2 * pairs * rows * rows,
        ),
        name="attn_backward",
    )(me, *operands)
    dq = outs[0]
    folded = outs[1] if finish is not None else None
    return dq, folded, outs[-1] if carry_out else None


def feed_kernel(sets, spans, place_ref, *refs):
    h_refs, c_refs, refs = refs[:sets], refs[sets : 2 * sets], refs[2 * sets :]
    pieces, refs = refs[: len(spans)], refs[len(spans) :]
    out_refs, dh_refs, refs = refs[:sets], refs[sets : 2 * sets], refs[2 * sets :]
    hid_ref, dg_ref, du_ref, w_ref, arrived = refs
    tiles = FF_PART // FF_TILE
    step = pl.program_id(0)
    former = step < pl.num_programs(0) // sets

    def fetch(index):
        piece, (column, width) = pieces[index], spans[index]
        rows = piece.shape[0]
        start = pl.multiple_of(place_ref[index] * rows, 16)
        source = piece.at[:, pl.ds(0, width)]
        target = w_ref.at[pl.ds(start, rows), pl.ds(column, width)]
        return pltpu.make_async_copy(source, target, arrived.at[index])

    @pl.when(step == 0)
    def _():
        for index in range(len(spans)):
            fetch(index).start()
        for index in range(len(spans)):
            fetch(index).wait()

    if sets == 1:
        h, c = h_refs[0][...], c_refs[0][...]
    else:
        h = jnp.where(former, h_refs[0][...], h_refs[1][...])
        c = jnp.where(former, c_refs[0][...], c_refs[1][...])
    for t in range(tiles):

        def weights(m):
            start = m * FF_PART + t * FF_TILE
            return w_ref[:, start : start + FF_TILE]

        gate = dot_nn(h, weights(0))
        up = dot_nn(h, weights(1))
        d_hid = dot_nn(c, weights(2))
        sig = jax.nn.sigmoid(gate)
        silu = gate * sig
        span = slice(t * FF_TILE, (t + 1) * FF_TILE)
        hid_ref[:, span] = (silu * up).astype(BF16)
        dg_ref[:, span] = (d_hid * up * sig * (1.0 + gate * (1.0 - sig))).astype(BF16)
        du_ref[:, span] = (d_hid * silu).astype(BF16)
    gates = w_ref[:, :FF_PART]
    ups = w_ref[:, FF_PART : 2 * FF_PART]
    downs = w_ref[:, 2 * FF_PART :]
    d_h = (dot_nt(dg_ref[...], gates) + dot_nt(du_ref[...], ups)).astype(BF16)
    out = dot_nt(hid_ref[...], downs).astype(BF16)

    @pl.when(former)
    def _():
        dh_refs[0][...] = d_h
        out_refs[0][...] = out

    @pl.when(jnp.logical_not(former))
    def _():
        dh_refs[-1][...] = d_h
        out_refs[-1][...] = out


def feed(h_sets, c_sets, pieces, places):
    sets = len(h_sets)
    count = h_sets[0].shape[0]
    rows = 256
    steps = count // rows
    one = pl.BlockSpec((rows, D), lambda i, place: (jnp.minimum(i, steps - 1), 0))
    two = pl.BlockSpec((rows, D), lambda i, place: (jnp.maximum(i - steps, 0), 0))
    token_specs = [one, two][:sets]
    hidden = pl.BlockSpec((rows, FF_PART), lambda i, place: (i, 0))
    spans = tuple(
        (column, min(array.shape[1], 3 * FF_PART - column)) for array, column in pieces
    )
    return pl.pallas_call(
        functools.partial(feed_kernel, sets, spans),
        grid_spec=pltpu.PrefetchScalarGridSpec(
            num_scalar_prefetch=1,
            grid=(sets * steps,),
            in_specs=token_specs * 2 + [pl.BlockSpec(memory_space=pl.ANY)] * len(pieces),
            out_specs=token_specs * 2 + [hidden, hidden, hidden],
            scratch_shapes=[
                pltpu.VMEM((D, 3 * FF_PART), BF16),
                pltpu.SemaphoreType.DMA((len(pieces),)),
            ],
        ),
        out_shape=[jax.ShapeDtypeStruct((count, D), BF16)] * (2 * sets)
        + [jax.ShapeDtypeStruct((sets * count, FF_PART), BF16)] * 3,
        compiler_params=pltpu.CompilerParams(vmem_limit_bytes=VMEM_BYTES),
        cost_estimate=pl.CostEstimate(
            flops=20 * sets * count * D * FF_PART,
            bytes_accessed=6 * D * FF_PART + sets * count * (8 * D + 6 * FF_PART),
            transcendentals=sets * count * FF_PART,
        ),
        name="feed",
    )(places, *h_sets, *c_sets, *[array for array, _ in pieces])


def columns_kernel(team_ref, *refs):
    parts, outs = refs[:TEAM], refs[TEAM:]
    team = team_ref[0]
    for place in range(TEAM):
        bit = team ^ place
        width = min(FF_PART, FF - place * FF_PART)
        for matrix, out in enumerate(outs):
            span = slice(matrix * FF_PART, matrix * FF_PART + width)
            low = jnp.where(bit == 0, parts[0][:, span].astype(F32), parts[1][:, span].astype(F32))
            high = jnp.where(bit == 2, parts[2][:, span].astype(F32), parts[3][:, span].astype(F32))
            out[:, place * FF_PART : place * FF_PART + width] = jnp.where(bit < 2, low, high)


def columns(team_place, parts):
    rows = parts[0].shape[0]
    return pl.pallas_call(
        columns_kernel,
        grid_spec=pltpu.PrefetchScalarGridSpec(
            num_scalar_prefetch=1,
            grid=(1,),
            in_specs=[pl.BlockSpec((rows, 3 * FF_PART), lambda i, team: (0, 0))] * TEAM,
            out_specs=[pl.BlockSpec((rows, FF), lambda i, team: (0, 0))] * 3,
        ),
        out_shape=[jax.ShapeDtypeStruct((rows, FF), F32)] * 3,
        compiler_params=pltpu.CompilerParams(vmem_limit_bytes=VMEM_BYTES),
        cost_estimate=pl.CostEstimate(
            flops=rows * FF, bytes_accessed=20 * rows * FF, transcendentals=0
        ),
        name="columns",
    )(team_place.astype(jnp.int32).reshape(1), *parts)


def project_kernel(first, h_ref, w_ref, b_ref, cos_ref, sin_ref, out_ref):
    block = pl.program_id(0) + first
    flat = dot_nn(h_ref[...], w_ref[...]) + b_ref[...]
    turned = flat * cos_ref[...] + swap_halves(flat) * sin_ref[...]
    kept = jnp.where(block < (QW + KW) // LANES, turned, flat)
    scale = jnp.where(block < QW // LANES, HEAD ** (-0.5), 1.0)
    out_ref[...] = (kept * scale).astype(BF16)


def project(h, weights, bias, cosine, sine, first, count):
    rows = h.shape[0]
    table = pl.BlockSpec((rows, LANES), lambda i: (0, 0))
    return pl.pallas_call(
        functools.partial(project_kernel, first),
        grid=(count,),
        in_specs=[
            pl.BlockSpec((rows, D), lambda i: (0, 0)),
            pl.BlockSpec((D, LANES), lambda i: (0, first + i)),
            pl.BlockSpec((1, LANES), lambda i: (0, first + i)),
            table,
            table,
        ],
        out_specs=pl.BlockSpec((rows, LANES), lambda i: (0, i)),
        out_shape=jax.ShapeDtypeStruct((rows, count * LANES), BF16),
        cost_estimate=pl.CostEstimate(
            flops=2 * rows * D * count * LANES,
            bytes_accessed=2 * (D * count * LANES + rows * D),
            transcendentals=0,
        ),
        name="project",
    )(h, weights, bias, cosine, sine)


def prepare_kernel(kv_ref, k_ref, v_ref, kt_ref, vt_ref):
    low = half_mask(0, jnp.int32) > 0
    for place, twice, turned in ((0, k_ref, kt_ref), (1, v_ref, vt_ref)):
        block = kv_ref[:, place * LANES : (place + 1) * LANES].astype(F32)
        other = pltpu.roll(block, HEAD, 1)
        twice[0] = jnp.where(low, block, other).astype(BF16)
        twice[1] = jnp.where(low, other, block).astype(BF16)
        across = jnp.transpose(block).astype(BF16)
        turned[0] = across[:HEAD]
        turned[1] = across[HEAD:]


def prepare(kv_whole):
    length = kv_whole.shape[0]
    rows = 512
    twice = pl.BlockSpec((KV_HEADS, rows, LANES), lambda i: (0, i, 0))
    turned = pl.BlockSpec((KV_HEADS, HEAD, rows), lambda i: (0, 0, i))
    return pl.pallas_call(
        prepare_kernel,
        grid=(length // rows,),
        in_specs=[pl.BlockSpec((rows, 2 * KW), lambda i: (i, 0))],
        out_specs=[twice, twice, turned, turned],
        out_shape=[jax.ShapeDtypeStruct((KV_HEADS, length, LANES), BF16)] * 2
        + [jax.ShapeDtypeStruct((KV_HEADS, HEAD, length), BF16)] * 2,
        cost_estimate=pl.CostEstimate(
            flops=8 * length * LANES, bytes_accessed=16 * length * LANES, transcendentals=0
        ),
        name="prepare",
    )(kv_whole)


def ring_order(place, count):
    up = 2 * place - 1
    down = 2 * (count - place)
    if isinstance(place, int):
        return 0 if place == 0 else up if place <= count // 2 else down
    return jnp.where(place == 0, 0, jnp.where(place <= count // 2, up, down))


class Ring:
    def __init__(self, count):
        order = [ring_order(place, count) for place in range(count)]
        self.count = count
        self.half = count // 2
        self.ahead = [(order[i], order[(i + 1) % count]) for i in range(count)]
        self.back = [(b, a) for a, b in self.ahead]
        mine = lax.axis_index("shard")
        self.place = jnp.where(mine % 2 == 1, (mine + 1) // 2, (count - mine // 2) % count)

    def owner(self, offset):
        return ring_order((self.place + self.count + offset) % self.count, self.count)

    def send(self, array, ahead):
        return lax.ppermute(array, "shard", self.ahead if ahead else self.back)


def tie(flows, *others):
    count = 2 * len(flows)
    sides = [side for flow in flows for side in (flow.right, flow.left)]
    tied = lax.optimization_barrier((*sides, *others))
    for index, flow in enumerate(flows):
        flow.right, flow.left = tied[2 * index : 2 * index + 2]
    others = tied[count:]
    return others[0] if len(others) == 1 else others


class Gather:
    def __init__(self, ring, array):
        self.ring = ring
        self.rows, self.cols = array.shape
        self.cut = (self.cols // (2 * LANES)) * LANES
        self.own = self.right = self.left = array
        self.done = 0
        self.pieces = [(array, 0, 0)]

    def step(self):
        self.done += 1
        if self.done < self.ring.half:
            self.right = self.ring.send(self.right, True)
            self.left = self.ring.send(self.left, False)
            self.pieces += [(self.right, -self.done, 0), (self.left, self.done, 0)]
        else:
            self.right = self.ring.send(self.right[:, : self.cut], True)
            self.left = self.ring.send(self.left[:, self.cut :], False)
            self.pieces += [(self.right, self.done, 0), (self.left, self.done, self.cut)]

    def owners(self):
        index = jnp.arange(len(self.pieces), dtype=jnp.int32)
        offset = (index + 1) // 2
        return self.ring.owner(jnp.where(index % 2 == 1, -offset, offset))

    def result(self, first=0):
        count = self.ring.count
        cols = self.cols - first
        whole = jnp.broadcast_to(self.own[None, :, first:], (count, self.rows, cols))
        for piece, offset, column in self.pieces[1:]:
            skip = max(first - column, 0)
            if skip < piece.shape[1]:
                start = (self.ring.owner(offset), 0, column + skip - first)
                whole = lax.dynamic_update_slice(whole, piece[None, :, skip:], start)
        return whole.reshape(count * self.rows, cols)

    def run(self):
        while self.done < self.ring.half:
            self.step()
        return self.result()


class ScatterSum:
    def __init__(self, ring, arrays):
        self.ring = ring
        self.rows = arrays[0].shape[0] // ring.count
        self.cols = sum(array.shape[1] for array in arrays)
        self.arrays = [array.reshape(ring.count, self.rows, -1) for array in arrays]
        self.cut = (self.cols // (2 * LANES)) * LANES
        self.done = 0
        far = self.chunk(ring.half)
        self.right = far[:, : self.cut]
        self.left = far[:, self.cut :]

    def chunk(self, offset):
        owner = self.ring.owner(offset)
        return jnp.concatenate(
            [lax.dynamic_index_in_dim(array, owner, 0, keepdims=False) for array in self.arrays],
            axis=1,
        )

    def add(self, offset, got, first, last):
        near = self.chunk(offset)
        part = (near[:, first:last].astype(F32) + got.astype(F32)).astype(BF16)
        return jnp.concatenate([near[:, :first], part, near[:, last:]], axis=1)

    def step(self):
        if self.done:
            offset = self.ring.half - self.done
            part = (0, self.cut, self.cols) if self.done == 1 else (0, self.cols, 0)
            self.right = self.add(offset, self.right, 0, part[1])
            self.left = self.add(-offset, self.left, part[1] if self.done == 1 else 0, self.cols)
        self.right = self.ring.send(self.right, True)
        self.left = self.ring.send(self.left, False)
        self.done += 1

    def result(self):
        return self.chunk(0).astype(F32) + self.right.astype(F32) + self.left.astype(F32)


def spread_sum(array):
    count = lax.axis_size("shard")
    arrived = lax.all_to_all(array, "shard", 0, 0, tiled=True)
    blocks = arrived.reshape(count, array.shape[0] // count, array.shape[1])
    return jnp.sum(blocks.astype(F32), axis=0)


def team_send(array, bit):
    return lax.ppermute(array, "rep", [(i, i ^ bit) for i in range(lax.axis_size("rep"))])


def rope_tables(positions):
    half_width = HEAD // 2
    inverse = jnp.exp(
        jnp.arange(half_width, dtype=F32) * (-2.0 * math.log(ROPE_BASE) / HEAD)
    )
    angles = positions.astype(F32)[:, None] * inverse[None, :]
    cosine = jnp.cos(angles)
    sine = jnp.sin(angles)
    return (
        jnp.concatenate([cosine] * 4, axis=1),
        jnp.concatenate([-sine, sine, -sine, sine], axis=1),
    )


def rotate(source, cosine, sine):
    times = source.shape[1] // LANES
    return source * jnp.tile(cosine, (1, times)) + swap_halves(source) * jnp.tile(sine, (1, times))


def rotate_back(source, cosine, sine):
    times = source.shape[1] // LANES
    return source * jnp.tile(cosine, (1, times)) + swap_halves(source * jnp.tile(sine, (1, times)))


def norm_back(grad_normed, normed, inv_scale, gain_row):
    scaled = grad_normed * gain_row
    return inv_scale * (scaled - normed * jnp.mean(scaled * normed, axis=1, keepdims=True))


def body(
    hidden_in,
    cotangent,
    norm_gains,
    q_bias,
    kv_bias,
    q_weight,
    kv_weight,
    out_weight,
    gate_weight,
    up_weight,
    down_weight,
):
    tok_rows = hidden_in.shape[1]
    shard_count = lax.axis_size("shard")
    rep_count = lax.axis_size("rep")
    shard_place = lax.axis_index("shard")
    rep_place = lax.axis_index("rep")
    team_place = rep_place % TEAM
    row_share = D // shard_count
    kv_share = 2 * KW // shard_count
    ring = Ring(shard_count)
    core_place = rep_place % 2
    qkv_width = QW + 2 * KW
    teams = rep_count // TEAM
    across = [[t * TEAM + i for t in range(teams)] for i in range(TEAM)]

    small = jnp.concatenate([norm_gains[0], norm_gains[1], q_bias, kv_bias])
    spare = jnp.pad(small[None, :], ((0, 15), (0, qkv_width - small.shape[0])))
    qkv_piece = jnp.concatenate([jnp.concatenate([q_weight, kv_weight], axis=1), spare], axis=0)
    half_rows = (row_share + 16) // 2
    qkv_half = lax.dynamic_slice_in_dim(qkv_piece, core_place * half_rows, half_rows, 0)
    grad_out = cotangent[0]
    qkv_flow = Gather(ring, qkv_half)
    qkv_flow.step()
    c_cross = team_send(grad_out, 2)
    gate_weight, up_weight, down_weight, out_weight = tie(
        [qkv_flow], gate_weight, up_weight, down_weight, out_weight
    )

    def quarter(weight):
        padded = jnp.pad(weight, ((0, 0), (0, TEAM * FF_PART - FF)))
        return lax.dynamic_slice_in_dim(padded, team_place * FF_PART, FF_PART, 1)

    feed_piece = jnp.concatenate(
        [quarter(gate_weight), quarter(up_weight), quarter(down_weight), out_weight], axis=1
    )
    for _ in range(ring.half - 1):
        qkv_flow.step()
    feed_piece, c_cross = tie([qkv_flow], feed_piece, c_cross)
    mine = qkv_flow.result()
    other = team_send(mine, 1)
    halves = (jnp.where(core_place == 0, mine, other), jnp.where(core_place == 0, other, mine))
    qkv_all = jnp.concatenate(
        [half.reshape(shard_count, half_rows, qkv_width) for half in halves], axis=1
    )
    qkv_full = qkv_all[:, :row_share].reshape(D, qkv_width)
    smalls = qkv_all[:, row_share].astype(F32)
    gain_one = smalls[:, :row_share].reshape(D)
    gain_two = smalls[:, row_share : 2 * row_share].reshape(D)
    q_bias_all = smalls[:, 2 * row_share : 3 * row_share].reshape(QW)
    kv_bias_all = smalls[:, 3 * row_share : 3 * row_share + kv_share].reshape(2 * KW)
    bias = jnp.concatenate([q_bias_all, kv_bias_all])[None, :]
    q_full = qkv_full[:, :QW]
    kv_full = qkv_full[:, QW:]

    inputs = hidden_in[0].astype(F32)
    inv_one = lax.rsqrt(jnp.mean(inputs * inputs, axis=1, keepdims=True) + EPS)
    normed_one = inputs * inv_one
    h_one = (normed_one * gain_one).astype(BF16)
    positions = shard_place * tok_rows + jnp.arange(tok_rows, dtype=jnp.int32)
    cosine, sine = rope_tables(positions)
    kv_local = project(h_one, qkv_full, bias, cosine, sine, QW // LANES, 2 * KW // LANES)

    feeding = Gather(ring, feed_piece)
    flows = [feeding]
    feeding.step()
    kv_flow = Gather(ring, kv_local)
    kv_flow.step()
    late_out = tie([kv_flow], grad_out)
    c_both = team_send(late_out, 3)
    kv_whole = kv_flow.run()
    q_scaled = project(h_one, qkv_full, bias, cosine, sine, 0, QW // LANES)
    me = shard_place.astype(jnp.int32).reshape(1)
    kv_whole, late_out = tie(flows, kv_whole, late_out)
    c_core = team_send(late_out, 1)
    feeding.step()
    k_twice, v_twice, k_turned, v_turned = prepare(kv_whole)
    attn_one, lse_one = attn_forward(me, q_scaled, k_twice, v_turned, 0, 3)
    attn_one, q_scaled, c_core, c_both = tie(flows, attn_one, q_scaled, c_core, c_both)
    feeding.step()
    attn_two, lse_two = attn_forward(me, q_scaled, k_twice, v_turned, 3, 3)
    attn_two, q_scaled = tie(flows, attn_two, q_scaled)
    feeding.step()
    attn_three, lse_three = attn_forward(me, q_scaled, k_twice, v_turned, 6, 1)
    attn_three = tie(flows, attn_three)
    attn_b = jnp.concatenate([attn_one, attn_two, attn_three], axis=1)
    lse = jnp.concatenate([lse_one, lse_two, lse_three], axis=0)
    out_full = feeding.result(3 * FF_PART)

    middle = inputs + dot_nt(attn_b, out_full)
    inv_two = lax.rsqrt(jnp.mean(middle * middle, axis=1, keepdims=True) + EPS)
    normed_two = middle * inv_two
    h_two = (normed_two * gain_two).astype(BF16)
    if row_share % 16:
        feed_pieces = [(feeding.result(), 0)]
        feed_places = jnp.zeros((1,), jnp.int32)
    else:
        feed_pieces = [(piece, column) for piece, _, column in feeding.pieces]
        feed_places = feeding.owners()

    h_core = team_send(h_two, 1)
    h_cross = team_send(h_two, 2)
    here = feed((h_two, h_core), (grad_out, c_core), feed_pieces, feed_places)
    h_cross, *here = lax.optimization_barrier((h_cross, *here))
    h_both = team_send(h_cross, 1)
    cross = feed((h_cross,), (c_cross,), feed_pieces, feed_places)
    h_both, *cross = lax.optimization_barrier((h_both, *cross))
    both = feed((h_both,), (c_both,), feed_pieces, feed_places)
    out_parts = (here[0], here[1], cross[0], both[0])
    dh_mine, dh_core, dh_cross, dh_both = here[2], here[3], cross[1], both[1]

    dh_home = team_send(dh_core, 1)
    dh_away = (dh_cross.astype(F32) + team_send(dh_both, 1).astype(F32)).astype(BF16)
    dh_away, *hidden = lax.optimization_barrier((dh_away, *both[2:]))
    dh_back = team_send(dh_away, 2)
    h_sets = jnp.concatenate([h_two, h_core, h_cross, h_both], axis=0)
    c_sets = jnp.concatenate([grad_out, c_core, c_cross, c_both], axis=0)
    hid_sets, dg_sets, du_sets = (
        jnp.concatenate(parts, axis=0) for parts in zip(here[4:], cross[2:], hidden)
    )
    gate_grads = dot_tn(h_sets, dg_sets).astype(BF16)
    up_grads = dot_tn(h_sets, du_sets).astype(BF16)
    down_grads = dot_tn(c_sets, hid_sets).astype(BF16)
    dh_back, gate_grads, up_grads, down_grads = lax.optimization_barrier(
        (dh_back, gate_grads, up_grads, down_grads)
    )
    grad_h_two = dh_mine.astype(F32) + dh_home.astype(F32) + dh_back.astype(F32)

    gain_two_grad = jnp.sum(grad_h_two * normed_two, axis=0)
    grad_middle = grad_out.astype(F32) + norm_back(grad_h_two, normed_two, inv_two, gain_two)
    grad_branch_b = grad_middle.astype(BF16)
    grad_attn = dot_nn(grad_branch_b, out_full).astype(BF16)
    out_grads = dot_tn(grad_branch_b, attn_b).astype(BF16)
    row_sum = ScatterSum(ring, [gate_grads, up_grads, down_grads, out_grads])
    row_sum.step()

    tables = (cosine, sine)

    def backward(first, pairs, raw):
        tensors = (q_scaled, k_twice, k_turned, v_twice, attn_b, grad_attn, lse)
        return attn_backward(me, tensors, tables, first, pairs, raw)

    flows = [row_sum]
    grad_attn = tie(flows, grad_attn)
    row_sum.step()
    dq_one, _, raw = backward(0, 2, None)
    dq_one, raw, grad_attn, *out_parts = tie(flows, dq_one, raw, grad_attn, *out_parts)
    out_mine, out_core, out_cross, out_both = out_parts
    row_sum.step()
    out_home = team_send(out_core, 1)
    out_near = team_send(out_both, 1)
    dq_two, dkv_zero, raw = backward(2, 2, raw)
    dkv_zero, raw, grad_attn, out_home, out_near = tie(
        flows, dkv_zero, raw, grad_attn, out_home, out_near
    )
    row_sum.step()
    out_away = team_send((out_cross.astype(F32) + out_near.astype(F32)).astype(BF16), 2)
    zero_sum = spread_sum(dkv_zero)
    dq_three, dkv_one, _ = backward(4, 3, raw)
    dq_three, dkv_one, zero_sum, out_away = tie(flows, dq_three, dkv_one, zero_sum, out_away)
    one_sum = spread_sum(dkv_one)
    mine, dq_three = lax.optimization_barrier((row_sum.result().astype(BF16), dq_three))
    cross = team_send(mine, 2)
    core = team_send(mine, 1)
    output = middle + (out_mine.astype(F32) + out_home.astype(F32) + out_away.astype(F32))
    grad_q_b = jnp.concatenate([dq_one, dq_two, dq_three], axis=1)

    def team_total(rows):
        core, cross, both = (team_send(rows, bit).astype(F32) for bit in (1, 2, 3))
        rows = (rows.astype(F32) + core) + (cross + both)
        if teams > 1:
            rows = lax.psum(rows.astype(BF16), "rep", axis_index_groups=across).astype(F32)
        return rows

    q_bias_sum = jnp.sum(grad_q_b.astype(F32), axis=0)
    grad_h_q = dot_nt(grad_q_b, q_full)
    q_grads = dot_tn(h_one, grad_q_b).astype(BF16)
    q_grads = q_grads.reshape(shard_count, 2, 2, row_share // TEAM, QW)
    one_sum, q_grads = lax.optimization_barrier((one_sum, q_grads))

    def halve(array, axis, place, bit):
        keep = lax.dynamic_index_in_dim(array, place, axis, keepdims=False)
        give = lax.dynamic_index_in_dim(array, 1 - place, axis, keepdims=False)
        return (keep.astype(F32) + team_send(give, bit).astype(F32)).astype(BF16)

    q_grads = halve(halve(q_grads, 2, core_place, 1), 1, team_place // 2, 2)

    grad_k = jnp.concatenate([zero_sum[:, :HEAD], one_sum[:, :HEAD]], axis=1)
    grad_v = jnp.concatenate([zero_sum[:, HEAD:], one_sum[:, HEAD:]], axis=1)
    grad_kv_b = jnp.concatenate([rotate_back(grad_k, cosine, sine), grad_v], axis=1).astype(BF16)
    kv_bias_sum = jnp.sum(grad_kv_b.astype(F32), axis=0)
    grad_h_one = grad_h_q + dot_nt(grad_kv_b, kv_full)
    gain_one_grad = jnp.sum(grad_h_one * normed_one, axis=0)
    input_grad = (grad_middle + norm_back(grad_h_one, normed_one, inv_one, gain_one)).astype(BF16)

    width = 2 * KW
    late_weight = dot_tn(h_one, grad_kv_b).reshape(shard_count, row_share, width)
    smalls = jnp.concatenate(
        [
            one.reshape(shard_count, -1)
            for one in (gain_one_grad, gain_two_grad, q_bias_sum, kv_bias_sum)
        ],
        axis=1,
    )
    smalls = jnp.pad(smalls, ((0, 0), (0, 16 * width - smalls.shape[1])))
    last_sum = jnp.concatenate([late_weight, smalls.reshape(shard_count, 16, width)], axis=1)
    last_sum, cross = lax.optimization_barrier(
        (last_sum.reshape(-1, width).astype(BF16), cross)
    )
    both = team_send(cross, 1)
    last_sum, q_grads, both = lax.optimization_barrier((spread_sum(last_sum), q_grads, both))
    q_part = spread_sum(q_grads.reshape(-1, QW))
    last_rows = team_total(last_sum.astype(BF16))
    kv_rows = last_rows[:row_share]
    smalls = last_rows[row_share:].reshape(-1)
    gains_grad = smalls[: 2 * row_share].reshape(2, row_share)
    q_bias_grad = smalls[2 * row_share : 3 * row_share]
    kv_bias_grad = smalls[3 * row_share : 3 * row_share + kv_share]

    parts = [mine, core, cross, both]
    if teams > 1:
        parts = [lax.psum(part, "rep", axis_index_groups=across) for part in parts]
    outs = [part[:, 3 * FF_PART :].astype(F32) for part in parts]
    out_rows = (outs[0] + outs[1]) + (outs[2] + outs[3])
    gate_grad, up_grad, down_grad = columns(team_place, parts)
    gate_grad, up_grad, down_grad, q_part = lax.optimization_barrier(
        (gate_grad, up_grad, down_grad, q_part)
    )
    if teams > 1:
        q_part = lax.psum(q_part.astype(BF16), "rep", axis_index_groups=across)
    q_part = q_part.astype(BF16)
    q_parts = [q_part] + [team_send(q_part, bit) for bit in (1, 2, 3)]

    def quarter_at(place):
        bit = team_place ^ place
        low = jnp.where(bit == 0, q_parts[0], q_parts[1])
        return jnp.where(bit < 2, low, jnp.where(bit == 2, q_parts[2], q_parts[3]))

    q_rows = jnp.concatenate([quarter_at(place) for place in range(TEAM)], axis=0).astype(F32)
    return (
        output.astype(BF16)[None],
        input_grad[None],
        gains_grad,
        q_bias_grad,
        kv_bias_grad,
        q_rows,
        kv_rows,
        out_rows,
        gate_grad,
        up_grad,
        down_grad,
    )


def solution(mesh):
    tokens = P("rep", "shard", None)
    rows = P("shard", None)
    placed = (tokens, tokens, P(None, "shard"), P("shard"), P("shard")) + (rows,) * 6
    return jax.shard_map(body, mesh=mesh, in_specs=placed, out_specs=placed, check_vma=False)
```
